32 devices in a mesh: fsdp: 32 (over z, y, x, core).
Axes of the slice: x: 2, y: 2, z: 4, core: 2. Of those that a mesh axis runs over, the one named last changes fastest.
Arguments:
- images: bfloat16 [64, 208, 768], P('fsdp'), may hold values from -6 to 6
- lengths: int32 [64], P('fsdp'), may hold values from 98 to 197, as said below
- norm_scale: bfloat16 [768], P('fsdp'), may hold values from 0.5 to 1.5
- norm_shift: bfloat16 [768], P('fsdp'), may hold values from -1 to 1
- attend_in: bfloat16 [768, 2304], P('fsdp'), may hold values from -0.21875 to 0.21875
- attend_out: bfloat16 [768, 768], P('fsdp'), may hold values from -1.5 to 1.5
- mixer_scale: bfloat16 [768], P('fsdp'), may hold values from 0.5 to 1.5
- mixer_shift: bfloat16 [768], P('fsdp'), may hold values from -1 to 1
- slot_params: bfloat16 [768, 4], P('fsdp'), may hold values from -0.15625 to 0.15625
- expert_in: bfloat16 [4, 768, 3072], P(None, None, 'fsdp'), may hold values from -0.875 to 0.875
- expert_out: bfloat16 [4, 3072, 768], P(None, 'fsdp'), may hold values from -0.21875 to 0.21875
- cotangent: bfloat16 [64, 208, 768], P('fsdp'), may hold values from -6 to 6
Outputs:
- block_out: bfloat16 [64, 208, 768], P('fsdp')
- images_grad: float32 [64, 208, 768], P('fsdp')
- nscale_grad: float32 [768], P('fsdp')
- nshift_grad: float32 [768], P('fsdp')
- attin_grad: float32 [768, 2304], P('fsdp')
- attout_grad: float32 [768, 768], P('fsdp')
- mscale_grad: float32 [768], P('fsdp')
- mshift_grad: float32 [768], P('fsdp')
- slots_grad: float32 [768, 4], P('fsdp')
- expin_grad: float32 [4, 768, 3072], P(None, None, 'fsdp')
- expout_grad: float32 [4, 3072, 768], P(None, 'fsdp')
The draws below stay inside these ranges and needn't reach their ends.
Inputs may be any that keep to these rules, and one draw needn't show every extreme that they name: `lengths`: each image's live rows are its first ones; some image in every draw has exactly 197 live rows.
All inputs are finite; a program needn't handle non-finite values.
Results may differ from the reference program's by a relative error of at most 0.017.
Values may be sent and summed in bfloat16 or wider, within the bound.
No kernel may reach another device: no remote copies, remote signals or barrier semaphores. Data moves between devices by JAX's collectives and lax.ppermute only.
A program may use at most 192 MiB of HBM per device.

```python
import jax
import jax.numpy as jnp
from jax import lax

D = 768
HEADS = 12
FF = 3072
E = 4
PATCHES = 197
ROWS = 208
IMG_DEV = 2
IMAGES = 64
N_FSDP = 32


def draw_lengths(key, part):
    first_key, second_key = jax.random.split(jax.random.fold_in(key, 11))
    drawn = jax.random.randint(first_key, (IMAGES,), PATCHES // 2, PATCHES + 1)
    full_place = jax.random.randint(second_key, (), 0, IMAGES)
    return jnp.where(jnp.arange(IMAGES) == full_place, PATCHES, drawn).astype(jnp.int32)


def spiked(values, own_key, source, target, parts, factor):
    owner, partner = [(jnp.arange(values.shape[axis_at]) // (values.shape[axis_at] // parts)).reshape([-1 if axis == axis_at else 1 for axis in range(values.ndim)]) for axis_at in (source, target)]
    chosen = jax.random.permutation(own_key, parts)[partner]
    strong = (owner == chosen) | (owner == (partner + parts // 2) % parts)
    return jnp.where(strong, factor * values, values)


def block_levels(key, shape, cuts, least, top_value):
    level = 1.0
    for axis_at, blocks in cuts:
        draws = jax.random.uniform(jax.random.fold_in(jax.random.fold_in(key, 6), axis_at), (blocks,), jnp.float32, least / len(cuts), top_value / len(cuts))
        level = level * jnp.repeat(jnp.exp(draws), shape[axis_at] // blocks).reshape((-1,) + (1,) * (len(shape) - 1 - axis_at))
    return level


def scatter_about(key, dims, width, bound, cuts=(), kind=jnp.bfloat16):
    values = jax.random.normal(key, dims, jnp.float32) * width
    if len(cuts) > 0:
        values = block_levels(key, dims, cuts, -0.22, 0.18) * values
    return jnp.clip(values, min=-bound, max=bound).astype(kind)


def gaussian_with(key, extent, deviation, reach, cuts, heavy, held_as=jnp.bfloat16):
    entries = deviation * jax.random.normal(key, extent, jnp.float32)
    if cuts:
        entries = entries * block_levels(key, extent, cuts, -0.22, 0.18)
    return jnp.clip(spiked(entries, jax.random.fold_in(key, 3), *heavy), -reach, reach).astype(held_as)


def setup_inputs(seed: int = 0) -> dict:
    streams_of = jax.random.split(jax.random.key(seed), 13)
    images = gaussian_with(streams_of[0], (IMAGES, ROWS, D), 1.0, 6.0, ((0, 32),), (0, 2, 32, 2.75))
    lengths = draw_lengths(jax.random.fold_in(streams_of[12], 71), 0)
    norm_scale = jnp.clip(1.0 + 0.1 * jax.random.normal(streams_of[2], (D,), jnp.float32), 0.5, 1.5).astype(jnp.bfloat16)
    norm_shift = scatter_about(streams_of[3], (D,), 0.2, 1.0, ((0, 32),))
    attend_in = scatter_about(streams_of[4], (D, 3 * D), D ** -0.5, 0.21875, ((0, 32),))
    attend_out = scatter_about(streams_of[5], (D, D), (D // 48) ** -0.5, 1.5, ((0, 32),))
    mixer_scale = jnp.clip(1.0 + 0.1 * jax.random.normal(streams_of[6], (D,), jnp.float32), 0.5, 1.5).astype(jnp.bfloat16)
    mixer_shift = scatter_about(streams_of[7], (D,), 0.2, 1.0, ((0, 32),))
    slot_params = scatter_about(streams_of[8], (D, E), (2 * D) ** -0.5, 0.15625, ((0, 32),))
    expert_in = scatter_about(streams_of[9], (E, D, FF), (D // 16) ** -0.5, 0.875, ((2, 32),))
    expert_out = scatter_about(streams_of[10], (E, FF, D), (FF // 4) ** -0.5, 0.21875, ((1, 32),))
    cotangent = scatter_about(streams_of[11], (IMAGES, ROWS, D), 1.0, 6.0, ((0, 32),))
    return dict(images=images, lengths=lengths, norm_scale=norm_scale, norm_shift=norm_shift, attend_in=attend_in, attend_out=attend_out, mixer_scale=mixer_scale, mixer_shift=mixer_shift, slot_params=slot_params, expert_in=expert_in, expert_out=expert_out, cotangent=cotangent)


NEGATIVE = -1e+30
EPSILON = 1e-06

@jax.custom_vjp
def low(v):
    return lax.optimization_barrier(v.astype(jnp.bfloat16)).astype(jnp.float32)

@jax.custom_vjp
def low_back(v):
    return v

def low_keep(v):
    return (low(v), None)

def low_pass(kept, grad):
    return (grad,)

def back_keep(v):
    return (v, None)

def back_low(kept, grad):
    return (low(grad),)
low.defvjp(low_keep, low_pass)
low_back.defvjp(back_keep, back_low)

def layer_norm(inputs, gain_row, shift_row):
    centre = inputs - lax.optimization_barrier(jnp.mean(inputs, axis=-1, keepdims=True))
    spread = lax.optimization_barrier(jnp.mean(centre * centre, axis=-1, keepdims=True))
    return centre * lax.rsqrt(spread + EPSILON) * gain_row + shift_row

def router(logits, live):
    dispatch = jax.nn.softmax(jnp.where(live[..., None], logits, NEGATIVE), axis=1)
    combine = jax.nn.softmax(logits, axis=2)
    return (dispatch, combine)

def forward(x_float, live, gain_a, shift_a, w_attend, w_out, gain_m, shift_m, w_slot, w_hidden, w_back):
    highest = lax.Precision.HIGHEST
    groups, row_count, model_width = x_float.shape
    head_dim = model_width // HEADS
    normed = low(layer_norm(x_float, gain_a, shift_a))
    joint = low_back(low(jnp.einsum('grd,de->gre', normed, w_attend, precision=highest)))
    query_rows = joint[..., :model_width].reshape(groups, row_count, HEADS, head_dim)
    key_rows = joint[..., model_width:2 * model_width].reshape(groups, row_count, HEADS, head_dim)
    value_rows = joint[..., 2 * model_width:].reshape(groups, row_count, HEADS, head_dim)
    scores = low_back(jnp.einsum('gqhd,gkhd->ghqk', query_rows, key_rows, precision=highest) * head_dim ** (-0.5))
    masked = jnp.where(live[:, None, None, :], scores, NEGATIVE)
    soft_probs = low(jax.nn.softmax(masked, axis=-1))
    mixed = jnp.einsum('ghqk,gkhd->gqhd', soft_probs, value_rows, precision=highest)
    mixed = low_back(low(mixed.reshape(groups, row_count, model_width)))
    branch = low_back(jnp.einsum('grd,de->gre', mixed, w_out, precision=highest))
    residual = x_float + branch
    normed2 = low(layer_norm(residual, gain_m, shift_m))
    logits = low_back(jnp.einsum('grd,de->gre', normed2, w_slot, precision=highest))
    dispatch, combine = router(logits, live)
    dispatch = low(dispatch)
    combine = low(combine)
    slot_in = low_back(low(jnp.einsum('gre,grd->ged', dispatch, normed2, precision=highest)))
    pre_act = low_back(jnp.einsum('ged,edf->gef', slot_in, w_hidden, precision=highest))
    active = low(jax.nn.gelu(pre_act, approximate=True))
    slot_out = low_back(low(jnp.einsum('gef,efd->ged', active, w_back, precision=highest)))
    expert_sum = low_back(jnp.einsum('gre,ged->grd', combine, slot_out, precision=highest))
    return jnp.where(live[..., None], residual + expert_sum, 0.0)

def reference(images, lengths, norm_scale, norm_shift, attend_in, attend_out, mixer_scale, mixer_shift, slot_params, expert_in, expert_out, cotangent):
    weights = tuple((w.astype(jnp.float32) for w in (norm_scale, norm_shift, attend_in, attend_out, mixer_scale, mixer_shift, slot_params, expert_in, expert_out)))
    x_blocks = images.reshape(N_FSDP, IMG_DEV, ROWS, D)
    len_blocks = lengths.reshape(N_FSDP, IMG_DEV)
    cot_blocks = cotangent.reshape(N_FSDP, IMG_DEV, ROWS, D)

    def block_step(carry, pieces):
        x_block, len_block, cot_block = pieces
        live = lax.broadcasted_iota(jnp.int32, (IMG_DEV, ROWS), 1) < len_block[:, None]

        def tied(x_float, *params):
            return forward(x_float, live, *params)
        result, pull = jax.vjp(tied, x_block.astype(jnp.float32), *weights)
        grads = pull(cot_block.astype(jnp.float32))
        carry = tuple((c + g for c, g in zip(carry, grads[1:])))
        return (carry, (result.astype(jnp.bfloat16), grads[0]))
    start = tuple((jnp.zeros(w.shape, jnp.float32) for w in weights))
    totals, (outputs, x_grads) = lax.scan(block_step, start, (x_blocks, len_blocks, cot_blocks))
    block_out = outputs.reshape(IMAGES, ROWS, D)
    images_grad = x_grads.reshape(IMAGES, ROWS, D)
    return (block_out, images_grad, totals[0], totals[1], totals[2], totals[3], totals[4], totals[5], totals[6], totals[7], totals[8])
```

```python
import jax
import jax.numpy as jnp
from jax import lax
from jax.experimental import pallas as pl
from jax.experimental.pallas import tpu as pltpu
from jax.sharding import PartitionSpec as P

HEADS = 12
NEGATIVE = -1e30
EPSILON = 1e-06
GELU_C = 0.7978845608
GELU_A = 0.044715
LANES = 128
CHUNK = 16
MIB = 1 << 20

bf16 = jnp.bfloat16
f32 = jnp.float32


def dot(a, b, ca, cb):
    return lax.dot_general(a, b, (((ca,), (cb,)), ((), ())), preferred_element_type=f32)


def nn(a, b):
    return dot(a, b, 1, 0)


def nt(a, b):
    return dot(a, b, 1, 1)


def tn(a, b):
    return dot(a, b, 0, 0)


def vmem():
    return pl.BlockSpec(memory_space=pltpu.VMEM)


def smem():
    return pl.BlockSpec(memory_space=pltpu.SMEM)


def call(body, outs, scratch, limit_mib, flops=0, bytes_accessed=0):
    def run(scalars, *args):
        return pl.pallas_call(
            body,
            out_shape=[jax.ShapeDtypeStruct(s, d) for s, d in outs],
            in_specs=[smem()] + [vmem()] * len(args),
            out_specs=[vmem()] * len(outs),
            scratch_shapes=[pltpu.VMEM(s, d) for s, d in scratch],
            compiler_params=pltpu.CompilerParams(vmem_limit_bytes=limit_mib * MIB),
            cost_estimate=pl.CostEstimate(
                flops=flops, bytes_accessed=bytes_accessed, transcendentals=0
            ),
        )(scalars, *args)

    return run


def rows_at(step, count):
    return pl.ds(pl.multiple_of(step * count, count), count)


def fold_rows(value):
    return value[:8] + value[8:]


def head_masks():
    lane = lax.broadcasted_iota(jnp.int32, (1, LANES), 1)
    return lane < LANES // 2


def stacked(pair):
    first = head_masks()
    zero = jnp.zeros_like(pair)
    return jnp.concatenate([jnp.where(first, pair, zero), jnp.where(first, zero, pair)], axis=0)


def unstacked(both):
    rows = both.shape[0] // 2
    return jnp.where(head_masks(), both[:rows], both[rows:])


def routing(logits, live):
    masked = jnp.where(live, logits, NEGATIVE)
    weight = jnp.exp(masked - jnp.max(masked, axis=1, keepdims=True))
    dispatch = weight / jnp.sum(weight, axis=1, keepdims=True)
    share = jnp.exp(logits - jnp.max(logits, axis=0, keepdims=True))
    combine = share / jnp.sum(share, axis=0, keepdims=True)
    return dispatch, combine


def forward_kernel(sizes):
    images, rows, width, experts, chips, part_rows, packed = sizes
    total = images * rows
    pairs = HEADS // 2
    pieces = packed is not None

    def body(meta, x_ref, cot_ref, *refs):
        if pieces:
            own_ref, oth_ref, *refs = refs
            (w_ref, par_ref, n1_ref, joint_ref, probs_ref, mixed_ref, res_ref, n2_ref, log_ref,
             slots_ref, small) = refs
            core = meta[images]

            @pl.loop(0, chips)
            def _(f):
                target = meta[images + 1 + f]
                for c0 in range(0, packed, 640):
                    c1 = min(packed, c0 + 640)
                    a = own_ref[f, :, c0:c1].astype(f32)
                    b = oth_ref[f, :, c0:c1].astype(f32)
                    both = jnp.concatenate(
                        [jnp.where(core == 0, a, b), jnp.where(core == 0, b, a)], axis=0
                    )
                    w_ref[rows_at(target, 2 * part_rows), c0:c1] = both.astype(bf16)
        else:
            w_ref, *refs = refs
            (par_ref, n1_ref, joint_ref, probs_ref, mixed_ref, res_ref, n2_ref, log_ref,
             slots_ref, small) = refs

        par_ref[...] = w_ref[:, 4 * width : 4 * width + LANES].astype(f32).T[:8]
        gain_a, shift_a = par_ref[0:1], par_ref[1:2]
        gain_m, shift_m = par_ref[2:3], par_ref[3:4]

        @pl.loop(0, total // CHUNK)
        def _(i):
            at = rows_at(i, CHUNK)
            x = x_ref[at].astype(f32)
            x = x - jnp.mean(x, axis=-1, keepdims=True)
            rstd = lax.rsqrt(jnp.mean(x * x, axis=-1, keepdims=True) + EPSILON)
            n1_ref[at] = (x * rstd * gain_a + shift_a).astype(bf16)

        @pl.loop(0, 3)
        def _(i):
            at = rows_at(i, width)
            joint_ref[:, at] = nn(n1_ref[...], w_ref[:, at]).astype(bf16)

        column = lax.broadcasted_iota(jnp.int32, (1, rows), 1)

        @pl.loop(0, pairs)
        def _(p):
            at_q = pl.ds(pl.multiple_of(p * LANES, LANES), LANES)
            at_k = pl.ds(pl.multiple_of(width + p * LANES, LANES), LANES)
            at_v = pl.ds(pl.multiple_of(2 * width + p * LANES, LANES), LANES)
            for img in range(images):
                span = slice(img * rows, (img + 1) * rows)
                query, key, value = joint_ref[span, at_q], joint_ref[span, at_k], joint_ref[span, at_v]
                scores = nt(stacked(query), key) * 0.125
                scores = jnp.where(column < meta[img], scores, NEGATIVE)
                weight = jnp.exp(scores - jnp.max(scores, axis=-1, keepdims=True))
                probs = weight * (1.0 / jnp.sum(weight, axis=-1, keepdims=True))
                probs = probs.astype(bf16)
                probs_ref[img, p] = probs
                mixed_ref[span, at_q] = unstacked(nn(probs, value)).astype(bf16)

        res_ref[...] = x_ref[...].astype(f32) + nn(mixed_ref[...], w_ref[:, 3 * width : 4 * width])

        @pl.loop(0, total // CHUNK)
        def _(i):
            at = rows_at(i, CHUNK)
            x = res_ref[at]
            x = x - jnp.mean(x, axis=-1, keepdims=True)
            rstd = lax.rsqrt(jnp.mean(x * x, axis=-1, keepdims=True) + EPSILON)
            n2_ref[at] = (x * rstd * gain_m + shift_m).astype(bf16)

        slot_w = par_ref[4 : 4 + experts].astype(bf16)
        for img in range(images):
            span = slice(img * rows, (img + 1) * rows)
            logits = nt(slot_w, n2_ref[span])
            log_ref[img] = logits
            live = column < meta[img]
            dispatch, combine = routing(logits, live)
            small[img * experts : (img + 1) * experts] = nn(dispatch.astype(bf16), n2_ref[span])
            combine = jnp.where(live, combine, 0.0).astype(bf16)
            small[(images + img) * experts : (images + img + 1) * experts] = nn(combine, cot_ref[span])
        slots_ref[...] = small[...].astype(bf16)

    return body


def expert_kernel(images, experts, width, hidden, chips):
    lanes = -(-hidden // LANES) * LANES
    per = images * experts
    half = chips * per

    def body(_, own_ref, oth_ref, in_ref, out_ref, mine_ref, other_ref, s_ref, g_ref, act_ref, gpre_ref,
             win, wout, so, gs):
        win[...] = jnp.zeros(win.shape, bf16)
        wout[...] = jnp.zeros(wout.shape, bf16)
        for e in range(experts):
            win[:, e * lanes : e * lanes + hidden] = in_ref[e]
            wout[e * lanes : e * lanes + hidden, :] = out_ref[e]

        for side, ref in enumerate((own_ref, oth_ref)):

            @pl.loop(0, chips // 2)
            def _(i):
                first, second = ref[2 * i].astype(f32), ref[2 * i + 1].astype(f32)
                at = pl.ds(pl.multiple_of(side * half + i * 2 * per, 2 * per), 2 * per)
                s_ref[at] = jnp.concatenate([first[:per], second[:per]], axis=0).astype(bf16)
                g_ref[at] = jnp.concatenate([first[per:], second[per:]], axis=0).astype(bf16)

        block = 2 * half if 2 * half <= 256 else 256

        @pl.loop(0, 2 * half // block)
        def _(i):
            at = rows_at(i, block)
            so[at, : experts * lanes] = nn(s_ref[at], win[...])
            gs[at, : experts * lanes] = nt(g_ref[at], wout[...])

        @pl.loop(0, 2 * half // CHUNK)
        def _(i):
            at = rows_at(i, CHUNK)
            shape = (CHUNK, experts * lanes)
            keep = (lax.broadcasted_iota(jnp.int32, shape, 0) % experts) == (
                lax.broadcasted_iota(jnp.int32, shape, 1) // lanes
            )
            v = so[at, : experts * lanes]
            grad = gs[at, : experts * lanes]
            tanh = jnp.tanh(GELU_C * (v + GELU_A * v * v * v))
            act = 0.5 * v * (1.0 + tanh)
            slope = 0.5 * (1.0 + tanh) + 0.5 * v * (1.0 - tanh * tanh) * (
                GELU_C * (1.0 + 3.0 * GELU_A * v * v)
            )
            act_ref[at] = jnp.where(keep, act, 0.0).astype(bf16)
            gpre_ref[at] = jnp.where(keep, slope * grad, 0.0).astype(bf16)

        @pl.loop(0, 2 * half // block)
        def _(i):
            at = rows_at(i, block)
            so[at, :width] = nn(act_ref[at], wout[...])
            gs[at, :width] = nt(gpre_ref[at], win[...])

        for side, ref in enumerate((mine_ref, other_ref)):

            @pl.loop(0, chips)
            def _(f):
                at = pl.ds(pl.multiple_of(side * half + f * per, per), per)
                ref[f] = jnp.concatenate([so[at, :width], gs[at, :width]], axis=0).astype(bf16)

    return body


def expert_grad_kernel(experts, hidden):
    lanes = -(-hidden // LANES) * LANES

    def body(_, s_ref, g_ref, act_ref, gpre_ref, in_ref, out_ref):
        for e in range(experts):
            at = slice(e * lanes, (e + 1) * lanes)
            in_ref[e] = tn(s_ref[...], gpre_ref[:, at])[:, :hidden]
            out_ref[e] = tn(act_ref[:, at], g_ref[...])[:hidden]

    return body


def norm_pull(x, gain, grad):
    x = x - jnp.mean(x, axis=-1, keepdims=True)
    rstd = lax.rsqrt(jnp.mean(x * x, axis=-1, keepdims=True) + EPSILON)
    x = x * rstd
    scaled = grad * gain
    first = jnp.mean(scaled, axis=-1, keepdims=True)
    second = jnp.mean(scaled * x, axis=-1, keepdims=True)
    return x, rstd * (scaled - first - x * second)


def backward_kernel(sizes):
    images, rows, width, experts, chips, part_rows, packed = sizes
    total = images * rows
    pairs = HEADS // 2
    pieces = packed is not None

    def body(meta, x_ref, cot_ref, w_ref, par_ref, n1_ref, joint_ref, probs_ref, mixed_ref, res_ref,
             n2_ref, log_ref, sum_ref, r1_ref, r2_ref, r3_ref, *refs):
        if pieces:
            block_ref, xgrad_ref, mine_ref, other_ref, gn, gb, gm, gj, tile, small, grads = refs
        else:
            block_ref, xgrad_ref, whole_ref, gn, gb, gm, gj, tile, small, grads = refs

        def put(first, count):
            if not pieces:
                whole_ref[:, first : first + count] = tile[:, :count]
                return
            core = meta[images]

            @pl.loop(0, chips)
            def _(f):
                at = rows_at(meta[images + 1 + f], 2 * part_rows)
                both = tile[at, :count]
                low, high = both[:part_rows], both[part_rows:]
                mine_ref[f, :, first : first + count] = jnp.where(core == 0, low, high).astype(bf16)
                other_ref[f, :, first : first + count] = jnp.where(core == 0, high, low).astype(bf16)

        sums = sum_ref[0].astype(f32) + r1_ref[0].astype(f32) + r2_ref[0].astype(f32) + r3_ref[0].astype(f32)
        small[...] = sums.astype(bf16).astype(f32)
        slot_w = par_ref[4 : 4 + experts]
        column = lax.broadcasted_iota(jnp.int32, (1, rows), 1)
        slot_grad = jnp.zeros((experts, width), f32)
        for img in range(images):
            span = slice(img * rows, (img + 1) * rows)
            live = column < meta[img]
            dispatch, combine = routing(log_ref[img], live)
            out32 = small[img * experts : (img + 1) * experts]
            grad32 = small[(images + img) * experts : (images + img + 1) * experts]
            slot_out = out32.astype(bf16)
            grad_comb = jnp.where(live, nt(slot_out, cot_ref[span]), 0.0)
            grad_disp = nt(grad32.astype(bf16), n2_ref[span])
            grad_log = combine * (grad_comb - jnp.sum(combine * grad_comb, axis=0, keepdims=True))
            grad_log = grad_log + dispatch * (
                grad_disp - jnp.sum(dispatch * grad_disp, axis=1, keepdims=True)
            )
            slot_grad = slot_grad + nn(grad_log.astype(bf16), n2_ref[span])
            left = jnp.concatenate([dispatch, grad_log], axis=0).astype(bf16)
            right = jnp.concatenate([grad32, slot_w], axis=0).astype(bf16)
            gn[span] = tn(left, right)
            live_row = lax.broadcasted_iota(jnp.int32, (rows, 1), 0) < meta[img]
            expert_sum = tn(combine.astype(bf16), slot_out)
            block_ref[span] = jnp.where(live_row, res_ref[span] + expert_sum, 0.0).astype(bf16)
        grads[4 : 4 + experts] = slot_grad

        gain_a, gain_m = par_ref[0:1], par_ref[2:3]
        zero = jnp.zeros((8, width), f32)
        for img in range(images):

            def step(i, carry):
                at = pl.ds(pl.multiple_of(img * rows + i * CHUNK, CHUNK), CHUNK)
                grad = gn[at]
                x, pulled = norm_pull(res_ref[at], gain_m, grad)
                row = i * CHUNK + lax.broadcasted_iota(jnp.int32, (CHUNK, 1), 0)
                pulled = pulled + jnp.where(row < meta[img], cot_ref[at].astype(f32), 0.0)
                xgrad_ref[at] = pulled
                gb[at] = pulled.astype(bf16)
                return carry[0] + fold_rows(grad * x), carry[1] + fold_rows(grad)

            sums = lax.fori_loop(0, rows // CHUNK, step, (zero, zero) if img == 0 else sums)
        grads[2:3] = jnp.sum(sums[0], axis=0, keepdims=True)
        grads[3:4] = jnp.sum(sums[1], axis=0, keepdims=True)

        tile[...] = tn(mixed_ref[...], gb[...])
        put(3 * width, width)
        gm[...] = nt(gb[...], w_ref[:, 3 * width : 4 * width]).astype(bf16)

        @pl.loop(0, pairs)
        def _(p):
            at_q = pl.ds(pl.multiple_of(p * LANES, LANES), LANES)
            at_k = pl.ds(pl.multiple_of(width + p * LANES, LANES), LANES)
            at_v = pl.ds(pl.multiple_of(2 * width + p * LANES, LANES), LANES)
            for img in range(images):
                span = slice(img * rows, (img + 1) * rows)
                query, key, value = joint_ref[span, at_q], joint_ref[span, at_k], joint_ref[span, at_v]
                grad = stacked(gm[span, at_q])
                low = probs_ref[img, p]
                probs = low.astype(f32)
                grad_probs = nt(grad, value)
                row_dot = jnp.sum(probs * grad_probs, axis=-1, keepdims=True)
                grad_scores = (probs * (grad_probs - row_dot)).astype(bf16)
                gj[span, at_q] = (unstacked(nn(grad_scores, key)) * 0.125).astype(bf16)
                gj[span, at_k] = (tn(grad_scores, stacked(query)) * 0.125).astype(bf16)
                gj[span, at_v] = tn(low, grad).astype(bf16)

        for i in range(3):
            at = slice(i * width, (i + 1) * width)
            tile[...] = tn(n1_ref[...], gj[:, at])
            put(i * width, width)
        gn[...] = nt(gj[...], w_ref[:, : 3 * width])

        def step(i, carry):
            at = rows_at(i, CHUNK)
            grad = gn[at]
            x, pulled = norm_pull(x_ref[at].astype(f32), gain_a, grad)
            xgrad_ref[at] = xgrad_ref[at] + pulled
            return carry[0] + fold_rows(grad * x), carry[1] + fold_rows(grad)

        sums = lax.fori_loop(0, total // CHUNK, step, (zero, zero))
        grads[0:1] = jnp.sum(sums[0], axis=0, keepdims=True)
        grads[1:2] = jnp.sum(sums[1], axis=0, keepdims=True)
        filled = jnp.concatenate([grads[...], jnp.zeros((LANES - 8, width), f32)], axis=0)
        tile[:, :LANES] = filled.T
        put(4 * width, LANES)

    return body


def split_sum(parts, first_type=f32):
    def run(*args):
        count, rest = args[0].shape[0], args[0].shape[1:]
        share = count // parts

        def body(*refs):
            ins, outs = refs[: len(args)], refs[len(args) :]
            for part in range(parts):

                @pl.loop(0, share)
                def _(i):
                    total = ins[0][part * share + i].astype(f32)
                    for ref in ins[1:]:
                        total = total + ref[part * share + i].astype(f32)
                    outs[part][i] = total.astype(outs[part].dtype)

        types = [first_type] + [bf16] * (parts - 1)
        return pl.pallas_call(
            body,
            out_shape=[jax.ShapeDtypeStruct((share,) + rest, t) for t in types],
            in_specs=[vmem()] * len(args),
            out_specs=[vmem()] * parts,
            compiler_params=pltpu.CompilerParams(vmem_limit_bytes=32 * MIB),
        )(*args)

    return run


def stages_of(devices):
    chips = devices // 2
    groups, bit = [], 1
    while bit < chips:
        count = min(4, chips // bit)
        groups.append([bit * i for i in range(count)])
        bit *= count
    return groups


def swap(value, devices, chip_offset, core_offset):
    mask = 2 * chip_offset + core_offset
    return lax.ppermute(value, "fsdp", [(i, i ^ mask) for i in range(devices)])


def gather_chips(block, devices):
    for group in reversed(stages_of(devices)):
        block = jnp.concatenate(
            [block] + [swap(block, devices, o, 0) for o in group[1:]], axis=0
        )
    return block, swap(block, devices, 0, 1)


def scatter_chips(mine, other, devices):
    terms = [mine, swap(other, devices, 0, 1)]
    for group in stages_of(devices):
        parts = split_sum(len(group))(*terms)
        terms = [parts[0]] + [swap(p, devices, o, 0) for p, o in zip(parts[1:], group[1:])]
    return terms


def build(devices):
    def shards(images, lengths, norm_scale, norm_shift, attend_in, attend_out, mixer_scale, mixer_shift,
               slot_params, expert_in, expert_out, cotangent):
        count, rows, width = images.shape
        experts, _, hidden = expert_in.shape
        part_rows = attend_in.shape[0]
        chips = devices // 2
        total = count * rows
        pairs = HEADS // 2
        packed = 4 * width + LANES
        pieces = part_rows % 8 == 0
        sizes = (count, rows, width, experts, chips, part_rows, packed if pieces else None)
        me = lax.axis_index("fsdp")

        offsets = jnp.zeros((1,), jnp.int32)
        for group in reversed(stages_of(devices)):
            offsets = (jnp.array(group, jnp.int32)[:, None] ^ offsets[None, :]).reshape(-1)
        meta = jnp.concatenate(
            [lengths, jnp.reshape(me % 2, (1,)).astype(jnp.int32), (me // 2).astype(jnp.int32) ^ offsets]
        )

        small = jnp.stack([norm_scale, norm_shift, mixer_scale, mixer_shift], axis=1)
        small = jnp.concatenate([small, slot_params], axis=1)
        small = jnp.pad(small, ((0, 0), (0, LANES - small.shape[1])))
        pack = jnp.concatenate([attend_in, attend_out, small], axis=1)
        x = images.reshape(total, width)
        cot = cotangent.reshape(total, width)

        outs = [
            ((8, width), f32),
            ((total, width), bf16),
            ((total, 3 * width), bf16),
            ((count, pairs, 2 * rows, rows), bf16),
            ((total, width), bf16),
            ((total, width), f32),
            ((total, width), bf16),
            ((count, experts, rows), f32),
            ((2 * count * experts, width), bf16),
        ]
        scratch = [((2 * count * experts, width), f32)]
        if pieces:
            own, oth = gather_chips(pack[None], devices)
            w, par, n1, joint, probs, mixed, res, n2, logs, slots = call(
                forward_kernel(sizes), [((width, packed), bf16)] + outs, scratch, 48
            )(meta, x, cot, own, oth)
        else:
            w = lax.all_gather(pack, "fsdp", axis=0, tiled=True)
            par, n1, joint, probs, mixed, res, n2, logs, slots = call(
                forward_kernel(sizes), outs, scratch, 48
            )(meta, x, cot, w)

        own, oth = gather_chips(slots[None], devices)
        lanes = -(-hidden // LANES) * LANES
        held = devices * count * experts
        wide = max(width, experts * lanes)
        mine, other, s_all, g_all, act, gpre = call(
            expert_kernel(count, experts, width, hidden, chips),
            [
                ((chips, 2 * count * experts, width), bf16),
                ((chips, 2 * count * experts, width), bf16),
                ((held, width), bf16),
                ((held, width), bf16),
                ((held, experts * lanes), bf16),
                ((held, experts * lanes), bf16),
            ],
            [
                ((width, experts * lanes), bf16),
                ((experts * lanes, width), bf16),
                ((held, wide), f32),
                ((held, wide), f32),
            ],
            40,
        )(meta, own, oth, expert_in, expert_out)
        expin_grad, expout_grad = call(
            expert_grad_kernel(experts, hidden),
            [((experts, width, hidden), f32), ((experts, hidden, width), f32)],
            [],
            32,
        )(meta, s_all, g_all, act, gpre)
        terms = scatter_chips(mine, other, devices)
        if len(terms) < 4:
            terms = terms + [jnp.zeros_like(terms[-1])] * (4 - len(terms))

        results = [((total, width), bf16), ((total, width), f32)]
        if pieces:
            results += [((chips, part_rows, packed), bf16)] * 2
        else:
            results += [((width, packed), f32)]
        block, xgrad, *weight_grads = call(
            backward_kernel(sizes),
            results,
            [
                ((total, width), f32),
                ((total, width), bf16),
                ((total, width), bf16),
                ((total, 3 * width), bf16),
                ((width, width), f32),
                ((2 * count * experts, width), f32),
                ((8, width), f32),
            ],
            56,
        )(meta, x, cot, w, par, n1, joint, probs, mixed, res, n2, logs, *terms)
        if pieces:
            grad = split_sum(1)(*scatter_chips(*weight_grads, devices))[0][0]
        else:
            grad = lax.psum_scatter(weight_grads[0], "fsdp", scatter_dimension=0, tiled=True)
        at = 4 * width
        return (
            block.reshape(images.shape),
            xgrad.reshape(images.shape),
            grad[:, at],
            grad[:, at + 1],
            grad[:, : 3 * width],
            grad[:, 3 * width : at],
            grad[:, at + 2],
            grad[:, at + 3],
            grad[:, at + 4 : at + 4 + experts],
            expin_grad,
            expout_grad,
        )

    return shards


def solution(mesh):
    rows = P("fsdp", None, None)
    cols = P(None, None, "fsdp")
    mids = P(None, "fsdp", None)
    flat = P("fsdp", None)
    vec = P("fsdp")
    return jax.shard_map(
        build(mesh.shape["fsdp"]),
        mesh=mesh,
        in_specs=(rows, vec, vec, vec, flat, flat, vec, vec, flat, cols, mids, rows),
        out_specs=(rows, rows, vec, vec, flat, flat, vec, vec, flat, cols, mids),
        check_vma=False,
    )
```

```python
import jax
import jax.numpy as jnp
from jax import lax
from jax.experimental import pallas as pl
from jax.experimental.pallas import tpu as pltpu
from jax.sharding import PartitionSpec as P

HEADS = 12
NEGATIVE = -1e30
EPSILON = 1e-06
GELU_C = 0.7978845608
GELU_A = 0.044715
LANES = 128
CHUNK = 16
UNROLL = 13
VMEM_MIB = 28
MIB = 1 << 20

bf16 = jnp.bfloat16
f32 = jnp.float32


def dot(a, b, ca, cb):
    return lax.dot_general(a, b, (((ca,), (cb,)), ((), ())), preferred_element_type=f32)


def nn(a, b):
    return dot(a, b, 1, 0)


def nt(a, b):
    return dot(a, b, 1, 1)


def tn(a, b):
    return dot(a, b, 0, 0)


def vmem():
    return pl.BlockSpec(memory_space=pltpu.VMEM)


def hbm():
    return pl.BlockSpec(memory_space=pltpu.HBM)


def smem():
    return pl.BlockSpec(memory_space=pltpu.SMEM)


def call(body, outs, scratch, limit_mib, flops=0, far_in=(), far_out=(), sems=0):
    def run(scalars, *args):
        return pl.pallas_call(
            body,
            out_shape=[
                pltpu.HBM(s, d) if i in far_out else jax.ShapeDtypeStruct(s, d)
                for i, (s, d) in enumerate(outs)
            ],
            in_specs=[smem()] + [hbm() if i in far_in else vmem() for i in range(len(args))],
            out_specs=[hbm() if i in far_out else vmem() for i in range(len(outs))],
            scratch_shapes=[pltpu.VMEM(s, d) for s, d in scratch]
            + ([pltpu.SemaphoreType.DMA((sems,))] if sems else []),
            compiler_params=pltpu.CompilerParams(vmem_limit_bytes=limit_mib * MIB),
            cost_estimate=pl.CostEstimate(flops=flops, bytes_accessed=0, transcendentals=0),
        )(
            scalars,
            *[pltpu.with_memory_space_constraint(a, pltpu.HBM) if i in far_in else a for i, a in enumerate(args)],
        )

    return run


def rows_at(step, count):
    return pl.ds(pl.multiple_of(step * count, count), count)


def fold_rows(value):
    return value[:8] + value[8:]


def head_masks():
    lane = lax.broadcasted_iota(jnp.int32, (1, LANES), 1)
    return lane < LANES // 2


def stacked(pair):
    first = head_masks()
    zero = jnp.zeros_like(pair)
    return jnp.concatenate([jnp.where(first, pair, zero), jnp.where(first, zero, pair)], axis=0)


def unstacked(both):
    rows = both.shape[0] // 2
    return jnp.where(head_masks(), both[:rows], both[rows:])


def routing(logits, live):
    masked = jnp.where(live, logits, NEGATIVE)
    weight = jnp.exp(masked - jnp.max(masked, axis=1, keepdims=True))
    dispatch = weight / jnp.sum(weight, axis=1, keepdims=True)
    share = jnp.exp(logits - jnp.max(logits, axis=0, keepdims=True))
    combine = share / jnp.sum(share, axis=0, keepdims=True)
    return dispatch, combine


def pack_kernel(width, experts):
    def body(in_ref, out_ref, ns_ref, nb_ref, ms_ref, mb_ref, slot_ref, pack_ref, square):
        pack_ref[:, : 3 * width] = in_ref[...]
        pack_ref[:, 3 * width : 4 * width] = out_ref[...]
        rows = in_ref.shape[0]
        square[...] = jnp.zeros_like(square)
        for i, ref in enumerate((ns_ref, nb_ref, ms_ref, mb_ref)):
            square[i : i + 1, :rows] = ref[...].astype(f32)
        square[4 : 4 + experts, :rows] = slot_ref[...].astype(f32)
        pack_ref[:, 4 * width :] = square[...].T[:rows].astype(bf16)

    return body


def block_chip(f, chips):
    k = f % 4
    return (lax.axis_index("fsdp") // 2) ^ (f // 4 + (k % 2) * (chips // 2) + (k // 2) * (chips // 4))


def assemble(meta, images, part_rows, own_ref, oth_ref, w_ref):
    columns = w_ref.shape[1]
    for own_first in (True, False):

        @pl.when(lax.axis_index("fsdp") % 2 == (0 if own_first else 1))
        def _():
            @pl.loop(0, own_ref.shape[0], unroll=2)
            def _(f):
                at = rows_at(block_chip(f, own_ref.shape[0]), 2 * part_rows)
                low_ref, high_ref = (own_ref, oth_ref) if own_first else (oth_ref, own_ref)
                for c0 in range(0, columns, 640):
                    c1 = min(columns, c0 + 640)
                    both = [low_ref[f, :, c0:c1].astype(f32), high_ref[f, :, c0:c1].astype(f32)]
                    w_ref[at, c0:c1] = jnp.concatenate(both, axis=0).astype(bf16)


def cut(meta, images, chips, part_rows, tile, count, mine_ref, other_ref, first):
    for own_first in (True, False):

        @pl.when(lax.axis_index("fsdp") % 2 == (0 if own_first else 1))
        def _():
            @pl.loop(0, chips, unroll=4)
            def _(f):
                at = rows_at(block_chip(f, chips), 2 * part_rows)
                for c0 in range(0, count, 384):
                    c1 = min(count, c0 + 384)
                    both = tile[at, c0:c1]
                    low, high = both[:part_rows].astype(bf16), both[part_rows:].astype(bf16)
                    mine_ref[f, :, first + c0 : first + c1] = low if own_first else high
                    other_ref[f, :, first + c0 : first + c1] = high if own_first else low


def forward_kernel(sizes):
    images, rows, width, experts, chips, part_rows, shares = sizes
    total = images * rows
    pairs = HEADS // 2
    pieces = len(shares)

    def body(meta, x_ref, cot_ref, *refs):
        ins, refs = refs[: 2 * pieces or 1], refs[2 * pieces or 1 :]
        par_ref, log_ref, slots_ref, n1_out, mixed_out, joint_out, probs_out, res_out, n2_out, *refs = refs
        if pieces:
            w_out, *refs = refs
        n1_ref, mixed_ref, joint_ref, probs_ref, res_ref, n2_ref, small, *refs = refs
        if pieces:
            w_ref, own_ref, oth_ref, sems = refs
            loads = []
            for side, stage in enumerate((own_ref, oth_ref)):
                first = 0
                for i, share in enumerate(shares):
                    ref = ins[side * pieces + i]
                    loads.append(
                        pltpu.make_async_copy(
                            ref, stage.at[first : first + share], sems.at[8 + pairs + side * pieces + i]
                        )
                    )
                    first += share
            for load in loads:
                load.start()
            for load in loads:
                load.wait()
            assemble(meta, images, part_rows, own_ref, oth_ref, w_ref)
        else:
            (sems,) = refs
            w_ref = ins[0]
        stores = []

        def store(ref, out):
            stores.append(pltpu.make_async_copy(ref, out, sems.at[len(stores)]))
            stores[-1].start()

        if pieces:
            store(w_ref, w_out)
        par_ref[...] = w_ref[:, 4 * width : 4 * width + LANES].astype(f32).T[:8]
        gain_a, shift_a = par_ref[0:1], par_ref[1:2]
        gain_m, shift_m = par_ref[2:3], par_ref[3:4]

        @pl.loop(0, total // CHUNK, unroll=UNROLL)
        def _(i):
            at = rows_at(i, CHUNK)
            x = x_ref[at].astype(f32)
            x = x - jnp.mean(x, axis=-1, keepdims=True)
            rstd = lax.rsqrt(jnp.mean(x * x, axis=-1, keepdims=True) + EPSILON)
            n1_ref[at] = (x * rstd * gain_a + shift_a).astype(bf16)

        store(n1_ref, n1_out)

        @pl.loop(0, 3)
        def _(i):
            at = rows_at(i, width)
            joint_ref[:, at] = nn(n1_ref[...], w_ref[:, at]).astype(bf16)

        store(joint_ref, joint_out)
        column = lax.broadcasted_iota(jnp.int32, (1, rows), 1)
        for p in range(pairs):
            at_q, at_k, at_v = [slice(i * width + p * LANES, i * width + (p + 1) * LANES) for i in range(3)]
            for img in range(images):
                span = slice(img * rows, (img + 1) * rows)
                query, key, value = joint_ref[span, at_q], joint_ref[span, at_k], joint_ref[span, at_v]
                scores = nt(stacked(query), key) * 0.125
                scores = jnp.where(column < meta[img], scores, NEGATIVE)
                weight = jnp.exp(scores - jnp.max(scores, axis=-1, keepdims=True))
                probs = weight * (1.0 / jnp.sum(weight, axis=-1, keepdims=True))
                probs = probs.astype(bf16)
                probs_ref[p, img] = probs
                mixed_ref[span, at_q] = unstacked(nn(probs, value)).astype(bf16)
            store(probs_ref.at[p], probs_out.at[p])
        store(mixed_ref, mixed_out)

        res_ref[...] = x_ref[...].astype(f32) + nn(mixed_ref[...], w_ref[:, 3 * width : 4 * width])
        store(res_ref, res_out)

        @pl.loop(0, total // CHUNK, unroll=UNROLL)
        def _(i):
            at = rows_at(i, CHUNK)
            x = res_ref[at]
            x = x - jnp.mean(x, axis=-1, keepdims=True)
            rstd = lax.rsqrt(jnp.mean(x * x, axis=-1, keepdims=True) + EPSILON)
            n2_ref[at] = (x * rstd * gain_m + shift_m).astype(bf16)

        store(n2_ref, n2_out)
        slot_w = par_ref[4 : 4 + experts].astype(bf16)
        for img in range(images):
            span = slice(img * rows, (img + 1) * rows)
            logits = nt(slot_w, n2_ref[span])
            log_ref[img] = logits
            live = column < meta[img]
            dispatch, combine = routing(logits, live)
            small[img * experts : (img + 1) * experts] = nn(dispatch.astype(bf16), n2_ref[span])
            combine = jnp.where(live, combine, 0.0).astype(bf16)
            small[(images + img) * experts : (images + img + 1) * experts] = nn(combine, cot_ref[span])
        slots_ref[...] = small[...].astype(bf16)
        for copy in stores:
            copy.wait()

    return body


def stack_kernel(count):
    def body(*refs):
        ins, out = refs[:count], refs[count]
        share = ins[0].shape[0]
        for i, ref in enumerate(ins):
            out[i * share : (i + 1) * share] = ref[...]

    return body


def expert_kernel(images, experts, width, hidden, chips, pieces):
    lanes = -(-hidden // LANES) * LANES
    per = images * experts
    half = chips * per

    def body(_, *refs):
        own_refs, oth_refs, refs = refs[:pieces], refs[pieces : 2 * pieces], refs[2 * pieces :]
        in_ref, out_ref, mine_ref, other_ref, s_ref, g_ref, act_ref, gpre_ref, win, wout, so, gs = refs
        win[...] = jnp.zeros(win.shape, bf16)
        wout[...] = jnp.zeros(wout.shape, bf16)
        for e in range(experts):
            win[e * lanes : e * lanes + hidden, :] = in_ref[e]
            wout[e * lanes : e * lanes + hidden, :] = out_ref[e]

        for side, group in enumerate((own_refs, oth_refs)):
            for j, ref in enumerate(group):
                share = ref.shape[0] // 2

                @pl.loop(0, share)
                def _(i):
                    first, second = ref[2 * i].astype(f32), ref[2 * i + 1].astype(f32)
                    at = pl.ds(pl.multiple_of(side * half + (j * share + i) * 2 * per, 2 * per), 2 * per)
                    s_ref[at] = jnp.concatenate([first[:per], second[:per]], axis=0).astype(bf16)
                    g_ref[at] = jnp.concatenate([first[per:], second[per:]], axis=0).astype(bf16)

        block = 2 * half if 2 * half <= 256 else 256

        @pl.loop(0, 2 * half // block)
        def _(i):
            at = rows_at(i, block)
            so[at, : experts * lanes] = nt(s_ref[at], win[...])
            gs[at, : experts * lanes] = nt(g_ref[at], wout[...])

        @pl.loop(0, 2 * half // CHUNK, unroll=4)
        def _(i):
            at = rows_at(i, CHUNK)
            shape = (CHUNK, experts * lanes)
            keep = (lax.broadcasted_iota(jnp.int32, shape, 0) % experts) == (
                lax.broadcasted_iota(jnp.int32, shape, 1) // lanes
            )
            v = so[at, : experts * lanes]
            grad = gs[at, : experts * lanes]
            tanh = jnp.tanh(GELU_C * (v + GELU_A * v * v * v))
            act = 0.5 * v * (1.0 + tanh)
            slope = 0.5 * (1.0 + tanh) + 0.5 * v * (1.0 - tanh * tanh) * (
                GELU_C * (1.0 + 3.0 * GELU_A * v * v)
            )
            act_ref[at] = jnp.where(keep, act, 0.0).astype(bf16)
            gpre_ref[at] = jnp.where(keep, slope * grad, 0.0).astype(bf16)

        @pl.loop(0, 2 * half // block)
        def _(i):
            at = rows_at(i, block)
            so[at, :width] = nn(act_ref[at], wout[...])
            gs[at, :width] = nn(gpre_ref[at], win[...])

        for side, ref in enumerate((mine_ref, other_ref)):

            @pl.loop(0, chips)
            def _(f):
                at = pl.ds(pl.multiple_of(side * half + f * per, per), per)
                ref[f] = jnp.concatenate([so[at, :width], gs[at, :width]], axis=0).astype(bf16)

    return body


def expert_grad_kernel(experts, hidden):
    lanes = -(-hidden // LANES) * LANES

    def body(_, s_ref, g_ref, act_ref, gpre_ref, in_ref, out_ref):
        for e in range(experts):
            at = slice(e * lanes, (e + 1) * lanes)
            in_ref[e] = tn(gpre_ref[:, at], s_ref[...])[:hidden]
            out_ref[e] = tn(act_ref[:, at], g_ref[...])[:hidden]

    return body


def norm_pull(x, gain, grad):
    x = x - jnp.mean(x, axis=-1, keepdims=True)
    rstd = lax.rsqrt(jnp.mean(x * x, axis=-1, keepdims=True) + EPSILON)
    x = x * rstd
    scaled = grad * gain
    first = jnp.mean(scaled, axis=-1, keepdims=True)
    second = jnp.mean(scaled * x, axis=-1, keepdims=True)
    return x, rstd * (scaled - first - x * second)


def attend_pull(meta, sizes, half, joint_ref, probs_ref, gm_ref, gj):
    images, rows, width, *_ = sizes
    share = HEADS // 4
    for q in range(share):
        at_q, at_k, at_v = [slice(i * width // 2 + q * LANES, i * width // 2 + (q + 1) * LANES) for i in range(3)]
        for img in range(images):
            span = slice(img * rows, (img + 1) * rows)
            query, key, value = joint_ref[span, at_q], joint_ref[span, at_k], joint_ref[span, at_v]
            p = half * share + q
            grad = stacked(gm_ref[span, p * LANES : (p + 1) * LANES])
            low = probs_ref[q, img]
            probs = low.astype(f32)
            grad_probs = nt(grad, value)
            row_dot = jnp.sum(probs * grad_probs, axis=-1, keepdims=True)
            grad_scores = (probs * (grad_probs - row_dot)).astype(bf16)
            gj[span, at_q] = (unstacked(nn(grad_scores, key)) * 0.125).astype(bf16)
            gj[span, at_k] = (tn(grad_scores, stacked(query)) * 0.125).astype(bf16)
            gj[span, at_v] = tn(low, grad).astype(bf16)


def half_loads(width, half, joint_in, joint_ref, probs_in, probs_ref, sems):
    part, share = width // 2, HEADS // 4
    loads = [
        pltpu.make_async_copy(
            joint_in.at[:, i * width + half * part : i * width + (half + 1) * part],
            joint_ref.at[:, i * part : (i + 1) * part],
            sems.at[i],
        )
        for i in range(3)
    ]
    loads.append(pltpu.make_async_copy(probs_in.at[half * share : (half + 1) * share], probs_ref, sems.at[3]))
    return loads


def slots_pull_kernel(sizes):
    images, rows, width, experts, chips, part_rows, shares = sizes
    pieces = len(shares)
    total = images * rows
    share = HEADS // 4

    def body(meta, cot_ref, par_ref, log_ref, sum_ref, r1_ref, r2_ref, r3_ref, w_in, n1_in, joint_in, probs_in,
             mixed_in, res_in, n2_in, block_ref, xgrad_ref, gm, gj, grads, *refs):
        outs, refs = refs[:-13], refs[-13:]
        gn, gb, tile, small, w_ref, n1_ref, joint_ref, probs_ref, mixed_ref, res_ref, n2_ref, _, sems = refs
        early = [
            pltpu.make_async_copy(n2_in, n2_ref, sems.at[0]),
            pltpu.make_async_copy(res_in, res_ref, sems.at[1]),
        ]
        late = [
            pltpu.make_async_copy(mixed_in, mixed_ref, sems.at[2]),
            pltpu.make_async_copy(w_in.at[:, 3 * width : 4 * width], w_ref, sems.at[3]),
            pltpu.make_async_copy(n1_in, n1_ref, sems.at[4]),
        ]
        loads = half_loads(width, 0, joint_in, joint_ref, probs_in, probs_ref, sems.at[5:9])
        for load in early + late + loads:
            load.start()

        def put(first, count):
            if pieces:
                cut(meta, images, chips, part_rows, tile, count, *outs, first)
            else:
                outs[0][:, first : first + count] = tile[:, :count]

        for load in early:
            load.wait()
        sums = sum_ref[0].astype(f32) + r1_ref[0].astype(f32) + r2_ref[0].astype(f32) + r3_ref[0].astype(f32)
        small[...] = sums.astype(bf16).astype(f32)
        slot_w = par_ref[4 : 4 + experts]
        column = lax.broadcasted_iota(jnp.int32, (1, rows), 1)
        slot_grad = jnp.zeros((experts, width), f32)
        for img in range(images):
            span = slice(img * rows, (img + 1) * rows)
            live = column < meta[img]
            dispatch, combine = routing(log_ref[img], live)
            out32 = small[img * experts : (img + 1) * experts]
            grad32 = small[(images + img) * experts : (images + img + 1) * experts]
            slot_out = out32.astype(bf16)
            grad_comb = jnp.where(live, nt(slot_out, cot_ref[span]), 0.0)
            grad_disp = nt(grad32.astype(bf16), n2_ref[span])
            grad_log = combine * (grad_comb - jnp.sum(combine * grad_comb, axis=0, keepdims=True))
            grad_log = grad_log + dispatch * (
                grad_disp - jnp.sum(dispatch * grad_disp, axis=1, keepdims=True)
            )
            slot_grad = slot_grad + nn(grad_log.astype(bf16), n2_ref[span])
            left = jnp.concatenate([dispatch, grad_log], axis=0).astype(bf16)
            right = jnp.concatenate([grad32, slot_w], axis=0).astype(bf16)
            gn[span] = tn(left, right)
            live_row = lax.broadcasted_iota(jnp.int32, (rows, 1), 0) < meta[img]
            expert_sum = tn(combine.astype(bf16), slot_out)
            block_ref[span] = jnp.where(live_row, res_ref[span] + expert_sum, 0.0).astype(bf16)
        grads[0:2] = jnp.zeros((2, width), f32)
        grads[4 : 4 + experts] = slot_grad

        gain_m = par_ref[2:3]
        zero = jnp.zeros((8, width), f32)
        for img in range(images):

            def step(i, carry):
                at = pl.ds(pl.multiple_of(img * rows + i * CHUNK, CHUNK), CHUNK)
                grad = gn[at]
                x, pulled = norm_pull(res_ref[at], gain_m, grad)
                row = i * CHUNK + lax.broadcasted_iota(jnp.int32, (CHUNK, 1), 0)
                pulled = pulled + jnp.where(row < meta[img], cot_ref[at].astype(f32), 0.0)
                xgrad_ref[at] = pulled
                gb[at] = pulled.astype(bf16)
                return carry[0] + fold_rows(grad * x), carry[1] + fold_rows(grad)

            sums = lax.fori_loop(0, rows // CHUNK, step, (zero, zero) if img == 0 else sums, unroll=UNROLL)
        grads[2:3] = jnp.sum(sums[0], axis=0, keepdims=True)
        grads[3:4] = jnp.sum(sums[1], axis=0, keepdims=True)

        for load in late:
            load.wait()
        tile[:, :width] = tn(mixed_ref[...], gb[...])
        put(0, width)
        gm[...] = nt(gb[...], w_ref[...]).astype(bf16)
        for load in loads:
            load.wait()
        attend_pull(meta, sizes, 0, joint_ref, probs_ref, gm, gj)
        tile[...] = tn(n1_ref[...], gj[...])
        put(width, 3 * width // 2)

    return body


def inputs_pull_kernel(sizes):
    images, rows, width, experts, chips, part_rows, shares = sizes
    pieces = len(shares)
    total = images * rows
    share = HEADS // 4
    half = 3 * width // 2

    def body(meta, x_ref, par_ref, gm_ref, gj_ref, part_ref, early_ref, w_in, n1_in, joint_in, probs_in,
             xgrad_ref, *refs):
        outs, (gn, gj, tile, grads, n1_ref, joint_ref, probs_ref, w_ref, sems) = refs[:-9], refs[-9:]
        loads = half_loads(width, 1, joint_in, joint_ref, probs_in, probs_ref, sems.at[0:4])
        late = [pltpu.make_async_copy(n1_in, n1_ref, sems.at[4])]
        part = width // 2
        for i in range(6):
            first = (i % 3) * width + (i // 3) * part
            late.append(
                pltpu.make_async_copy(
                    w_in.at[:, first : first + part], w_ref.at[:, i * part : (i + 1) * part], sems.at[5 + i]
                )
            )
        for load in loads + late:
            load.start()

        def put(first, count):
            if pieces:
                cut(meta, images, chips, part_rows, tile, count, *outs, first)
            else:
                outs[0][:, first : first + count] = tile[:, :count]

        for load in loads:
            load.wait()
        attend_pull(meta, sizes, 1, joint_ref, probs_ref, gm_ref, gj)
        for load in late:
            load.wait()
        tile[...] = tn(n1_ref[...], gj[...])
        put(0, half)
        gn[...] = nt(gj_ref[...], w_ref[:, :half]) + nt(gj[...], w_ref[:, half : 2 * half])
        gain_a = par_ref[0:1]
        zero = jnp.zeros((8, width), f32)

        def step(i, carry):
            at = rows_at(i, CHUNK)
            grad = gn[at]
            x, pulled = norm_pull(x_ref[at].astype(f32), gain_a, grad)
            xgrad_ref[at] = part_ref[at] + pulled
            return carry[0] + fold_rows(grad * x), carry[1] + fold_rows(grad)

        sums = lax.fori_loop(0, total // CHUNK, step, (zero, zero), unroll=UNROLL)
        grads[...] = early_ref[...]
        grads[0:1] = jnp.sum(sums[0], axis=0, keepdims=True)
        grads[1:2] = jnp.sum(sums[1], axis=0, keepdims=True)
        filled = jnp.concatenate([grads[...], jnp.zeros((LANES - 8, width), f32)], axis=0)
        tile[:, :LANES] = filled.T
        put(half, LANES)

    return body


def split_sum(parts, first_type=f32):
    def run(*args):
        count, rest = args[0].shape[0], args[0].shape[1:]
        share = count // parts

        def body(*refs):
            ins, outs = refs[: len(args)], refs[len(args) :]
            for part in range(parts):

                @pl.loop(0, share)
                def _(i):
                    total = ins[0][part * share + i].astype(f32)
                    for ref in ins[1:]:
                        total = total + ref[part * share + i].astype(f32)
                    outs[part][i] = total.astype(outs[part].dtype)

        types = [first_type] + [bf16] * (parts - 1)
        return pl.pallas_call(
            body,
            out_shape=[jax.ShapeDtypeStruct((share,) + rest, t) for t in types],
            in_specs=[vmem()] * len(args),
            out_specs=[vmem()] * parts,
            compiler_params=pltpu.CompilerParams(vmem_limit_bytes=32 * MIB),
        )(*args)

    return run


def add_kernel(groups, terms, types):
    def run(*args):
        rest = args[0].shape[1:]

        def body(*refs):
            ins, outs = refs[: len(args)], refs[len(args) :]
            for out, count, parts in zip(outs, groups, terms):
                for i in range(count):
                    total = ins[parts[0][0]][parts[0][1] + i].astype(f32)
                    for a, first in parts[1:]:
                        total = total + ins[a][first + i].astype(f32)
                    out[i] = total.astype(out.dtype)

        return pl.pallas_call(
            body,
            out_shape=[jax.ShapeDtypeStruct((c,) + rest, t) for c, t in zip(groups, types)],
            in_specs=[vmem()] * len(args),
            out_specs=[vmem()] * len(groups),
            compiler_params=pltpu.CompilerParams(vmem_limit_bytes=16 * MIB),
        )(*args)

    return run


def finish_kernel(width, experts):
    half = width // 2

    def body(a0, a1, b0, b1, out_ref, in_ref, ns_ref, nb_ref, ms_ref, mb_ref, slot_ref, square):
        first = a0[0] + a1[0].astype(f32)
        second = b0[0] + b1[0].astype(f32)
        rows = first.shape[0]
        out_ref[...] = first[:, :width]
        for i in range(3):
            in_ref[:, i * width : i * width + half] = first[:, width + i * half : width + (i + 1) * half]
            in_ref[:, i * width + half : (i + 1) * width] = second[:, i * half : (i + 1) * half]
        small = second[:, 3 * half : 3 * half + LANES]
        square[...] = jnp.zeros_like(square)
        square[:rows] = small
        turned = square[...].T
        for i, ref in enumerate((ns_ref, nb_ref, ms_ref, mb_ref)):
            ref[...] = turned[i : i + 1, :rows]
        slot_ref[...] = turned[4 : 4 + experts, :rows]

    return body


def stages_of(devices):
    chips = devices // 2
    groups, bit = [], 1
    while bit < chips:
        count = min(4, chips // bit)
        groups.append([bit * i for i in range(count)])
        bit *= count
    return groups


def swap(value, devices, chip_offset, core_offset):
    mask = 2 * chip_offset + core_offset
    return lax.ppermute(value, "fsdp", [(i, i ^ mask) for i in range(devices)])


def gather_slots(block, devices):
    *lower, last = stages_of(devices)[::-1]
    for group in lower:
        parts = [block] + [swap(block, devices, o, 0) for o in group[1:]]
        block = pl.pallas_call(
            stack_kernel(len(parts)),
            out_shape=jax.ShapeDtypeStruct((len(parts) * block.shape[0],) + block.shape[1:], block.dtype),
            in_specs=[vmem()] * len(parts),
            out_specs=vmem(),
        )(*parts)
    own = [block] + [swap(block, devices, o, 0) for o in last[1:]]
    return own, [swap(part, devices, 0, 1) for part in own]


def scatter_chips(mine, other, devices):
    terms = [mine, swap(other, devices, 0, 1)]
    for group in stages_of(devices):
        parts = split_sum(len(group))(*terms)
        terms = [parts[0]] + [swap(p, devices, o, 0) for p, o in zip(parts[1:], group[1:])]
    return terms


SHARES = (2,) * 8


def gather_pieces(block, devices):
    z0 = block[None]
    z0 = jnp.concatenate([z0, swap(z0, devices, 8, 0)], axis=0)
    z1 = swap(z0, devices, 4, 0)
    x0, y0 = swap(z0, devices, 1, 0), swap(z0, devices, 2, 0)
    x1, y1 = swap(z1, devices, 1, 0), swap(z1, devices, 2, 0)
    d0, d1 = swap(y0, devices, 1, 0), swap(x1, devices, 2, 0)
    own = [z0, z1, x0, x1, y0, y1, d0, d1]
    return own + [swap(piece, devices, 0, 1) for piece in own]


def scatter_pieces(mine, other, devices):
    got = swap(other, devices, 0, 1)
    two = [[(0, 2 * g), (1, 2 * g)] for g in range(8)]
    z0, z1, x0, x1, y0, y1, d0, d1 = add_kernel([2] * 8, two, [f32, f32] + [bf16] * 6)(mine, got)
    to_y0, to_x1 = swap(d0, devices, 1, 0), swap(d1, devices, 2, 0)
    x1, y0 = add_kernel([2, 2], [[(0, 0), (1, 0)], [(2, 0), (3, 0)]], [bf16, bf16])(x1, to_x1, y0, to_y0)
    from_x1, from_y1 = swap(x1, devices, 1, 0), swap(y1, devices, 2, 0)
    from_x0, from_y0 = swap(x0, devices, 1, 0), swap(y0, devices, 2, 0)
    (z1,) = add_kernel([2], [[(0, 0), (1, 0), (2, 0)]], [bf16])(z1, from_x1, from_y1)
    from_z1 = swap(z1, devices, 4, 0)
    keep, send = add_kernel(
        [1, 1], [[(a, i) for a in range(4)] for i in range(2)], [f32, bf16]
    )(z0, from_x0, from_y0, from_z1)
    return keep, swap(send, devices, 8, 0)


def build(devices):
    def shards(images, lengths, norm_scale, norm_shift, attend_in, attend_out, mixer_scale, mixer_shift,
               slot_params, expert_in, expert_out, cotangent):
        count, rows, width = images.shape
        experts, _, hidden = expert_in.shape
        part_rows = attend_in.shape[0]
        chips = devices // 2
        total = count * rows
        pairs = HEADS // 2
        half = width // 2
        wide = 4 * width + LANES
        shares = SHARES if part_rows % 8 == 0 and chips == 16 else ()
        sizes = (count, rows, width, experts, chips, part_rows, shares)
        meta = lengths
        x = images.reshape(total, width)
        cot = cotangent.reshape(total, width)
        vectors = [v.reshape(1, part_rows) for v in (norm_scale, norm_shift, mixer_scale, mixer_shift)]
        pack = pl.pallas_call(
            pack_kernel(width, experts),
            out_shape=jax.ShapeDtypeStruct((part_rows, wide), bf16),
            in_specs=[vmem()] * 7,
            out_specs=vmem(),
            scratch_shapes=[pltpu.VMEM((LANES, LANES), f32)],
        )(attend_in, attend_out, *vectors, slot_params.T)
        if shares:
            weights = gather_pieces(pack, devices)
        else:
            weights = [lax.all_gather(pack, "fsdp", axis=0, tiled=True)]
        kept = [
            ((total, width), bf16),
            ((total, width), bf16),
            ((total, 3 * width), bf16),
            ((pairs, count, 2 * rows, rows), bf16),
            ((total, width), f32),
            ((total, width), bf16),
        ]
        outs = [
            ((8, width), f32),
            ((count, experts, rows), f32),
            ((2 * count * experts, width), bf16),
        ] + kept
        scratch = kept + [((2 * count * experts, width), f32)]
        if shares:
            outs.append(((width, wide), bf16))
            scratch += [outs[-1]] + [((chips, part_rows, wide), bf16)] * 2
        par, logs, slots, n1, mixed, joint, probs, res, n2, *more = call(
            forward_kernel(sizes),
            outs,
            scratch,
            40,
            far_in=range(2, 2 + 2 * len(shares)),
            far_out=range(3, len(outs)),
            sems=8 + pairs + 2 * len(shares),
        )(meta, x, cot, *weights)
        w = more[0] if shares else weights[0]

        own, oth = gather_slots(slots[None], devices)
        lanes = -(-hidden // LANES) * LANES
        held = devices * count * experts
        most = max(width, experts * lanes)
        mine, other, s_all, g_all, act, gpre = call(
            expert_kernel(count, experts, width, hidden, chips, len(own)),
            [
                ((chips, 2 * count * experts, width), bf16),
                ((chips, 2 * count * experts, width), bf16),
                ((held, width), bf16),
                ((held, width), bf16),
                ((held, experts * lanes), bf16),
                ((held, experts * lanes), bf16),
            ],
            [
                ((experts * lanes, width), bf16),
                ((experts * lanes, width), bf16),
                ((held, most), f32),
                ((held, most), f32),
            ],
            24 if held <= 256 else 56,
        )(meta, *own, *oth, jnp.swapaxes(expert_in, 1, 2), expert_out)
        expin_grad, expout_grad = call(
            expert_grad_kernel(experts, hidden),
            [((experts, hidden, width), f32), ((experts, hidden, width), f32)],
            [],
            24 if held <= 256 else 56,
            flops=2 * 10**9,
        )(meta, s_all, g_all, act, gpre)
        terms = scatter_chips(mine, other, devices)
        if len(terms) < 4:
            terms = terms + [jnp.zeros_like(terms[-1])] * (4 - len(terms))
        terms[0], expin_grad, expout_grad = lax.optimization_barrier((terms[0], expin_grad, expout_grad))

        def blocks(columns):
            if shares:
                return [((chips, part_rows, columns), bf16)] * 2
            return [((width, columns), f32)]

        halves = [((total, 3 * half), bf16), ((pairs // 2, count, 2 * rows, rows), bf16)]
        block, part, gm, gj, early, *first = call(
            slots_pull_kernel(sizes),
            [
                ((total, width), bf16),
                ((total, width), f32),
                ((total, width), bf16),
                ((total, 3 * half), bf16),
                ((8, width), f32),
            ]
            + blocks(width + 3 * half),
            [
                ((total, width), f32),
                ((total, width), bf16),
                ((width, 3 * half), f32),
                ((2 * count * experts, width), f32),
                ((width, width), bf16),
                ((total, width), bf16),
            ]
            + halves
            + [
                ((total, width), bf16),
                ((total, width), f32),
                ((total, width), bf16),
                ((8, LANES), f32),
            ],
            VMEM_MIB,
            far_in=range(7, 14),
            sems=9,
        )(meta, cot, par, logs, *terms, w, n1, joint, probs, mixed, res, n2)
        xgrad, *second = call(
            inputs_pull_kernel(sizes),
            [((total, width), f32)] + blocks(3 * half + LANES),
            [
                ((total, width), f32),
                ((total, 3 * half), bf16),
                ((width, 3 * half), f32),
                ((8, width), f32),
                ((total, width), bf16),
            ]
            + halves
            + [((width, 3 * width), bf16)],
            VMEM_MIB,
            flops=8 * 10**9,
            far_in=range(6, 10),
            sems=11,
        )(meta, x, par, gm, gj, part, early, w, n1, joint, probs)
        if shares:
            ends = [*scatter_pieces(*first, devices), *scatter_pieces(*second, devices)]
        else:
            ends = []
            for full in (first[0], second[0]):
                full = lax.psum_scatter(full, "fsdp", scatter_dimension=0, tiled=True)[None]
                ends += [full, jnp.zeros_like(full)]
        out_grad, in_grad, ns, nb, ms, mb, slot_grad = pl.pallas_call(
            finish_kernel(width, experts),
            out_shape=[jax.ShapeDtypeStruct((part_rows, c), f32) for c in (width, 3 * width)]
            + [jax.ShapeDtypeStruct((1, part_rows), f32)] * 4
            + [jax.ShapeDtypeStruct((experts, part_rows), f32)],
            in_specs=[vmem()] * 4,
            out_specs=[vmem()] * 7,
            scratch_shapes=[pltpu.VMEM((LANES, LANES), f32)],
        )(*ends)
        return (
            block.reshape(images.shape),
            xgrad.reshape(images.shape),
            ns.reshape(part_rows),
            nb.reshape(part_rows),
            in_grad,
            out_grad,
            ms.reshape(part_rows),
            mb.reshape(part_rows),
            slot_grad.T,
            jnp.swapaxes(expin_grad, 1, 2),
            expout_grad,
        )

    return shards


def solution(mesh):
    rows = P("fsdp", None, None)
    cols = P(None, None, "fsdp")
    mids = P(None, "fsdp", None)
    flat = P("fsdp", None)
    vec = P("fsdp")
    return jax.shard_map(
        build(mesh.shape["fsdp"]),
        mesh=mesh,
        in_specs=(rows, vec, vec, vec, flat, flat, vec, vec, flat, cols, mids, rows),
        out_specs=(rows, rows, vec, vec, flat, flat, vec, vec, flat, cols, mids),
        check_vma=False,
    )
```

```python
import jax
import jax.numpy as jnp
from jax import lax
from jax.experimental import pallas as pl
from jax.experimental.pallas import tpu as pltpu
from jax.sharding import PartitionSpec as P

HEADS = 12
NEGATIVE = -1e30
EPSILON = 1e-06
GELU_C = 0.7978845608
GELU_A = 0.044715
LANES = 128
CHUNK = 16
UNROLL = 13
VMEM_MIB = 28
MIB = 1 << 20

bf16 = jnp.bfloat16
f32 = jnp.float32


def dot(a, b, ca, cb):
    return lax.dot_general(a, b, (((ca,), (cb,)), ((), ())), preferred_element_type=f32)


def nn(a, b):
    return dot(a, b, 1, 0)


def nt(a, b):
    return dot(a, b, 1, 1)


def tn(a, b):
    return dot(a, b, 0, 0)


def vmem():
    return pl.BlockSpec(memory_space=pltpu.VMEM)


def hbm():
    return pl.BlockSpec(memory_space=pltpu.HBM)


def smem():
    return pl.BlockSpec(memory_space=pltpu.SMEM)


def call(body, outs, scratch, limit_mib, flops=0, far_in=(), far_out=(), sems=0):
    def run(scalars, *args):
        return pl.pallas_call(
            body,
            out_shape=[
                pltpu.HBM(s, d) if i in far_out else jax.ShapeDtypeStruct(s, d)
                for i, (s, d) in enumerate(outs)
            ],
            in_specs=[smem()] + [hbm() if i in far_in else vmem() for i in range(len(args))],
            out_specs=[hbm() if i in far_out else vmem() for i in range(len(outs))],
            scratch_shapes=[pltpu.VMEM(s, d) for s, d in scratch]
            + ([pltpu.SemaphoreType.DMA((sems,))] if sems else []),
            compiler_params=pltpu.CompilerParams(vmem_limit_bytes=limit_mib * MIB),
            cost_estimate=pl.CostEstimate(flops=flops, bytes_accessed=0, transcendentals=0),
        )(
            scalars,
            *[pltpu.with_memory_space_constraint(a, pltpu.HBM) if i in far_in else a for i, a in enumerate(args)],
        )

    return run


def rows_at(step, count):
    return pl.ds(pl.multiple_of(step * count, count), count)


def fold_rows(value):
    return value[:8] + value[8:]


def head_masks():
    lane = lax.broadcasted_iota(jnp.int32, (1, LANES), 1)
    return lane < LANES // 2


def stacked(pair):
    first = head_masks()
    zero = jnp.zeros_like(pair)
    return jnp.concatenate([jnp.where(first, pair, zero), jnp.where(first, zero, pair)], axis=0)


def unstacked(both):
    rows = both.shape[0] // 2
    return jnp.where(head_masks(), both[:rows], both[rows:])


def routing(logits, live):
    masked = jnp.where(live, logits, NEGATIVE)
    weight = jnp.exp(masked - jnp.max(masked, axis=1, keepdims=True))
    dispatch = weight / jnp.sum(weight, axis=1, keepdims=True)
    share = jnp.exp(logits - jnp.max(logits, axis=0, keepdims=True))
    combine = share / jnp.sum(share, axis=0, keepdims=True)
    return dispatch, combine


def pack_kernel(width, experts):
    def body(in_ref, out_ref, ns_ref, nb_ref, ms_ref, mb_ref, slot_ref, pack_ref, square):
        pack_ref[:, : 3 * width] = in_ref[...]
        pack_ref[:, 3 * width : 4 * width] = out_ref[...]
        rows = in_ref.shape[0]
        square[...] = jnp.zeros_like(square)
        for i, ref in enumerate((ns_ref, nb_ref, ms_ref, mb_ref)):
            square[i : i + 1, :rows] = ref[...].astype(f32)
        square[4 : 4 + experts, :rows] = slot_ref[...].astype(f32)
        pack_ref[:, 4 * width :] = square[...].T[:rows].astype(bf16)

    return body


def gathered_chip(f, chips):
    return (lax.axis_index("fsdp") // 2) ^ (f // 4 + (f % 4) * (chips // 4))


def scattered_chip(f, chips):
    k = f % 4
    return (lax.axis_index("fsdp") // 2) ^ (f // 4 + (k % 2) * (chips // 2) + (k // 2) * (chips // 4))


def assemble(first, share, chips, part_rows, own_ref, oth_ref, w_ref):
    columns = w_ref.shape[1]
    for own_first in (True, False):

        @pl.when(lax.axis_index("fsdp") % 2 == (0 if own_first else 1))
        def _():
            low_ref, high_ref = (own_ref, oth_ref) if own_first else (oth_ref, own_ref)
            for f in range(first, first + share):
                at = rows_at(gathered_chip(f, chips), 2 * part_rows)
                for c0 in range(0, columns, 640):
                    c1 = min(columns, c0 + 640)
                    both = [low_ref[f, :, c0:c1].astype(f32), high_ref[f, :, c0:c1].astype(f32)]
                    w_ref[at, c0:c1] = jnp.concatenate(both, axis=0).astype(bf16)


def cut(meta, images, chips, part_rows, tile, count, mine_ref, other_ref, first):
    for own_first in (True, False):

        @pl.when(lax.axis_index("fsdp") % 2 == (0 if own_first else 1))
        def _():
            @pl.loop(0, chips, unroll=4)
            def _(f):
                at = rows_at(scattered_chip(f, chips), 2 * part_rows)
                for c0 in range(0, count, 384):
                    c1 = min(count, c0 + 384)
                    both = tile[at, c0:c1]
                    low, high = both[:part_rows].astype(bf16), both[part_rows:].astype(bf16)
                    mine_ref[f, :, first + c0 : first + c1] = low if own_first else high
                    other_ref[f, :, first + c0 : first + c1] = high if own_first else low


def column_sums(ref):
    total = jnp.zeros((CHUNK, ref.shape[1]), f32)
    for i in range(ref.shape[0] // CHUNK):
        total = total + ref[i * CHUNK : (i + 1) * CHUNK].astype(f32)
    return jnp.sum(total, axis=0, keepdims=True)


def cut_scaled(chips, part_rows, tile, sums, w_ref, col_ref, small_ref, outs, first):
    count = tile.shape[1]
    rows = 2 * part_rows if len(outs) == 2 else 48
    lane = lax.broadcasted_iota(jnp.int32, (1, LANES), 1)

    def step(at, write):
        gain = col_ref[at, 0:1].astype(f32)
        shift = col_ref[at, 1:2].astype(f32)
        by_gain = jnp.zeros((rows, LANES), f32)
        by_shift = jnp.zeros((rows, LANES), f32)
        for c0 in range(0, count, LANES):
            c1 = c0 + LANES
            value, weight = tile[at, c0:c1], w_ref[at, c0:c1].astype(f32)
            by_gain = by_gain + value * weight
            by_shift = by_shift + sums[:, c0:c1] * weight
            write(c0, c1, value * gain + shift * sums[:, c0:c1])
        by_gain = jnp.sum(by_gain, axis=1, keepdims=True)
        by_shift = jnp.sum(by_shift, axis=1, keepdims=True)
        small_ref[at] = small_ref[at] + jnp.where(lane == 0, by_gain, jnp.where(lane == 1, by_shift, 0.0))

    if len(outs) == 1:

        @pl.loop(0, tile.shape[0] // rows)
        def _(i):
            at = rows_at(i, rows)

            def write(c0, c1, value):
                outs[0][at, first + c0 : first + c1] = value

            step(at, write)

        return
    for own_first in (True, False):

        @pl.when(lax.axis_index("fsdp") % 2 == (0 if own_first else 1))
        def _():
            low_ref, high_ref = outs if own_first else outs[::-1]

            @pl.loop(0, chips, unroll=2)
            def _(f):
                at = rows_at(scattered_chip(f, chips), rows)

                def write(c0, c1, value):
                    low_ref[f, :, first + c0 : first + c1] = value[:part_rows].astype(bf16)
                    high_ref[f, :, first + c0 : first + c1] = value[part_rows:].astype(bf16)

                step(at, write)


def weight_loads(width, half, w_in, w_ref, col_ref, sems):
    part = width // 2
    loads = [
        pltpu.make_async_copy(
            w_in.at[:, i * width + half * part : i * width + (half + 1) * part],
            w_ref.at[:, i * part : (i + 1) * part],
            sems.at[i],
        )
        for i in range(3)
    ]
    loads.append(pltpu.make_async_copy(w_in.at[:, 4 * width : 4 * width + LANES], col_ref, sems.at[3]))
    return loads


def forward_kernel(sizes):
    images, rows, width, experts, chips, part_rows, shares = sizes
    total = images * rows
    pairs = HEADS // 2
    pieces = len(shares)

    def body(meta, x_in, cot_in, *refs):
        ins, refs = refs[: 2 * pieces or 1], refs[2 * pieces or 1 :]
        par_ref, log_ref, slots_ref, xh_out, mixed_out, joint_out, probs_out, res_out, n2_out, *refs = refs
        if pieces:
            w_out, *refs = refs
        xh_ref, mixed_ref, joint_ref, probs_ref, res_ref, n2_ref, small, x_ref, cot_ref, n1_ref, *refs = refs
        given = [
            pltpu.make_async_copy(x_in, x_ref, refs[-1].at[8 + pairs + 2 * pieces]),
            pltpu.make_async_copy(cot_in, cot_ref, refs[-1].at[9 + pairs + 2 * pieces]),
        ]
        for load in given:
            load.start()
        if pieces:
            w_ref, own_ref, oth_ref, sems = refs
            loads, first = [], 0
            for i, share in enumerate(shares):
                loads.append(
                    [
                        pltpu.make_async_copy(
                            ins[side * pieces + i],
                            stage.at[first : first + share],
                            sems.at[8 + pairs + side * pieces + i],
                        )
                        for side, stage in enumerate((own_ref, oth_ref))
                    ]
                )
                first += share
            for load in sum(loads, []):
                load.start()
            first = 0
            for pair, share in zip(loads, shares):
                for load in pair:
                    load.wait()
                assemble(first, share, chips, part_rows, own_ref, oth_ref, w_ref)
                first += share
        else:
            (sems,) = refs
            w_ref = ins[0]
        stores = []

        def store(ref, out):
            stores.append(pltpu.make_async_copy(ref, out, sems.at[len(stores)]))
            stores[-1].start()

        if pieces:
            store(w_ref, w_out)
        par_ref[...] = w_ref[:, 4 * width : 4 * width + LANES].astype(f32).T[:8]
        gain_a, shift_a = par_ref[0:1], par_ref[1:2]
        gain_m, shift_m = par_ref[2:3], par_ref[3:4]
        for load in given:
            load.wait()

        @pl.loop(0, total // CHUNK, unroll=UNROLL)
        def _(i):
            at = rows_at(i, CHUNK)
            x = x_ref[at].astype(f32)
            x = x - jnp.mean(x, axis=-1, keepdims=True)
            rstd = lax.rsqrt(jnp.mean(x * x, axis=-1, keepdims=True) + EPSILON)
            x = x * rstd
            xh_ref[at] = x.astype(bf16)
            n1_ref[at] = (x * gain_a + shift_a).astype(bf16)

        store(xh_ref, xh_out)

        @pl.loop(0, 3)
        def _(i):
            at = rows_at(i, width)
            joint_ref[:, at] = nn(n1_ref[...], w_ref[:, at]).astype(bf16)

        store(joint_ref, joint_out)
        column = lax.broadcasted_iota(jnp.int32, (1, rows), 1)
        for p in range(pairs):
            at_q, at_k, at_v = [slice(i * width + p * LANES, i * width + (p + 1) * LANES) for i in range(3)]
            for img in range(images):
                span = slice(img * rows, (img + 1) * rows)
                query, key, value = joint_ref[span, at_q], joint_ref[span, at_k], joint_ref[span, at_v]
                scores = nt(stacked(query), key) * 0.125
                scores = jnp.where(column < meta[img], scores, NEGATIVE)
                weight = jnp.exp(scores - jnp.max(scores, axis=-1, keepdims=True))
                probs = weight * (1.0 / jnp.sum(weight, axis=-1, keepdims=True))
                probs = probs.astype(bf16)
                probs_ref[p, img] = probs
                mixed_ref[span, at_q] = unstacked(nn(probs, value)).astype(bf16)
            store(probs_ref.at[p], probs_out.at[p])
        store(mixed_ref, mixed_out)

        res_ref[...] = x_ref[...].astype(f32) + nn(mixed_ref[...], w_ref[:, 3 * width : 4 * width])
        store(res_ref, res_out)

        @pl.loop(0, total // CHUNK, unroll=UNROLL)
        def _(i):
            at = rows_at(i, CHUNK)
            x = res_ref[at]
            x = x - jnp.mean(x, axis=-1, keepdims=True)
            rstd = lax.rsqrt(jnp.mean(x * x, axis=-1, keepdims=True) + EPSILON)
            n2_ref[at] = (x * rstd * gain_m + shift_m).astype(bf16)

        store(n2_ref, n2_out)
        slot_w = par_ref[4 : 4 + experts].astype(bf16)
        for img in range(images):
            span = slice(img * rows, (img + 1) * rows)
            logits = nt(slot_w, n2_ref[span])
            log_ref[img] = logits
            live = column < meta[img]
            dispatch, combine = routing(logits, live)
            small[img * experts : (img + 1) * experts] = nn(dispatch.astype(bf16), n2_ref[span])
            combine = jnp.where(live, combine, 0.0).astype(bf16)
            small[(images + img) * experts : (images + img + 1) * experts] = nn(combine, cot_ref[span])
        slots_ref[...] = small[...].astype(bf16)
        for copy in stores:
            copy.wait()

    return body


def expert_kernel(images, experts, width, hidden, chips, pieces):
    lanes = -(-hidden // LANES) * LANES
    per = images * experts
    half = chips * per

    def body(_, *refs):
        own_refs, oth_refs, refs = refs[:pieces], refs[pieces : 2 * pieces], refs[2 * pieces :]
        in_ref, out_ref, mine_ref, other_ref, s_ref, g_ref, act_ref, gpre_ref, win, wout, so, gs = refs
        win[...] = jnp.zeros(win.shape, bf16)
        wout[...] = jnp.zeros(wout.shape, bf16)
        for e in range(experts):
            win[e * lanes : e * lanes + hidden, :] = in_ref[e]
            wout[e * lanes : e * lanes + hidden, :] = out_ref[e]

        for side, group in enumerate((own_refs, oth_refs)):
            for j, ref in enumerate(group):
                share = ref.shape[0] // 2

                @pl.loop(0, share)
                def _(i):
                    first, second = ref[2 * i].astype(f32), ref[2 * i + 1].astype(f32)
                    at = pl.ds(pl.multiple_of(side * half + (j * share + i) * 2 * per, 2 * per), 2 * per)
                    s_ref[at] = jnp.concatenate([first[:per], second[:per]], axis=0).astype(bf16)
                    g_ref[at] = jnp.concatenate([first[per:], second[per:]], axis=0).astype(bf16)

        block = 2 * half if 2 * half <= 256 else 256

        @pl.loop(0, 2 * half // block)
        def _(i):
            at = rows_at(i, block)
            so[at, : experts * lanes] = nt(s_ref[at], win[...])
            gs[at, : experts * lanes] = nt(g_ref[at], wout[...])

        @pl.loop(0, 2 * half // CHUNK, unroll=4)
        def _(i):
            at = rows_at(i, CHUNK)
            shape = (CHUNK, experts * lanes)
            keep = (lax.broadcasted_iota(jnp.int32, shape, 0) % experts) == (
                lax.broadcasted_iota(jnp.int32, shape, 1) // lanes
            )
            v = so[at, : experts * lanes]
            grad = gs[at, : experts * lanes]
            tanh = jnp.tanh(GELU_C * (v + GELU_A * v * v * v))
            act = 0.5 * v * (1.0 + tanh)
            slope = 0.5 * (1.0 + tanh) + 0.5 * v * (1.0 - tanh * tanh) * (
                GELU_C * (1.0 + 3.0 * GELU_A * v * v)
            )
            act_ref[at] = jnp.where(keep, act, 0.0).astype(bf16)
            gpre_ref[at] = jnp.where(keep, slope * grad, 0.0).astype(bf16)

        @pl.loop(0, 2 * half // block)
        def _(i):
            at = rows_at(i, block)
            so[at, :width] = nn(act_ref[at], wout[...])
            gs[at, :width] = nn(gpre_ref[at], win[...])

        for side, ref in enumerate((mine_ref, other_ref)):

            @pl.loop(0, chips)
            def _(f):
                at = pl.ds(pl.multiple_of(side * half + f * per, per), per)
                ref[f] = jnp.concatenate([so[at, :width], gs[at, :width]], axis=0).astype(bf16)

    return body


def expert_grad_kernel(experts, hidden):
    lanes = -(-hidden // LANES) * LANES

    def body(_, s_ref, g_ref, act_ref, gpre_ref, in_ref, out_ref):
        for e in range(experts):
            at = slice(e * lanes, (e + 1) * lanes)
            in_ref[e] = tn(gpre_ref[:, at], s_ref[...])[:hidden]
            out_ref[e] = tn(act_ref[:, at], g_ref[...])[:hidden]

    return body


def norm_pull(x, rstd, gain, grad):
    scaled = grad * gain
    first = jnp.mean(scaled, axis=-1, keepdims=True)
    second = jnp.mean(scaled * x, axis=-1, keepdims=True)
    return rstd * (scaled - first - x * second)


def attend_pull(meta, sizes, half, joint_ref, probs_ref, gm_ref, gj):
    images, rows, width, *_ = sizes
    share = HEADS // 4
    for q in range(share):
        at_q, at_k, at_v = [slice(i * width // 2 + q * LANES, i * width // 2 + (q + 1) * LANES) for i in range(3)]
        for img in range(images):
            span = slice(img * rows, (img + 1) * rows)
            query, key, value = joint_ref[span, at_q], joint_ref[span, at_k], joint_ref[span, at_v]
            p = half * share + q
            grad = stacked(gm_ref[span, p * LANES : (p + 1) * LANES])
            low = probs_ref[q, img]
            probs = low.astype(f32)
            grad_probs = nt(grad, value)
            row_dot = jnp.sum(probs * grad_probs, axis=-1, keepdims=True)
            grad_scores = (probs * (grad_probs - row_dot)).astype(bf16)
            gj[span, at_q] = (unstacked(nn(grad_scores, key)) * 0.125).astype(bf16)
            gj[span, at_k] = (tn(grad_scores, stacked(query)) * 0.125).astype(bf16)
            gj[span, at_v] = tn(low, grad).astype(bf16)


def half_loads(width, half, joint_in, joint_ref, probs_in, probs_ref, sems):
    part, share = width // 2, HEADS // 4
    loads = [
        pltpu.make_async_copy(
            joint_in.at[:, i * width + half * part : i * width + (half + 1) * part],
            joint_ref.at[:, i * part : (i + 1) * part],
            sems.at[i],
        )
        for i in range(3)
    ]
    loads.append(pltpu.make_async_copy(probs_in.at[half * share : (half + 1) * share], probs_ref, sems.at[3]))
    return loads


def second_norm_kernel(sizes):
    images, rows, width, *_ = sizes

    def body(meta, res_in, n2_in, xn_ref, dev_ref, n2_ref, res_ref, sems):
        loads = [pltpu.make_async_copy(res_in, res_ref, sems.at[0]), pltpu.make_async_copy(n2_in, n2_ref, sems.at[1])]
        for load in loads:
            load.start()
        loads[0].wait()

        @pl.loop(0, images * rows // CHUNK, unroll=UNROLL)
        def _(i):
            at = rows_at(i, CHUNK)
            x = res_ref[at]
            x = x - jnp.mean(x, axis=-1, keepdims=True)
            rstd = lax.rsqrt(jnp.mean(x * x, axis=-1, keepdims=True) + EPSILON)
            xn_ref[at] = x * rstd
            dev_ref[at] = jnp.broadcast_to(rstd, (CHUNK, LANES))

        loads[1].wait()

    return body


def slots_pull_kernel(sizes):
    images, rows, width, experts, chips, part_rows, shares = sizes
    pieces = len(shares)
    total = images * rows
    share = HEADS // 4

    def body(meta, cot_ref, par_ref, log_ref, sum_ref, r1_ref, r2_ref, r3_ref, xn_ref, dev_ref, n2_ref, w_in, xh_in,
             joint_in, probs_in, mixed_in, res_in, block_ref, xgrad_ref, gm, gj, grads, part_ref, xh_ref, w_half,
             joint_late, probs_late, *refs):
        outs, (gn, gb, tile, small, w_ref, joint_ref, probs_ref, mixed_ref, res_ref, col_ref, sems) = refs[:-11], refs[-11:]
        early = [pltpu.make_async_copy(res_in, res_ref, sems.at[0])]
        late = [
            pltpu.make_async_copy(mixed_in, mixed_ref, sems.at[1]),
            pltpu.make_async_copy(w_in.at[:, 3 * width : 4 * width], w_ref, sems.at[2]),
        ]
        loads = half_loads(width, 0, joint_in, joint_ref, probs_in, probs_ref, sems.at[3:7])
        last = [pltpu.make_async_copy(xh_in, xh_ref, sems.at[7])]
        last += weight_loads(width, 0, w_in, w_half, col_ref, sems.at[8:12])
        ahead = half_loads(width, 1, joint_in, joint_late, probs_in, probs_late, sems.at[12:16])
        for load in early + late + loads + last + ahead:
            load.start()

        def put(first, count):
            if pieces:
                cut(meta, images, chips, part_rows, tile, count, *outs, first)
            else:
                outs[0][:, first : first + count] = tile[:, :count]

        sums = sum_ref[0].astype(f32) + r1_ref[0].astype(f32) + r2_ref[0].astype(f32) + r3_ref[0].astype(f32)
        small[...] = sums.astype(bf16).astype(f32)
        slot_w = par_ref[4 : 4 + experts]
        column = lax.broadcasted_iota(jnp.int32, (1, rows), 1)
        slot_grad = jnp.zeros((experts, width), f32)
        for img in range(images):
            span = slice(img * rows, (img + 1) * rows)
            live = column < meta[img]
            dispatch, combine = routing(log_ref[img], live)
            out32 = small[img * experts : (img + 1) * experts]
            grad32 = small[(images + img) * experts : (images + img + 1) * experts]
            slot_out = out32.astype(bf16)
            grad_comb = jnp.where(live, nt(slot_out, cot_ref[span]), 0.0)
            grad_disp = nt(grad32.astype(bf16), n2_ref[span])
            grad_log = combine * (grad_comb - jnp.sum(combine * grad_comb, axis=0, keepdims=True))
            grad_log = grad_log + dispatch * (
                grad_disp - jnp.sum(dispatch * grad_disp, axis=1, keepdims=True)
            )
            slot_grad = slot_grad + nn(grad_log.astype(bf16), n2_ref[span])
            left = jnp.concatenate([dispatch, grad_log], axis=0).astype(bf16)
            right = jnp.concatenate([grad32, slot_w], axis=0).astype(bf16)
            gn[span] = tn(left, right)
            live_row = lax.broadcasted_iota(jnp.int32, (rows, 1), 0) < meta[img]
            expert_sum = tn(combine.astype(bf16), slot_out)
            for load in early if img == 0 else []:
                load.wait()
            block_ref[span] = jnp.where(live_row, res_ref[span] + expert_sum, 0.0).astype(bf16)
        grads[0:2] = jnp.zeros((2, width), f32)
        grads[4 : 4 + experts] = slot_grad

        gain_m = par_ref[2:3]
        zero = jnp.zeros((8, width), f32)
        for img in range(images):

            def step(i, carry):
                at = pl.ds(pl.multiple_of(img * rows + i * CHUNK, CHUNK), CHUNK)
                grad = gn[at]
                x = xn_ref[at]
                pulled = norm_pull(x, dev_ref[at, 0:1], gain_m, grad)
                row = i * CHUNK + lax.broadcasted_iota(jnp.int32, (CHUNK, 1), 0)
                pulled = pulled + jnp.where(row < meta[img], cot_ref[at].astype(f32), 0.0)
                xgrad_ref[at] = pulled
                gb[at] = pulled.astype(bf16)
                return carry[0] + fold_rows(grad * x), carry[1] + fold_rows(grad)

            sums = lax.fori_loop(0, rows // CHUNK, step, (zero, zero) if img == 0 else sums, unroll=UNROLL)
        grads[2:3] = jnp.sum(sums[0], axis=0, keepdims=True)
        grads[3:4] = jnp.sum(sums[1], axis=0, keepdims=True)

        for load in late:
            load.wait()
        tile[:, :width] = tn(mixed_ref[...], gb[...])
        put(0, width)
        gm[...] = nt(gb[...], w_ref[...]).astype(bf16)
        for load in loads:
            load.wait()
        attend_pull(meta, sizes, 0, joint_ref, probs_ref, gm, gj)
        for load in last:
            load.wait()
        tile[...] = tn(xh_ref[...], gj[...])
        part_ref[...] = jnp.zeros_like(part_ref)
        cut_scaled(chips, part_rows, tile, column_sums(gj), w_half, col_ref, part_ref, outs, width)
        for load in ahead:
            load.wait()

    return body


def heads_pull_kernel(sizes):
    width = sizes[2]

    def body(meta, gm_ref, joint_ref, probs_ref, w_in, gj, w_half, col_ref, sems):
        loads = weight_loads(width, 1, w_in, w_half, col_ref, sems)
        for load in loads:
            load.start()
        attend_pull(meta, sizes, 1, joint_ref, probs_ref, gm_ref, gj)
        for load in loads:
            load.wait()

    return body


def heads_grad_kernel(sizes):
    images, rows, width, experts, chips, part_rows, shares = sizes
    half = 3 * width // 2

    def body(meta, gj, grads, part_ref, w_half, col_ref, xh_ref, *refs):
        outs, (tile, small) = refs[:-2], refs[-2:]
        filled = jnp.concatenate([grads[...], jnp.zeros((LANES - 8, width), f32)], axis=0)
        small[...] = part_ref[...] + filled.T
        tile[...] = tn(xh_ref[...], gj[...])
        cut_scaled(chips, part_rows, tile, column_sums(gj), w_half, col_ref, small, outs, 0)
        if shares:
            cut(meta, images, chips, part_rows, small, LANES, *outs, half)
        else:
            outs[0][:, half : half + LANES] = small[...]

    return body


def inputs_pull_kernel(sizes):
    images, rows, width, experts, chips, part_rows, shares = sizes
    total = images * rows
    half = 3 * width // 2

    def body(meta, x_ref, par_ref, gj0_ref, gj1_ref, w0_ref, w1_ref, part_ref, xgrad_ref, gn):
        gn[...] = nt(gj0_ref[...], w0_ref[...]) + nt(gj1_ref[...], w1_ref[...])
        gain_a = par_ref[0:1]

        @pl.loop(0, total // CHUNK, unroll=UNROLL)
        def _(i):
            at = rows_at(i, CHUNK)
            x = x_ref[at].astype(f32)
            x = x - jnp.mean(x, axis=-1, keepdims=True)
            rstd = lax.rsqrt(jnp.mean(x * x, axis=-1, keepdims=True) + EPSILON)
            xgrad_ref[at] = part_ref[at] + norm_pull(x * rstd, rstd, gain_a, gn[at])

    return body


def split_sum(parts, first_type=f32):
    def run(*args):
        count, rest = args[0].shape[0], args[0].shape[1:]
        share = count // parts

        def body(*refs):
            ins, outs = refs[: len(args)], refs[len(args) :]
            for part in range(parts):

                @pl.loop(0, share)
                def _(i):
                    total = ins[0][part * share + i].astype(f32)
                    for ref in ins[1:]:
                        total = total + ref[part * share + i].astype(f32)
                    outs[part][i] = total.astype(outs[part].dtype)

        types = [first_type] + [bf16] * (parts - 1)
        return pl.pallas_call(
            body,
            out_shape=[jax.ShapeDtypeStruct((share,) + rest, t) for t in types],
            in_specs=[vmem()] * len(args),
            out_specs=[vmem()] * parts,
            compiler_params=pltpu.CompilerParams(vmem_limit_bytes=32 * MIB),
        )(*args)

    return run


def add_kernel(groups, types, share=2):
    def run(*args):
        rest = args[0].shape[1:]
        sizes = [share * len(g) for g in groups]

        def body(*refs):
            ins, outs = refs[: len(args)], refs[len(args) :]
            for out, group in zip(outs, groups):
                for j, terms in enumerate(group):
                    for i in range(share):
                        total = ins[terms[0][0]][terms[0][1] + i].astype(f32)
                        for a, first in terms[1:]:
                            total = total + ins[a][first + i].astype(f32)
                        out[j * share + i] = total.astype(out.dtype)

        return pl.pallas_call(
            body,
            out_shape=[jax.ShapeDtypeStruct((c,) + rest, t) for c, t in zip(sizes, types)],
            in_specs=[vmem()] * len(args),
            out_specs=[vmem()] * len(groups),
            compiler_params=pltpu.CompilerParams(vmem_limit_bytes=16 * MIB),
        )(*args)

    return run


def finish_kernel(width, experts):
    half = width // 2

    def body(a0, a1, b0, b1, out_ref, in_ref, ns_ref, nb_ref, ms_ref, mb_ref, slot_ref, square):
        first = a0[0] + a1[0].astype(f32)
        second = b0[0] + b1[0].astype(f32)
        rows = first.shape[0]
        out_ref[...] = first[:, :width]
        for i in range(3):
            in_ref[:, i * width : i * width + half] = first[:, width + i * half : width + (i + 1) * half]
            in_ref[:, i * width + half : (i + 1) * width] = second[:, i * half : (i + 1) * half]
        small = second[:, 3 * half : 3 * half + LANES]
        square[...] = jnp.zeros_like(square)
        square[:rows] = small
        turned = square[...].T
        for i, ref in enumerate((ns_ref, nb_ref, ms_ref, mb_ref)):
            ref[...] = turned[i : i + 1, :rows]
        slot_ref[...] = turned[4 : 4 + experts, :rows]

    return body


def stages_of(devices):
    chips = devices // 2
    groups, bit = [], 1
    while bit < chips:
        count = min(4, chips // bit)
        groups.append([bit * i for i in range(count)])
        bit *= count
    return groups


def swap(value, devices, chip_offset, core_offset):
    mask = 2 * chip_offset + core_offset
    return lax.ppermute(value, "fsdp", [(i, i ^ mask) for i in range(devices)])


def gather_slots(block, devices):
    *lower, last = stages_of(devices)[::-1]
    for group in lower:
        parts = [block] + [swap(block, devices, o, 0) for o in group[1:]]
        block = jnp.concatenate(parts, axis=0)
    own = [block] + [swap(block, devices, o, 0) for o in last[1:]]
    return own, [swap(part, devices, 0, 1) for part in own]


def scatter_chips(mine, other, devices):
    terms = [mine, swap(other, devices, 0, 1)]
    for group in stages_of(devices):
        parts = split_sum(len(group))(*terms)
        terms = [parts[0]] + [swap(p, devices, o, 0) for p, o in zip(parts[1:], group[1:])]
    return terms


SHARES = (2,) * 8


def gather_pieces(block, devices):
    block = block[None]
    far = swap(block, devices, 8, 0)
    z0 = jnp.concatenate([block, swap(block, devices, 4, 0)], axis=0)
    x0, y0 = swap(z0, devices, 1, 0), swap(z0, devices, 2, 0)
    z1 = jnp.concatenate([far, swap(far, devices, 4, 0)], axis=0)
    x1, y1 = swap(z1, devices, 1, 0), swap(z1, devices, 2, 0)
    d0, d1 = swap(y0, devices, 1, 0), swap(x1, devices, 2, 0)
    own = [z0, z1, x0, x1, y0, y1, d0, d1]
    return own + [swap(piece, devices, 0, 1) for piece in own]


def after(values, events):
    return lax.optimization_barrier((*values, *events))[: len(values)]


def scatter_begin(mine, other, devices, events=()):
    got = swap(other, devices, 0, 1)
    if events:
        (got,) = after([got], events)
    z0, z1, x0, x1, y0, y1, d0, d1 = [[(0, i), (1, i)] for i in range(0, 16, 2)]
    return add_kernel(
        [[z0], [z1], [d0, x0], [d1, y1], [x1], [y0]], [f32, f32, bf16, bf16, bf16, bf16]
    )(mine, got)


def scatter_middle(parts, devices, events=()):
    z0, z1, to_x, to_y, x1, y0 = parts
    from_x, from_y = swap(to_x, devices, 1, 0), swap(to_y, devices, 2, 0)
    if events:
        x1, y0 = after([x1, y0], events)
    x1, y0 = add_kernel([[[(0, 0), (2, 0)]], [[(1, 0), (3, 0)]]], [bf16, bf16])(x1, y0, from_y, from_x)
    return z0, z1, x1, y0, from_x, from_y


def scatter_near(parts, devices):
    z0, z1, x1, y0, from_x, from_y = parts
    from_x1, from_y0 = swap(x1, devices, 1, 0), swap(y0, devices, 2, 0)
    (z1,) = add_kernel([[[(0, 0), (1, 0), (2, 2)]]], [bf16])(z1, from_x1, from_y)
    return z0, from_x, from_y0, swap(z1, devices, 4, 0)


def scatter_end(parts, devices):
    z0, from_x, from_y0, from_z1 = parts
    keep, send = add_kernel(
        [[[(0, i), (1, 2 + i), (2, i), (3, i)]] for i in range(2)], [f32, bf16], 1
    )(z0, from_x, from_y0, from_z1)
    return keep, swap(send, devices, 8, 0)


def build(devices):
    def shards(images, lengths, norm_scale, norm_shift, attend_in, attend_out, mixer_scale, mixer_shift,
               slot_params, expert_in, expert_out, cotangent):
        count, rows, width = images.shape
        experts, _, hidden = expert_in.shape
        part_rows = attend_in.shape[0]
        chips = devices // 2
        total = count * rows
        pairs = HEADS // 2
        half = width // 2
        wide = 4 * width + LANES
        shares = SHARES if part_rows % 8 == 0 and chips == 16 else ()
        sizes = (count, rows, width, experts, chips, part_rows, shares)
        meta = lengths
        x = images.reshape(total, width)
        cot = cotangent.reshape(total, width)
        vectors = [v.reshape(1, part_rows) for v in (norm_scale, norm_shift, mixer_scale, mixer_shift)]
        pack = pl.pallas_call(
            pack_kernel(width, experts),
            out_shape=jax.ShapeDtypeStruct((part_rows, wide), bf16),
            in_specs=[vmem()] * 7,
            out_specs=vmem(),
            scratch_shapes=[pltpu.VMEM((LANES, LANES), f32)],
        )(attend_in, attend_out, *vectors, slot_params.T)
        if shares:
            weights = gather_pieces(pack, devices)
        else:
            weights = [lax.all_gather(pack, "fsdp", axis=0, tiled=True)]
        kept = [
            ((total, width), bf16),
            ((total, width), bf16),
            ((total, 3 * width), bf16),
            ((pairs, count, 2 * rows, rows), bf16),
            ((total, width), f32),
            ((total, width), bf16),
        ]
        outs = [
            ((8, width), f32),
            ((count, experts, rows), f32),
            ((2 * count * experts, width), bf16),
        ] + kept
        scratch = kept + [((2 * count * experts, width), f32)] + [((total, width), bf16)] * 3
        if shares:
            outs.append(((width, wide), bf16))
            scratch += [outs[-1]] + [((chips, part_rows, wide), bf16)] * 2
        par, logs, slots, xh, mixed, joint, probs, res, n2, *more = call(
            forward_kernel(sizes),
            outs,
            scratch,
            40,
            far_in=range(0, 2 + 2 * len(shares)),
            far_out=range(3, len(outs)),
            sems=10 + pairs + 2 * len(shares),
        )(meta, x, cot, *weights)
        w = more[0] if shares else weights[0]

        own, oth = gather_slots(slots[None], devices)
        lanes = -(-hidden // LANES) * LANES
        held = devices * count * experts
        most = max(width, experts * lanes)
        mine, other, s_all, g_all, act, gpre = call(
            expert_kernel(count, experts, width, hidden, chips, len(own)),
            [
                ((chips, 2 * count * experts, width), bf16),
                ((chips, 2 * count * experts, width), bf16),
                ((held, width), bf16),
                ((held, width), bf16),
                ((held, experts * lanes), bf16),
                ((held, experts * lanes), bf16),
            ],
            [
                ((experts * lanes, width), bf16),
                ((experts * lanes, width), bf16),
                ((held, most), f32),
                ((held, most), f32),
            ],
            24 if held <= 256 else 56,
        )(meta, *own, *oth, jnp.swapaxes(expert_in, 1, 2), expert_out)
        expin_grad, expout_grad = call(
            expert_grad_kernel(experts, hidden),
            [((experts, hidden, width), f32), ((experts, hidden, width), f32)],
            [],
            24 if held <= 256 else 56,
            flops=2 * 10**9,
        )(meta, s_all, g_all, act, gpre)
        terms = scatter_chips(mine, other, devices)
        if len(terms) < 4:
            terms = terms + [jnp.zeros_like(terms[-1])] * (4 - len(terms))
        terms[0], expin_grad, expout_grad = lax.optimization_barrier((terms[0], expin_grad, expout_grad))

        def blocks(columns):
            if shares:
                return [((chips, part_rows, columns), bf16)] * 2
            return [((width, columns), f32)]

        halves = [((total, 3 * half), bf16), ((pairs // 2, count, 2 * rows, rows), bf16)]
        xn, dev, n2 = call(
            second_norm_kernel(sizes),
            [((total, width), f32), ((total, LANES), f32), ((total, width), bf16)],
            [((total, width), f32)],
            16,
            flops=10**9,
            far_in=range(2),
            sems=2,
        )(meta, res, n2)
        columns = ((width, 3 * half), bf16)
        block, part, gm, gj, early, tiny, xh, w0, joint1, probs1, *first = call(
            slots_pull_kernel(sizes),
            [
                ((total, width), bf16),
                ((total, width), f32),
                ((total, width), bf16),
                ((total, 3 * half), bf16),
                ((8, width), f32),
                ((width, LANES), f32),
                ((total, width), bf16),
                columns,
            ]
            + halves
            + blocks(width + 3 * half),
            [
                ((total, width), f32),
                ((total, width), bf16),
                ((width, 3 * half), f32),
                ((2 * count * experts, width), f32),
                ((width, width), bf16),
            ]
            + halves
            + [
                ((total, width), bf16),
                ((total, width), f32),
                ((width, LANES), bf16),
            ],
            VMEM_MIB,
            far_in=range(10, 16),
            sems=16,
        )(meta, cot, par, logs, *terms, xn, dev, n2, w, xh, joint, probs, mixed, res)
        gj1, w1, tail = call(
            heads_pull_kernel(sizes),
            [((total, 3 * half), bf16), columns, ((width, LANES), bf16)],
            [],
            VMEM_MIB,
            flops=3 * 10**9,
            far_in=range(3, 4),
            sems=4,
        )(meta, gm, joint1, probs1, w)
        gj_late = gj1
        if shares:
            first = scatter_begin(*first, devices)
            gj_late = after([gj1], first)[0]
        second = call(
            heads_grad_kernel(sizes),
            blocks(3 * half + LANES),
            [((width, 3 * half), f32), ((width, LANES), f32)],
            VMEM_MIB,
            flops=4 * 10**9,
        )(meta, gj_late, early, tiny, w1, tail, xh)
        if shares:
            first = scatter_middle(first, devices)
            second = scatter_begin(*after(second, first[2:4]), devices)
            part = after([part], [*second, first[2]])[0]
            first = scatter_near(first, devices)
        xgrad = call(
            inputs_pull_kernel(sizes),
            [((total, width), f32)],
            [((total, width), f32)],
            VMEM_MIB,
            flops=5 * 10**9,
        )(meta, x, par, gj, gj1, w0, w1, part)[0]
        if shares:
            second = scatter_middle(second, devices, [xgrad, first[2]])
            second = scatter_near(second, devices)
            ends = [*scatter_end(first, devices), *scatter_end(second, devices)]
        else:
            ends = []
            for full in (first[0], second[0]):
                full = lax.psum_scatter(full, "fsdp", scatter_dimension=0, tiled=True)[None]
                ends += [full, jnp.zeros_like(full)]
        out_grad, in_grad, ns, nb, ms, mb, slot_grad = pl.pallas_call(
            finish_kernel(width, experts),
            out_shape=[jax.ShapeDtypeStruct((part_rows, c), f32) for c in (width, 3 * width)]
            + [jax.ShapeDtypeStruct((1, part_rows), f32)] * 4
            + [jax.ShapeDtypeStruct((experts, part_rows), f32)],
            in_specs=[vmem()] * 4,
            out_specs=[vmem()] * 7,
            scratch_shapes=[pltpu.VMEM((LANES, LANES), f32)],
        )(*ends)
        return (
            block.reshape(images.shape),
            xgrad.reshape(images.shape),
            ns.reshape(part_rows),
            nb.reshape(part_rows),
            in_grad,
            out_grad,
            ms.reshape(part_rows),
            mb.reshape(part_rows),
            slot_grad.T,
            jnp.swapaxes(expin_grad, 1, 2),
            expout_grad,
        )

    return shards


def solution(mesh):
    rows = P("fsdp", None, None)
    cols = P(None, None, "fsdp")
    mids = P(None, "fsdp", None)
    flat = P("fsdp", None)
    vec = P("fsdp")
    return jax.shard_map(
        build(mesh.shape["fsdp"]),
        mesh=mesh,
        in_specs=(rows, vec, vec, vec, flat, flat, vec, vec, flat, cols, mids, rows),
        out_specs=(rows, rows, vec, vec, flat, flat, vec, vec, flat, cols, mids),
        check_vma=False,
    )
```

```python
import jax
import jax.numpy as jnp
from jax import lax
from jax.experimental import pallas as pl
from jax.experimental.pallas import tpu as pltpu
from jax.sharding import PartitionSpec as P

HEADS = 12
NEGATIVE = -1e30
EPSILON = 1e-06
GELU_C = 0.7978845608
GELU_A = 0.044715
LANES = 128
CHUNK = 16
UNROLL = 13
VMEM_MIB = 28
MIB = 1 << 20

bf16 = jnp.bfloat16
f32 = jnp.float32


def dot(a, b, ca, cb):
    return lax.dot_general(a, b, (((ca,), (cb,)), ((), ())), preferred_element_type=f32)


def nn(a, b):
    return dot(a, b, 1, 0)


def nt(a, b):
    return dot(a, b, 1, 1)


def tn(a, b):
    return dot(a, b, 0, 0)


def vmem():
    return pl.BlockSpec(memory_space=pltpu.VMEM)


def anywhere():
    return pl.BlockSpec(memory_space=pl.ANY)


def hbm():
    return pl.BlockSpec(memory_space=pltpu.HBM)


def smem():
    return pl.BlockSpec(memory_space=pltpu.SMEM)


def call(body, outs, scratch, limit_mib, flops=0, far_in=(), any_in=(), far_out=(), sems=0):
    def run(scalars, *args):
        return pl.pallas_call(
            body,
            out_shape=[
                pltpu.HBM(s, d) if i in far_out else jax.ShapeDtypeStruct(s, d)
                for i, (s, d) in enumerate(outs)
            ],
            in_specs=[smem()]
            + [hbm() if i in far_in else anywhere() if i in any_in else vmem() for i in range(len(args))],
            out_specs=[hbm() if i in far_out else vmem() for i in range(len(outs))],
            scratch_shapes=[pltpu.VMEM(s, d) for s, d in scratch]
            + ([pltpu.SemaphoreType.DMA((sems,))] if sems else []),
            compiler_params=pltpu.CompilerParams(vmem_limit_bytes=limit_mib * MIB),
            cost_estimate=pl.CostEstimate(flops=flops, bytes_accessed=0, transcendentals=0),
        )(
            scalars,
            *[pltpu.with_memory_space_constraint(a, pltpu.HBM) if i in far_in else a for i, a in enumerate(args)],
        )

    return run


def rows_at(step, count):
    return pl.ds(pl.multiple_of(step * count, count), count)


def fold_rows(value):
    return value[:8] + value[8:]


def head_masks():
    lane = lax.broadcasted_iota(jnp.int32, (1, LANES), 1)
    return lane < LANES // 2


def stacked(pair):
    first = head_masks()
    zero = jnp.zeros_like(pair)
    return jnp.concatenate([jnp.where(first, pair, zero), jnp.where(first, zero, pair)], axis=0)


def unstacked(both):
    rows = both.shape[0] // 2
    return jnp.where(head_masks(), both[:rows], both[rows:])


def routing(logits, live):
    masked = jnp.where(live, logits, NEGATIVE)
    weight = jnp.exp(masked - jnp.max(masked, axis=1, keepdims=True))
    dispatch = weight / jnp.sum(weight, axis=1, keepdims=True)
    share = jnp.exp(logits - jnp.max(logits, axis=0, keepdims=True))
    combine = share / jnp.sum(share, axis=0, keepdims=True)
    return dispatch, combine


def pack_kernel(width, experts):
    def body(*refs):
        given, pack_ref, square, here, sems = refs[:7], refs[7], refs[8], refs[9:16], refs[16]
        loads = [pltpu.make_async_copy(a, b, sems.at[i]) for i, (a, b) in enumerate(zip(given, here))]
        for load in loads:
            load.start()
        for load in loads:
            load.wait()
        in_ref, out_ref, ns_ref, nb_ref, ms_ref, mb_ref, slot_ref = here
        pack_ref[:, : 3 * width] = in_ref[...]
        pack_ref[:, 3 * width : 4 * width] = out_ref[...]
        rows = in_ref.shape[0]
        square[...] = jnp.zeros_like(square)
        for i, ref in enumerate((ns_ref, nb_ref, ms_ref, mb_ref)):
            square[i : i + 1, :rows] = ref[...].astype(f32)
        square[4 : 4 + experts, :rows] = slot_ref[...].astype(f32)
        pack_ref[:, 4 * width :] = square[...].T[:rows].astype(bf16)

    return body


def gathered_chip(f, chips):
    return (lax.axis_index("fsdp") // 2) ^ (f // 4 + (f % 4) * (chips // 4))


def scattered_chip(f, chips):
    k = f % 4
    return (lax.axis_index("fsdp") // 2) ^ (f // 4 + (k % 2) * (chips // 2) + (k // 2) * (chips // 4))


def assemble(first, share, chips, part_rows, own_ref, oth_ref, w_ref):
    columns = w_ref.shape[1]
    for own_first in (True, False):

        @pl.when(lax.axis_index("fsdp") % 2 == (0 if own_first else 1))
        def _():
            low_ref, high_ref = (own_ref, oth_ref) if own_first else (oth_ref, own_ref)
            for f in range(first, first + share):
                at = rows_at(gathered_chip(f, chips), 2 * part_rows)
                for c0 in range(0, columns, 640):
                    c1 = min(columns, c0 + 640)
                    both = [low_ref[f, :, c0:c1].astype(f32), high_ref[f, :, c0:c1].astype(f32)]
                    w_ref[at, c0:c1] = jnp.concatenate(both, axis=0).astype(bf16)


def cut(meta, images, chips, part_rows, tile, count, mine_ref, other_ref, first):
    for own_first in (True, False):

        @pl.when(lax.axis_index("fsdp") % 2 == (0 if own_first else 1))
        def _():
            @pl.loop(0, chips, unroll=4)
            def _(f):
                at = rows_at(scattered_chip(f, chips), 2 * part_rows)
                for c0 in range(0, count, 384):
                    c1 = min(count, c0 + 384)
                    both = tile[at, c0:c1]
                    low, high = both[:part_rows].astype(bf16), both[part_rows:].astype(bf16)
                    mine_ref[f, :, first + c0 : first + c1] = low if own_first else high
                    other_ref[f, :, first + c0 : first + c1] = high if own_first else low


def column_sums(ref):
    total = jnp.zeros((CHUNK, ref.shape[1]), f32)
    for i in range(ref.shape[0] // CHUNK):
        total = total + ref[i * CHUNK : (i + 1) * CHUNK].astype(f32)
    return jnp.sum(total, axis=0, keepdims=True)


def weight_loads(width, w_in, w_ref, sems):
    part = width // 2
    loads = []
    for i in range(6):
        first = (i % 3) * width + (i // 3) * part
        loads.append(
            pltpu.make_async_copy(
                w_in.at[:, first : first + part], w_ref.at[:, i * part : (i + 1) * part], sems.at[i]
            )
        )
    return loads


def forward_kernel(sizes):
    images, rows, width, experts, chips, part_rows, shares = sizes
    total = images * rows
    pairs = HEADS // 2
    pieces = len(shares)

    def body(meta, x_in, cot_in, *refs):
        ins, refs = refs[: 2 * pieces or 1], refs[2 * pieces or 1 :]
        par_ref, log_ref, slots_ref, xh_out, mixed_out, joint_out, probs_out, res_out, n2_out, *refs = refs
        if pieces:
            w_out, *refs = refs
        xh_ref, mixed_ref, joint_ref, probs_ref, res_ref, n2_ref, small, x_ref, cot_ref, n1_ref, *refs = refs
        given = [
            pltpu.make_async_copy(x_in, x_ref, refs[-1].at[8 + pairs + 2 * pieces]),
            pltpu.make_async_copy(cot_in, cot_ref, refs[-1].at[9 + pairs + 2 * pieces]),
        ]
        for load in given:
            load.start()
        if pieces:
            w_ref, own_ref, oth_ref, sems = refs
            loads, first = [], 0
            for i, share in enumerate(shares):
                loads.append(
                    [
                        pltpu.make_async_copy(
                            ins[side * pieces + i],
                            stage.at[first : first + share],
                            sems.at[8 + pairs + side * pieces + i],
                        )
                        for side, stage in enumerate((own_ref, oth_ref))
                    ]
                )
                first += share
            for load in sum(loads, []):
                load.start()
            first = 0
            for pair, share in zip(loads, shares):
                for load in pair:
                    load.wait()
                assemble(first, share, chips, part_rows, own_ref, oth_ref, w_ref)
                first += share
        else:
            (sems,) = refs
            w_ref = ins[0]
        stores = []

        def store(ref, out):
            stores.append(pltpu.make_async_copy(ref, out, sems.at[len(stores)]))
            stores[-1].start()

        if pieces:
            store(w_ref, w_out)
        par_ref[...] = w_ref[:, 4 * width : 4 * width + LANES].astype(f32).T[:8]
        gain_a, shift_a = par_ref[0:1], par_ref[1:2]
        gain_m, shift_m = par_ref[2:3], par_ref[3:4]
        for load in given:
            load.wait()

        @pl.loop(0, total // CHUNK, unroll=UNROLL)
        def _(i):
            at = rows_at(i, CHUNK)
            x = x_ref[at].astype(f32)
            x = x - jnp.mean(x, axis=-1, keepdims=True)
            rstd = lax.rsqrt(jnp.mean(x * x, axis=-1, keepdims=True) + EPSILON)
            x = x * rstd
            xh_ref[at] = x.astype(bf16)
            n1_ref[at] = (x * gain_a + shift_a).astype(bf16)

        store(xh_ref, xh_out)

        @pl.loop(0, 3)
        def _(i):
            at = rows_at(i, width)
            joint_ref[:, at] = nn(n1_ref[...], w_ref[:, at]).astype(bf16)

        store(joint_ref, joint_out)
        column = lax.broadcasted_iota(jnp.int32, (1, rows), 1)
        for p in range(pairs):
            at_q, at_k, at_v = [slice(i * width + p * LANES, i * width + (p + 1) * LANES) for i in range(3)]
            for img in range(images):
                span = slice(img * rows, (img + 1) * rows)
                query, key, value = joint_ref[span, at_q], joint_ref[span, at_k], joint_ref[span, at_v]
                scores = nt(stacked(query), key) * 0.125
                scores = jnp.where(column < meta[img], scores, NEGATIVE)
                weight = jnp.exp(scores - jnp.max(scores, axis=-1, keepdims=True))
                probs = weight * (1.0 / jnp.sum(weight, axis=-1, keepdims=True))
                probs = probs.astype(bf16)
                probs_ref[p, img] = probs
                mixed_ref[span, at_q] = unstacked(nn(probs, value)).astype(bf16)
            store(probs_ref.at[p], probs_out.at[p])
        store(mixed_ref, mixed_out)

        res_ref[...] = x_ref[...].astype(f32) + nn(mixed_ref[...], w_ref[:, 3 * width : 4 * width])
        store(res_ref, res_out)

        @pl.loop(0, total // CHUNK, unroll=UNROLL)
        def _(i):
            at = rows_at(i, CHUNK)
            x = res_ref[at]
            x = x - jnp.mean(x, axis=-1, keepdims=True)
            rstd = lax.rsqrt(jnp.mean(x * x, axis=-1, keepdims=True) + EPSILON)
            n2_ref[at] = (x * rstd * gain_m + shift_m).astype(bf16)

        store(n2_ref, n2_out)
        slot_w = par_ref[4 : 4 + experts].astype(bf16)
        for img in range(images):
            span = slice(img * rows, (img + 1) * rows)
            logits = nt(slot_w, n2_ref[span])
            log_ref[img] = logits
            live = column < meta[img]
            dispatch, combine = routing(logits, live)
            small[img * experts : (img + 1) * experts] = nn(dispatch.astype(bf16), n2_ref[span])
            combine = jnp.where(live, combine, 0.0).astype(bf16)
            small[(images + img) * experts : (images + img + 1) * experts] = nn(combine, cot_ref[span])
        slots_ref[...] = small[...].astype(bf16)
        for copy in stores:
            copy.wait()

    return body


def expert_kernel(images, experts, width, hidden, chips, pieces):
    lanes = -(-hidden // LANES) * LANES
    per = images * experts
    half = chips * per

    def body(_, *refs):
        own_refs, oth_refs, refs = refs[:pieces], refs[pieces : 2 * pieces], refs[2 * pieces :]
        in_ref, out_ref, mine_ref, other_ref, s_ref, g_ref, act_ref, gpre_ref, win, wout, so, gs = refs
        win[...] = jnp.zeros(win.shape, bf16)
        wout[...] = jnp.zeros(wout.shape, bf16)
        for e in range(experts):
            win[e * lanes : e * lanes + hidden, :] = in_ref[e]
            wout[e * lanes : e * lanes + hidden, :] = out_ref[e]

        for side, group in enumerate((own_refs, oth_refs)):
            for j, ref in enumerate(group):
                share = ref.shape[0] // 2

                @pl.loop(0, share)
                def _(i):
                    first, second = ref[2 * i].astype(f32), ref[2 * i + 1].astype(f32)
                    at = pl.ds(pl.multiple_of(side * half + (j * share + i) * 2 * per, 2 * per), 2 * per)
                    s_ref[at] = jnp.concatenate([first[:per], second[:per]], axis=0).astype(bf16)
                    g_ref[at] = jnp.concatenate([first[per:], second[per:]], axis=0).astype(bf16)

        block = 2 * half if 2 * half <= 256 else 256

        @pl.loop(0, 2 * half // block)
        def _(i):
            at = rows_at(i, block)
            so[at, : experts * lanes] = nt(s_ref[at], win[...])
            gs[at, : experts * lanes] = nt(g_ref[at], wout[...])

        @pl.loop(0, 2 * half // CHUNK, unroll=4)
        def _(i):
            at = rows_at(i, CHUNK)
            shape = (CHUNK, experts * lanes)
            keep = (lax.broadcasted_iota(jnp.int32, shape, 0) % experts) == (
                lax.broadcasted_iota(jnp.int32, shape, 1) // lanes
            )
            v = so[at, : experts * lanes]
            grad = gs[at, : experts * lanes]
            tanh = jnp.tanh(GELU_C * (v + GELU_A * v * v * v))
            act = 0.5 * v * (1.0 + tanh)
            slope = 0.5 * (1.0 + tanh) + 0.5 * v * (1.0 - tanh * tanh) * (
                GELU_C * (1.0 + 3.0 * GELU_A * v * v)
            )
            act_ref[at] = jnp.where(keep, act, 0.0).astype(bf16)
            gpre_ref[at] = jnp.where(keep, slope * grad, 0.0).astype(bf16)

        @pl.loop(0, 2 * half // block)
        def _(i):
            at = rows_at(i, block)
            so[at, :width] = nn(act_ref[at], wout[...])
            gs[at, :width] = nn(gpre_ref[at], win[...])

        for side, ref in enumerate((mine_ref, other_ref)):

            @pl.loop(0, chips)
            def _(f):
                at = pl.ds(pl.multiple_of(side * half + f * per, per), per)
                ref[f] = jnp.concatenate([so[at, :width], gs[at, :width]], axis=0).astype(bf16)

    return body


def expert_grad_kernel(experts, hidden):
    lanes = -(-hidden // LANES) * LANES

    def body(_, s_ref, g_ref, act_ref, gpre_ref, in_ref, out_ref):
        for e in range(experts):
            at = slice(e * lanes, (e + 1) * lanes)
            in_ref[e] = tn(gpre_ref[:, at], s_ref[...])[:hidden]
            out_ref[e] = tn(act_ref[:, at], g_ref[...])[:hidden]

    return body


def norm_pull(x, rstd, gain, grad):
    scaled = grad * gain
    first = jnp.mean(scaled, axis=-1, keepdims=True)
    second = jnp.mean(scaled * x, axis=-1, keepdims=True)
    return rstd * (scaled - first - x * second)


def attend_pull(meta, sizes, half, joint_ref, probs_ref, gm_ref, gj):
    images, rows, width, *_ = sizes
    share = HEADS // 4
    for q in range(share):
        at_q, at_k, at_v = [slice(i * width // 2 + q * LANES, i * width // 2 + (q + 1) * LANES) for i in range(3)]
        for img in range(images):
            span = slice(img * rows, (img + 1) * rows)
            query, key, value = joint_ref[span, at_q], joint_ref[span, at_k], joint_ref[span, at_v]
            p = half * share + q
            grad = stacked(gm_ref[span, p * LANES : (p + 1) * LANES])
            low = probs_ref[q, img]
            probs = low.astype(f32)
            grad_probs = nt(grad, value)
            row_dot = jnp.sum(probs * grad_probs, axis=-1, keepdims=True)
            grad_scores = (probs * (grad_probs - row_dot)).astype(bf16)
            gj[span, at_q] = (unstacked(nn(grad_scores, key)) * 0.125).astype(bf16)
            gj[span, at_k] = (tn(grad_scores, stacked(query)) * 0.125).astype(bf16)
            gj[span, at_v] = tn(low, grad).astype(bf16)


def sums_lanes(width, part_rows):
    return slice(8, 8 + 3 * width // part_rows)


def small_lanes(width, part_rows):
    return -(-sums_lanes(width, part_rows).stop // LANES) * LANES


def half_loads(width, half, joint_in, joint_ref, probs_in, probs_ref, sems):
    part, share = width // 2, HEADS // 4
    loads = [
        pltpu.make_async_copy(
            joint_in.at[:, i * width + half * part : i * width + (half + 1) * part],
            joint_ref.at[:, i * part : (i + 1) * part],
            sems.at[i],
        )
        for i in range(3)
    ]
    loads.append(pltpu.make_async_copy(probs_in.at[half * share : (half + 1) * share], probs_ref, sems.at[3]))
    return loads


def second_norm_kernel(sizes):
    images, rows, width, *_ = sizes

    def body(meta, res_in, n2_in, xn_ref, dev_ref, n2_ref, res_ref, sems):
        loads = [pltpu.make_async_copy(res_in, res_ref, sems.at[0]), pltpu.make_async_copy(n2_in, n2_ref, sems.at[1])]
        for load in loads:
            load.start()
        loads[0].wait()

        @pl.loop(0, images * rows // CHUNK, unroll=UNROLL)
        def _(i):
            at = rows_at(i, CHUNK)
            x = res_ref[at]
            x = x - jnp.mean(x, axis=-1, keepdims=True)
            rstd = lax.rsqrt(jnp.mean(x * x, axis=-1, keepdims=True) + EPSILON)
            xn_ref[at] = x * rstd
            dev_ref[at] = jnp.broadcast_to(rstd, (CHUNK, LANES))

        loads[1].wait()

    return body


def slots_pull_kernel(sizes):
    images, rows, width, experts, chips, part_rows, shares = sizes
    pieces = len(shares)
    total = images * rows
    share = HEADS // 4

    def body(meta, cot_ref, par_ref, log_ref, sum_ref, r1_ref, r2_ref, r3_ref, xn_ref, dev_ref, n2_ref, w_in, xh_in,
             joint_in, probs_in, mixed_in, res_in, block_ref, xgrad_ref, gm, gj, grads, sums_ref, xh_ref,
             joint_late, probs_late, *refs):
        outs, (gn, gb, tile, small, w_ref, joint_ref, probs_ref, mixed_ref, res_ref, sems) = refs[:-10], refs[-10:]
        early = [pltpu.make_async_copy(res_in, res_ref, sems.at[0])]
        late = [
            pltpu.make_async_copy(mixed_in, mixed_ref, sems.at[1]),
            pltpu.make_async_copy(w_in.at[:, 3 * width : 4 * width], w_ref, sems.at[2]),
        ]
        loads = half_loads(width, 0, joint_in, joint_ref, probs_in, probs_ref, sems.at[3:7])
        last = [pltpu.make_async_copy(xh_in, xh_ref, sems.at[7])]
        ahead = half_loads(width, 1, joint_in, joint_late, probs_in, probs_late, sems.at[8:12])
        for load in early + late + loads + last + ahead:
            load.start()

        def put(first, count):
            if pieces:
                cut(meta, images, chips, part_rows, tile, count, *outs, first)
            else:
                outs[0][:, first : first + count] = tile[:, :count]

        sums = sum_ref[0].astype(f32) + r1_ref[0].astype(f32) + r2_ref[0].astype(f32) + r3_ref[0].astype(f32)
        small[...] = sums.astype(bf16).astype(f32)
        slot_w = par_ref[4 : 4 + experts]
        column = lax.broadcasted_iota(jnp.int32, (1, rows), 1)
        slot_grad = jnp.zeros((experts, width), f32)
        for img in range(images):
            span = slice(img * rows, (img + 1) * rows)
            live = column < meta[img]
            dispatch, combine = routing(log_ref[img], live)
            out32 = small[img * experts : (img + 1) * experts]
            grad32 = small[(images + img) * experts : (images + img + 1) * experts]
            slot_out = out32.astype(bf16)
            grad_comb = jnp.where(live, nt(slot_out, cot_ref[span]), 0.0)
            grad_disp = nt(grad32.astype(bf16), n2_ref[span])
            grad_log = combine * (grad_comb - jnp.sum(combine * grad_comb, axis=0, keepdims=True))
            grad_log = grad_log + dispatch * (
                grad_disp - jnp.sum(dispatch * grad_disp, axis=1, keepdims=True)
            )
            slot_grad = slot_grad + nn(grad_log.astype(bf16), n2_ref[span])
            left = jnp.concatenate([dispatch, grad_log], axis=0).astype(bf16)
            right = jnp.concatenate([grad32, slot_w], axis=0).astype(bf16)
            gn[span] = tn(left, right)
            live_row = lax.broadcasted_iota(jnp.int32, (rows, 1), 0) < meta[img]
            expert_sum = tn(combine.astype(bf16), slot_out)
            for load in early if img == 0 else []:
                load.wait()
            block_ref[span] = jnp.where(live_row, res_ref[span] + expert_sum, 0.0).astype(bf16)
        grads[0:2] = jnp.zeros((2, width), f32)
        grads[4 : 4 + experts] = slot_grad

        gain_m = par_ref[2:3]
        zero = jnp.zeros((8, width), f32)
        for img in range(images):

            def step(i, carry):
                at = pl.ds(pl.multiple_of(img * rows + i * CHUNK, CHUNK), CHUNK)
                grad = gn[at]
                x = xn_ref[at]
                pulled = norm_pull(x, dev_ref[at, 0:1], gain_m, grad)
                row = i * CHUNK + lax.broadcasted_iota(jnp.int32, (CHUNK, 1), 0)
                pulled = pulled + jnp.where(row < meta[img], cot_ref[at].astype(f32), 0.0)
                xgrad_ref[at] = pulled
                gb[at] = pulled.astype(bf16)
                return carry[0] + fold_rows(grad * x), carry[1] + fold_rows(grad)

            sums = lax.fori_loop(0, rows // CHUNK, step, (zero, zero) if img == 0 else sums, unroll=UNROLL)
        grads[2:3] = jnp.sum(sums[0], axis=0, keepdims=True)
        grads[3:4] = jnp.sum(sums[1], axis=0, keepdims=True)

        for load in late:
            load.wait()
        tile[:, :width] = tn(mixed_ref[...], gb[...])
        put(0, width)
        gm[...] = nt(gb[...], w_ref[...]).astype(bf16)
        for load in loads:
            load.wait()
        attend_pull(meta, sizes, 0, joint_ref, probs_ref, gm, gj)
        for load in last:
            load.wait()
        tile[...] = tn(xh_ref[...], gj[...])
        sums_ref[0:1] = column_sums(gj)
        put(width, 3 * width // 2)
        for load in ahead:
            load.wait()

    return body


def heads_pull_kernel(sizes):
    width = sizes[2]

    def body(meta, gm_ref, joint_ref, probs_ref, gj):
        attend_pull(meta, sizes, 1, joint_ref, probs_ref, gm_ref, gj)

    return body


def heads_grad_kernel(sizes):
    images, rows, width, experts, chips, part_rows, shares = sizes
    half = 3 * width // 2

    def body(meta, gj, grads, sums_ref, xh_ref, w_in, w_ref, *refs):
        outs, (tile, small, sems) = refs[:-3], refs[-3:]
        loads = weight_loads(width, w_in, w_ref, sems)
        for load in loads:
            load.start()
        sums = [sums_ref[0:1], column_sums(gj)]
        wide = sums_lanes(width, part_rows)
        small[:, :LANES] = jnp.concatenate([grads[...], jnp.zeros((LANES - 8, width), f32)], axis=0).T
        each = 3 * width // part_rows
        for r in range(part_rows):
            row = [s[:, c0 - i * half : c1 - i * half] for i, s in enumerate(sums)
                   for c0, c1 in [(max(r * each, i * half), min((r + 1) * each, (i + 1) * half))] if c0 < c1]
            small[r : r + 1, wide] = jnp.concatenate(row, axis=1)
        for t in range(1, width // part_rows):
            small[t * part_rows : (t + 1) * part_rows, wide] = small[:part_rows, wide]
        tile[...] = tn(xh_ref[...], gj[...])

        def put(ref, count, first):
            if shares:
                cut(meta, images, chips, part_rows, ref, count, *outs, first)
            else:
                outs[0][:, first : first + count] = ref[:, :count]

        put(tile, half, 0)
        put(small, small.shape[1], half)
        for load in loads:
            load.wait()

    return body


def inputs_pull_kernel(sizes):
    images, rows, width, experts, chips, part_rows, shares = sizes
    total = images * rows
    half = 3 * width // 2

    def body(meta, x_ref, par_ref, gj0_ref, gj1_ref, w_ref, part_ref, xgrad_ref, gn):
        gn[...] = nt(gj0_ref[...], w_ref[:, :half]) + nt(gj1_ref[...], w_ref[:, half:])
        gain_a = par_ref[0:1]

        @pl.loop(0, total // CHUNK, unroll=UNROLL)
        def _(i):
            at = rows_at(i, CHUNK)
            x = x_ref[at].astype(f32)
            x = x - jnp.mean(x, axis=-1, keepdims=True)
            rstd = lax.rsqrt(jnp.mean(x * x, axis=-1, keepdims=True) + EPSILON)
            xgrad_ref[at] = part_ref[at] + norm_pull(x * rstd, rstd, gain_a, gn[at])

    return body


def split_sum(parts, first_type=f32):
    def run(*args):
        count, rest = args[0].shape[0], args[0].shape[1:]
        share = count // parts

        def body(*refs):
            ins, outs = refs[: len(args)], refs[len(args) :]
            for part in range(parts):

                @pl.loop(0, share)
                def _(i):
                    total = ins[0][part * share + i].astype(f32)
                    for ref in ins[1:]:
                        total = total + ref[part * share + i].astype(f32)
                    outs[part][i] = total.astype(outs[part].dtype)

        types = [first_type] + [bf16] * (parts - 1)
        return pl.pallas_call(
            body,
            out_shape=[jax.ShapeDtypeStruct((share,) + rest, t) for t in types],
            in_specs=[vmem()] * len(args),
            out_specs=[vmem()] * parts,
            compiler_params=pltpu.CompilerParams(vmem_limit_bytes=32 * MIB),
        )(*args)

    return run


def add_kernel(groups, types, share=2):
    def run(*args):
        rest = args[0].shape[1:]
        sizes = [share * len(g) for g in groups]

        def body(*refs):
            ins, outs = refs[: len(args)], refs[len(args) :]
            for out, group in zip(outs, groups):
                for j, terms in enumerate(group):
                    for i in range(share):
                        total = ins[terms[0][0]][terms[0][1] + i].astype(f32)
                        for a, first in terms[1:]:
                            total = total + ins[a][first + i].astype(f32)
                        out[j * share + i] = total.astype(out.dtype)

        return pl.pallas_call(
            body,
            out_shape=[jax.ShapeDtypeStruct((c,) + rest, t) for c, t in zip(sizes, types)],
            in_specs=[vmem()] * len(args),
            out_specs=[vmem()] * len(groups),
            compiler_params=pltpu.CompilerParams(vmem_limit_bytes=16 * MIB),
        )(*args)

    return run


def finish_kernel(width, experts, part_rows):
    half = width // 2
    wide = sums_lanes(width, part_rows)

    def body(a0, a1, b0, b1, w_ref, gain_ref, shift_ref, out_ref, in_ref, ns_ref, nb_ref, ms_ref, mb_ref, slot_ref,
             square, sums):
        first = a0[0] + a1[0].astype(f32)
        second = b0[0] + b1[0].astype(f32)
        out_ref[...] = first[:, :width]
        small = second[:, 3 * half :]
        each = 3 * width // part_rows
        for r in range(part_rows):
            sums[0:1, r * each : (r + 1) * each] = small[r : r + 1, wide]
        square[...] = jnp.zeros_like(square)
        square[0:1, :part_rows] = gain_ref[...].astype(f32)
        square[1:2, :part_rows] = shift_ref[...].astype(f32)
        turned = square[...].T
        gain, shift = turned[:part_rows, 0:1], turned[:part_rows, 1:2]
        by_gain = jnp.zeros((part_rows, half), f32)
        by_shift = jnp.zeros((part_rows, half), f32)
        for i in range(3):
            for j, value in enumerate((first[:, width + i * half : width + (i + 1) * half], second[:, i * half : (i + 1) * half])):
                at = slice(i * width + j * half, i * width + (j + 1) * half)
                total = sums[0:1, (j * 3 + i) * half : (j * 3 + i + 1) * half]
                weight = w_ref[:, at].astype(f32)
                in_ref[:, at] = value * gain + shift * total
                by_gain = by_gain + value * weight
                by_shift = by_shift + total * weight
        lane = lax.broadcasted_iota(jnp.int32, (1, LANES), 1)
        small = jnp.where(lane == 0, jnp.sum(by_gain, axis=1, keepdims=True), small[:, :LANES])
        small = jnp.where(lane == 1, jnp.sum(by_shift, axis=1, keepdims=True), small)
        square[:part_rows] = small
        turned = square[...].T
        for i, ref in enumerate((ns_ref, nb_ref, ms_ref, mb_ref)):
            ref[...] = turned[i : i + 1, :part_rows]
        slot_ref[...] = turned[4 : 4 + experts, :part_rows]

    return body


def stages_of(devices):
    chips = devices // 2
    groups, bit = [], 1
    while bit < chips:
        count = min(4, chips // bit)
        groups.append([bit * i for i in range(count)])
        bit *= count
    return groups


def swap(value, devices, chip_offset, core_offset):
    mask = 2 * chip_offset + core_offset
    return lax.ppermute(value, "fsdp", [(i, i ^ mask) for i in range(devices)])


def gather_slots(block, devices):
    *lower, last = stages_of(devices)[::-1]
    for group in lower:
        parts = [block] + [swap(block, devices, o, 0) for o in group[1:]]
        block = jnp.concatenate(parts, axis=0)
    own = [block] + [swap(block, devices, o, 0) for o in last[1:]]
    return own, [swap(part, devices, 0, 1) for part in own]


def scatter_chips(mine, other, devices):
    terms = [mine, swap(other, devices, 0, 1)]
    for group in stages_of(devices):
        parts = split_sum(len(group))(*terms)
        terms = [parts[0]] + [swap(p, devices, o, 0) for p, o in zip(parts[1:], group[1:])]
    return terms


SHARES = (2,) * 8


def gather_pieces(block, devices):
    block = block[None]
    far = swap(block, devices, 8, 0)
    z0 = jnp.concatenate([block, swap(block, devices, 4, 0)], axis=0)
    x0, y0 = swap(z0, devices, 1, 0), swap(z0, devices, 2, 0)
    z1 = jnp.concatenate([far, swap(far, devices, 4, 0)], axis=0)
    x1, y1 = swap(z1, devices, 1, 0), swap(z1, devices, 2, 0)
    d0, d1 = swap(y0, devices, 1, 0), swap(x1, devices, 2, 0)
    own = [z0, z1, x0, x1, y0, y1, d0, d1]
    return own + [swap(piece, devices, 0, 1) for piece in own]


def after(values, events):
    return lax.optimization_barrier((*values, *events))[: len(values)]


def scatter_begin(mine, other, devices, events=()):
    got = swap(other, devices, 0, 1)
    if events:
        (got,) = after([got], events)
    z0, z1, x0, x1, y0, y1, d0, d1 = [[(0, i), (1, i)] for i in range(0, 16, 2)]
    return add_kernel(
        [[z0], [z1], [d0, x0], [d1, y1], [x1], [y0]], [f32, f32, bf16, bf16, bf16, bf16]
    )(mine, got)


def scatter_middle(parts, devices, events=()):
    z0, z1, to_x, to_y, x1, y0 = parts
    from_x, from_y = swap(to_x, devices, 1, 0), swap(to_y, devices, 2, 0)
    if events:
        x1, y0 = after([x1, y0], events)
    x1, y0 = add_kernel([[[(0, 0), (2, 0)]], [[(1, 0), (3, 0)]]], [bf16, bf16])(x1, y0, from_y, from_x)
    return z0, z1, x1, y0, from_x, from_y


def scatter_near(parts, devices):
    z0, z1, x1, y0, from_x, from_y = parts
    from_x1, from_y0 = swap(x1, devices, 1, 0), swap(y0, devices, 2, 0)
    (z1,) = add_kernel([[[(0, 0), (1, 0), (2, 2)]]], [bf16])(z1, from_x1, from_y)
    return z0, from_x, from_y0, swap(z1, devices, 4, 0), z1


def scatter_end(parts, devices):
    z0, from_x, from_y0, from_z1, _ = parts
    keep, send = add_kernel(
        [[[(0, i), (1, 2 + i), (2, i), (3, i)]] for i in range(2)], [f32, bf16], 1
    )(z0, from_x, from_y0, from_z1)
    return keep, swap(send, devices, 8, 0)


def build(devices):
    def shards(images, lengths, norm_scale, norm_shift, attend_in, attend_out, mixer_scale, mixer_shift,
               slot_params, expert_in, expert_out, cotangent):
        count, rows, width = images.shape
        experts, _, hidden = expert_in.shape
        part_rows = attend_in.shape[0]
        chips = devices // 2
        total = count * rows
        pairs = HEADS // 2
        half = width // 2
        wide = 4 * width + LANES
        shares = SHARES if part_rows % 8 == 0 and chips == 16 else ()
        sizes = (count, rows, width, experts, chips, part_rows, shares)
        meta = lengths
        x = images.reshape(total, width)
        cot = cotangent.reshape(total, width)
        vectors = [v.reshape(1, part_rows) for v in (norm_scale, norm_shift, mixer_scale, mixer_shift)]
        given = [attend_in, attend_out, *vectors, slot_params.T]
        pack = pl.pallas_call(
            pack_kernel(width, experts),
            out_shape=jax.ShapeDtypeStruct((part_rows, wide), bf16),
            in_specs=[hbm()] * 7,
            out_specs=vmem(),
            scratch_shapes=[pltpu.VMEM((LANES, LANES), f32)]
            + [pltpu.VMEM(a.shape, bf16) for a in given]
            + [pltpu.SemaphoreType.DMA((7,))],
            compiler_params=pltpu.CompilerParams(vmem_limit_bytes=8 * MIB),
        )(*[pltpu.with_memory_space_constraint(a, pltpu.HBM) for a in given])
        if shares:
            weights = gather_pieces(pack, devices)
        else:
            weights = [lax.all_gather(pack, "fsdp", axis=0, tiled=True)]
        kept = [
            ((total, width), bf16),
            ((total, width), bf16),
            ((total, 3 * width), bf16),
            ((pairs, count, 2 * rows, rows), bf16),
            ((total, width), f32),
            ((total, width), bf16),
        ]
        outs = [
            ((8, width), f32),
            ((count, experts, rows), f32),
            ((2 * count * experts, width), bf16),
        ] + kept
        scratch = kept + [((2 * count * experts, width), f32)] + [((total, width), bf16)] * 3
        if shares:
            outs.append(((width, wide), bf16))
            scratch += [outs[-1]] + [((chips, part_rows, wide), bf16)] * 2
        par, logs, slots, xh, mixed, joint, probs, res, n2, *more = call(
            forward_kernel(sizes),
            outs,
            scratch,
            40,
            far_in=range(2),
            any_in=range(2, 2 + 2 * len(shares)),
            far_out=range(3, len(outs)),
            sems=10 + pairs + 2 * len(shares),
        )(meta, x, cot, *weights)
        w = more[0] if shares else weights[0]

        own, oth = gather_slots(slots[None], devices)
        lanes = -(-hidden // LANES) * LANES
        held = devices * count * experts
        most = max(width, experts * lanes)
        mine, other, s_all, g_all, act, gpre = call(
            expert_kernel(count, experts, width, hidden, chips, len(own)),
            [
                ((chips, 2 * count * experts, width), bf16),
                ((chips, 2 * count * experts, width), bf16),
                ((held, width), bf16),
                ((held, width), bf16),
                ((held, experts * lanes), bf16),
                ((held, experts * lanes), bf16),
            ],
            [
                ((experts * lanes, width), bf16),
                ((experts * lanes, width), bf16),
                ((held, most), f32),
                ((held, most), f32),
            ],
            24 if held <= 256 else 56,
        )(meta, *own, *oth, jnp.swapaxes(expert_in, 1, 2), expert_out)
        expin_grad, expout_grad = call(
            expert_grad_kernel(experts, hidden),
            [((experts, hidden, width), f32), ((experts, hidden, width), f32)],
            [],
            24 if held <= 256 else 56,
            flops=2 * 10**9,
        )(meta, s_all, g_all, act, gpre)
        terms = scatter_chips(mine, other, devices)
        if len(terms) < 4:
            terms = terms + [jnp.zeros_like(terms[-1])] * (4 - len(terms))
        terms[0], expin_grad, expout_grad = lax.optimization_barrier((terms[0], expin_grad, expout_grad))

        def blocks(columns):
            if shares:
                return [((chips, part_rows, columns), bf16)] * 2
            return [((width, columns), f32)]

        halves = [((total, 3 * half), bf16), ((pairs // 2, count, 2 * rows, rows), bf16)]
        xn, dev, n2 = call(
            second_norm_kernel(sizes),
            [((total, width), f32), ((total, LANES), f32), ((total, width), bf16)],
            [((total, width), f32)],
            16,
            flops=10**9,
            far_in=range(2),
            sems=2,
        )(meta, res, n2)
        block, part, gm, gj, early, sums, xh, joint1, probs1, *first = call(
            slots_pull_kernel(sizes),
            [
                ((total, width), bf16),
                ((total, width), f32),
                ((total, width), bf16),
                ((total, 3 * half), bf16),
                ((8, width), f32),
                ((8, 3 * half), f32),
                ((total, width), bf16),
            ]
            + halves
            + blocks(width + 3 * half),
            [
                ((total, width), f32),
                ((total, width), bf16),
                ((width, 3 * half), f32),
                ((2 * count * experts, width), f32),
                ((width, width), bf16),
            ]
            + halves
            + [
                ((total, width), bf16),
                ((total, width), f32),
            ],
            VMEM_MIB,
            far_in=range(10, 16),
            sems=12,
        )(meta, cot, par, logs, *terms, xn, dev, n2, w, xh, joint, probs, mixed, res)
        gj1 = call(
            heads_pull_kernel(sizes), [((total, 3 * half), bf16)], [], VMEM_MIB, flops=3 * 10**9
        )(meta, gm, joint1, probs1)[0]
        gj_late = gj1
        if shares:
            first = scatter_begin(*first, devices)
            gj_late = after([gj1], first)[0]
        tiny = small_lanes(width, part_rows)
        w_all, *second = call(
            heads_grad_kernel(sizes),
            [((width, 3 * width), bf16)] + blocks(3 * half + tiny),
            [((width, 3 * half), f32), ((width, tiny), f32)],
            VMEM_MIB,
            flops=4 * 10**9,
            far_in=range(4, 5),
            sems=6,
        )(meta, gj_late, early, sums, xh, w)
        if shares:
            second = scatter_begin(*second, devices)
            part = after([part], second)[0]
        xgrad = call(
            inputs_pull_kernel(sizes),
            [((total, width), f32)],
            [((total, width), f32)],
            VMEM_MIB,
            flops=5 * 10**9,
        )(meta, x, par, gj, gj1, w_all, part)[0]
        if shares:
            first = scatter_middle(first, devices, [xgrad])
            second = scatter_middle(second, devices, first[2:4])
            first, second = scatter_near(first, devices), scatter_near(second, devices)
            ends = [*scatter_end(first, devices), *scatter_end(second, devices)]
        else:
            ends = []
            for full in (first[0], second[0]):
                full = lax.psum_scatter(full, "fsdp", scatter_dimension=0, tiled=True)[None]
                ends += [full, jnp.zeros_like(full)]
        out_grad, in_grad, ns, nb, ms, mb, slot_grad = pl.pallas_call(
            finish_kernel(width, experts, part_rows),
            out_shape=[jax.ShapeDtypeStruct((part_rows, c), f32) for c in (width, 3 * width)]
            + [jax.ShapeDtypeStruct((1, part_rows), f32)] * 4
            + [jax.ShapeDtypeStruct((experts, part_rows), f32)],
            in_specs=[vmem()] * 7,
            out_specs=[vmem()] * 7,
            scratch_shapes=[pltpu.VMEM((LANES, LANES), f32), pltpu.VMEM((8, 3 * width), f32)],
            compiler_params=pltpu.CompilerParams(vmem_limit_bytes=8 * MIB),
        )(*ends, attend_in, *vectors[:2])
        return (
            block.reshape(images.shape),
            xgrad.reshape(images.shape),
            ns.reshape(part_rows),
            nb.reshape(part_rows),
            in_grad,
            out_grad,
            ms.reshape(part_rows),
            mb.reshape(part_rows),
            slot_grad.T,
            jnp.swapaxes(expin_grad, 1, 2),
            expout_grad,
        )

    return shards


def solution(mesh):
    rows = P("fsdp", None, None)
    cols = P(None, None, "fsdp")
    mids = P(None, "fsdp", None)
    flat = P("fsdp", None)
    vec = P("fsdp")
    return jax.shard_map(
        build(mesh.shape["fsdp"]),
        mesh=mesh,
        in_specs=(rows, vec, vec, vec, flat, flat, vec, vec, flat, cols, mids, rows),
        out_specs=(rows, rows, vec, vec, flat, flat, vec, vec, flat, cols, mids),
        check_vma=False,
    )
```

```python
import jax
import jax.numpy as jnp
from jax import lax
from jax.experimental import pallas as pl
from jax.experimental.pallas import tpu as pltpu
from jax.sharding import PartitionSpec as P

HEADS = 12
NEGATIVE = -1e30
EPSILON = 1e-06
GELU_C = 0.7978845608
GELU_A = 0.044715
LANES = 128
CHUNK = 16
UNROLL = 13
VMEM_MIB = 28
MIB = 1 << 20

bf16 = jnp.bfloat16
f32 = jnp.float32


def dot(a, b, ca, cb):
    return lax.dot_general(a, b, (((ca,), (cb,)), ((), ())), preferred_element_type=f32)


def nn(a, b):
    return dot(a, b, 1, 0)


def nt(a, b):
    return dot(a, b, 1, 1)


def tn(a, b):
    return dot(a, b, 0, 0)


def vmem():
    return pl.BlockSpec(memory_space=pltpu.VMEM)


def anywhere():
    return pl.BlockSpec(memory_space=pl.ANY)


def hbm():
    return pl.BlockSpec(memory_space=pltpu.HBM)


def smem():
    return pl.BlockSpec(memory_space=pltpu.SMEM)


def call(body, outs, scratch, limit_mib, flops=0, far_in=(), any_in=(), far_out=(), sems=0):
    def run(scalars, *args):
        return pl.pallas_call(
            body,
            out_shape=[
                pltpu.HBM(s, d) if i in far_out else jax.ShapeDtypeStruct(s, d)
                for i, (s, d) in enumerate(outs)
            ],
            in_specs=[smem()]
            + [hbm() if i in far_in else anywhere() if i in any_in else vmem() for i in range(len(args))],
            out_specs=[hbm() if i in far_out else vmem() for i in range(len(outs))],
            scratch_shapes=[pltpu.VMEM(s, d) for s, d in scratch]
            + ([pltpu.SemaphoreType.DMA((sems,))] if sems else []),
            compiler_params=pltpu.CompilerParams(vmem_limit_bytes=limit_mib * MIB),
            cost_estimate=pl.CostEstimate(flops=flops, bytes_accessed=0, transcendentals=0),
        )(
            scalars,
            *[pltpu.with_memory_space_constraint(a, pltpu.HBM) if i in far_in else a for i, a in enumerate(args)],
        )

    return run


def rows_at(step, count):
    return pl.ds(pl.multiple_of(step * count, count), count)


def fold_rows(value):
    return value[:8] + value[8:]


def head_masks():
    lane = lax.broadcasted_iota(jnp.int32, (1, LANES), 1)
    return lane < LANES // 2


def stacked(pair):
    first = head_masks()
    zero = jnp.zeros_like(pair)
    return jnp.concatenate([jnp.where(first, pair, zero), jnp.where(first, zero, pair)], axis=0)


def beside(left, right):
    return jnp.concatenate([left, right], axis=1)


def unstacked(both):
    rows = both.shape[0] // 2
    return jnp.where(head_masks(), both[:rows], both[rows:])


def routing(logits, live):
    masked = jnp.where(live, logits, NEGATIVE)
    weight = jnp.exp(masked - jnp.max(masked, axis=1, keepdims=True))
    dispatch = weight / jnp.sum(weight, axis=1, keepdims=True)
    share = jnp.exp(logits - jnp.max(logits, axis=0, keepdims=True))
    combine = share / jnp.sum(share, axis=0, keepdims=True)
    return dispatch, combine


def pack_kernel(width, experts):
    def body(*refs):
        given, pack_ref, square, here, sems = refs[:7], refs[7], refs[8], refs[9:16], refs[16]
        loads = [pltpu.make_async_copy(a, b, sems.at[i]) for i, (a, b) in enumerate(zip(given, here))]
        for load in loads:
            load.start()
        for load in loads:
            load.wait()
        in_ref, out_ref, ns_ref, nb_ref, ms_ref, mb_ref, slot_ref = here
        pack_ref[:, : 3 * width] = in_ref[...]
        pack_ref[:, 3 * width : 4 * width] = out_ref[...]
        rows = in_ref.shape[0]
        square[...] = jnp.zeros_like(square)
        for i, ref in enumerate((ns_ref, nb_ref, ms_ref, mb_ref)):
            square[i : i + 1, :rows] = ref[...].astype(f32)
        square[4 : 4 + experts, :rows] = slot_ref[...].astype(f32)
        pack_ref[:, 4 * width :] = square[...].T[:rows].astype(bf16)

    return body


def gathered_chip(f, chips):
    return (lax.axis_index("fsdp") // 2) ^ (f // 4 + (f % 4) * (chips // 4))


def scattered_chip(f, chips):
    k = f % 4
    return (lax.axis_index("fsdp") // 2) ^ (f // 4 + (k % 2) * (chips // 2) + (k // 2) * (chips // 4))


def assemble(first, share, chips, part_rows, own_ref, oth_ref, w_ref):
    columns = w_ref.shape[1]
    for own_first in (True, False):

        @pl.when(lax.axis_index("fsdp") % 2 == (0 if own_first else 1))
        def _():
            low_ref, high_ref = (own_ref, oth_ref) if own_first else (oth_ref, own_ref)
            for f in range(first, first + share):
                at = rows_at(gathered_chip(f, chips), 2 * part_rows)
                for c0 in range(0, columns, 640):
                    c1 = min(columns, c0 + 640)
                    both = [low_ref[f, :, c0:c1].astype(f32), high_ref[f, :, c0:c1].astype(f32)]
                    w_ref[at, c0:c1] = jnp.concatenate(both, axis=0).astype(bf16)


def cut(meta, images, chips, part_rows, tile, count, mine_ref, other_ref, first):
    for own_first in (True, False):

        @pl.when(lax.axis_index("fsdp") % 2 == (0 if own_first else 1))
        def _():
            @pl.loop(0, chips, unroll=4)
            def _(f):
                at = rows_at(scattered_chip(f, chips), 2 * part_rows)
                for c0 in range(0, count, 384):
                    c1 = min(count, c0 + 384)
                    both = tile[at, c0:c1]
                    low, high = both[:part_rows].astype(bf16), both[part_rows:].astype(bf16)
                    mine_ref[f, :, first + c0 : first + c1] = low if own_first else high
                    other_ref[f, :, first + c0 : first + c1] = high if own_first else low


def column_sums(ref):
    total = jnp.zeros((CHUNK, ref.shape[1]), f32)
    for i in range(ref.shape[0] // CHUNK):
        total = total + ref[i * CHUNK : (i + 1) * CHUNK].astype(f32)
    return jnp.sum(total, axis=0, keepdims=True)


def weight_loads(width, w_in, w_ref, sems):
    part = width // 2
    loads = []
    for i in range(6):
        first = (i % 3) * width + (i // 3) * part
        loads.append(
            pltpu.make_async_copy(
                w_in.at[:, first : first + part], w_ref.at[:, i * part : (i + 1) * part], sems.at[i]
            )
        )
    return loads


def forward_kernel(sizes):
    images, rows, width, experts, chips, part_rows, shares = sizes
    total = images * rows
    pairs = HEADS // 2
    pieces = len(shares)

    def body(meta, x_in, cot_in, *refs):
        ins, refs = refs[: 2 * pieces or 1], refs[2 * pieces or 1 :]
        par_ref, log_ref, slots_ref, xh_out, mixed_out, joint_out, probs_out, res_out, n2_out, *refs = refs
        if pieces:
            w_out, *refs = refs
        xh_ref, mixed_ref, joint_ref, probs_ref, res_ref, n2_ref, small, x_ref, cot_ref, n1_ref, *refs = refs
        given = [
            pltpu.make_async_copy(x_in, x_ref, refs[-1].at[8 + pairs + 2 * pieces]),
            pltpu.make_async_copy(cot_in, cot_ref, refs[-1].at[9 + pairs + 2 * pieces]),
        ]
        for load in given:
            load.start()
        if pieces:
            w_ref, own_ref, oth_ref, sems = refs
            loads, first = [], 0
            for i, share in enumerate(shares):
                loads.append(
                    [
                        pltpu.make_async_copy(
                            ins[side * pieces + i],
                            stage.at[first : first + share],
                            sems.at[8 + pairs + side * pieces + i],
                        )
                        for side, stage in enumerate((own_ref, oth_ref))
                    ]
                )
                first += share
            for load in sum(loads, []):
                load.start()
            first = 0
            for pair, share in zip(loads, shares):
                for load in pair:
                    load.wait()
                assemble(first, share, chips, part_rows, own_ref, oth_ref, w_ref)
                first += share
        else:
            (sems,) = refs
            w_ref = ins[0]
        stores = []

        def store(ref, out):
            stores.append(pltpu.make_async_copy(ref, out, sems.at[len(stores)]))
            stores[-1].start()

        if pieces:
            store(w_ref, w_out)
        par_ref[...] = w_ref[:, 4 * width : 4 * width + LANES].astype(f32).T[:8]
        gain_a, shift_a = par_ref[0:1], par_ref[1:2]
        gain_m, shift_m = par_ref[2:3], par_ref[3:4]
        for load in given:
            load.wait()

        @pl.loop(0, total // CHUNK, unroll=UNROLL)
        def _(i):
            at = rows_at(i, CHUNK)
            x = x_ref[at].astype(f32)
            x = x - jnp.mean(x, axis=-1, keepdims=True)
            rstd = lax.rsqrt(jnp.mean(x * x, axis=-1, keepdims=True) + EPSILON)
            x = x * rstd
            xh_ref[at] = x.astype(bf16)
            n1_ref[at] = (x * gain_a + shift_a).astype(bf16)

        store(xh_ref, xh_out)

        @pl.loop(0, 3)
        def _(i):
            at = rows_at(i, width)
            joint_ref[:, at] = nn(n1_ref[...], w_ref[:, at]).astype(bf16)

        store(joint_ref, joint_out)
        column = lax.broadcasted_iota(jnp.int32, (1, rows), 1)
        ones = jnp.ones((rows, LANES), bf16)
        lane = lax.broadcasted_iota(jnp.int32, (2 * rows, LANES), 1)
        first_lane = jnp.where(lane == 0, 1.0, 0.0).astype(bf16)
        row = lax.broadcasted_iota(jnp.int32, (rows, LANES), 0)
        bias = [jnp.where((row >= meta[i]) & (lane[:rows] == 0), NEGATIVE, 0.0).astype(bf16) for i in range(images)]
        for p in range(pairs):
            at_q, at_k, at_v = [slice(i * width + p * LANES, i * width + (p + 1) * LANES) for i in range(3)]
            for img in range(images):
                span = slice(img * rows, (img + 1) * rows)
                query, key, value = joint_ref[span, at_q], joint_ref[span, at_k], joint_ref[span, at_v]
                scores = nt(beside(stacked(query * 0.125), first_lane), beside(key, bias[img]))
                weight = jnp.exp(scores - jnp.max(scores, axis=-1, keepdims=True))
                sums = nn(weight.astype(bf16), beside(value, ones))
                share = 1.0 / sums[:, LANES:]
                probs_ref[p, img] = (weight * jnp.concatenate([share, share[:, : rows - LANES]], axis=1)).astype(bf16)
                mixed_ref[span, at_q] = unstacked(sums[:, :LANES] * share).astype(bf16)
            store(probs_ref.at[p], probs_out.at[p])
        store(mixed_ref, mixed_out)

        res_ref[...] = x_ref[...].astype(f32) + nn(mixed_ref[...], w_ref[:, 3 * width : 4 * width])
        store(res_ref, res_out)

        @pl.loop(0, total // CHUNK, unroll=UNROLL)
        def _(i):
            at = rows_at(i, CHUNK)
            x = res_ref[at]
            x = x - jnp.mean(x, axis=-1, keepdims=True)
            rstd = lax.rsqrt(jnp.mean(x * x, axis=-1, keepdims=True) + EPSILON)
            n2_ref[at] = (x * rstd * gain_m + shift_m).astype(bf16)

        store(n2_ref, n2_out)
        slot_w = par_ref[4 : 4 + experts].astype(bf16)
        for img in range(images):
            span = slice(img * rows, (img + 1) * rows)
            logits = nt(slot_w, n2_ref[span])
            log_ref[img] = logits
            live = column < meta[img]
            dispatch, combine = routing(logits, live)
            small[img * experts : (img + 1) * experts] = nn(dispatch.astype(bf16), n2_ref[span])
            combine = jnp.where(live, combine, 0.0).astype(bf16)
            small[(images + img) * experts : (images + img + 1) * experts] = nn(combine, cot_ref[span])
        slots_ref[...] = small[...].astype(bf16)
        for copy in stores:
            copy.wait()

    return body


def expert_kernel(images, experts, width, hidden, chips, pieces):
    lanes = -(-hidden // LANES) * LANES
    per = images * experts
    half = chips * per

    def body(_, *refs):
        own_refs, oth_refs, refs = refs[:pieces], refs[pieces : 2 * pieces], refs[2 * pieces :]
        in_ref, out_ref, mine_ref, other_ref, s_ref, g_ref, act_ref, gpre_ref, win, wout, so, gs = refs
        win[...] = jnp.zeros(win.shape, bf16)
        wout[...] = jnp.zeros(wout.shape, bf16)
        for e in range(experts):
            win[e * lanes : e * lanes + hidden, :] = in_ref[e]
            wout[e * lanes : e * lanes + hidden, :] = out_ref[e]

        for side, group in enumerate((own_refs, oth_refs)):
            for j, ref in enumerate(group):
                share = ref.shape[0] // 2

                @pl.loop(0, share)
                def _(i):
                    first, second = ref[2 * i].astype(f32), ref[2 * i + 1].astype(f32)
                    at = pl.ds(pl.multiple_of(side * half + (j * share + i) * 2 * per, 2 * per), 2 * per)
                    s_ref[at] = jnp.concatenate([first[:per], second[:per]], axis=0).astype(bf16)
                    g_ref[at] = jnp.concatenate([first[per:], second[per:]], axis=0).astype(bf16)

        block = 2 * half if 2 * half <= 256 else 256

        @pl.loop(0, 2 * half // block)
        def _(i):
            at = rows_at(i, block)
            so[at, : experts * lanes] = nt(s_ref[at], win[...])
            gs[at, : experts * lanes] = nt(g_ref[at], wout[...])

        @pl.loop(0, 2 * half // CHUNK, unroll=4)
        def _(i):
            at = rows_at(i, CHUNK)
            shape = (CHUNK, experts * lanes)
            keep = (lax.broadcasted_iota(jnp.int32, shape, 0) % experts) == (
                lax.broadcasted_iota(jnp.int32, shape, 1) // lanes
            )
            v = so[at, : experts * lanes]
            grad = gs[at, : experts * lanes]
            tanh = jnp.tanh(GELU_C * (v + GELU_A * v * v * v))
            act = 0.5 * v * (1.0 + tanh)
            slope = 0.5 * (1.0 + tanh) + 0.5 * v * (1.0 - tanh * tanh) * (
                GELU_C * (1.0 + 3.0 * GELU_A * v * v)
            )
            act_ref[at] = jnp.where(keep, act, 0.0).astype(bf16)
            gpre_ref[at] = jnp.where(keep, slope * grad, 0.0).astype(bf16)

        @pl.loop(0, 2 * half // block)
        def _(i):
            at = rows_at(i, block)
            so[at, :width] = nn(act_ref[at], wout[...])
            gs[at, :width] = nn(gpre_ref[at], win[...])

        for side, ref in enumerate((mine_ref, other_ref)):

            @pl.loop(0, chips)
            def _(f):
                at = pl.ds(pl.multiple_of(side * half + f * per, per), per)
                ref[f] = jnp.concatenate([so[at, :width], gs[at, :width]], axis=0).astype(bf16)

    return body


def expert_grad_kernel(experts, hidden):
    lanes = -(-hidden // LANES) * LANES

    def body(_, s_ref, g_ref, act_ref, gpre_ref, in_ref, out_ref):
        for e in range(experts):
            at = slice(e * lanes, (e + 1) * lanes)
            in_ref[e] = tn(gpre_ref[:, at], s_ref[...])[:hidden]
            out_ref[e] = tn(act_ref[:, at], g_ref[...])[:hidden]

    return body


def norm_pull(x, rstd, gain, grad):
    scaled = grad * gain
    first = jnp.mean(scaled, axis=-1, keepdims=True)
    second = jnp.mean(scaled * x, axis=-1, keepdims=True)
    return rstd * (scaled - first - x * second)


def attend_pull(meta, sizes, half, joint_ref, probs_ref, mixed_ref, gm_ref, gj):
    images, rows, width, *_ = sizes
    share = HEADS // 4
    ones = jnp.ones((rows, LANES), bf16)
    for q in range(share):
        at_q, at_k, at_v = [slice(i * width // 2 + q * LANES, i * width // 2 + (q + 1) * LANES) for i in range(3)]
        for img in range(images):
            span = slice(img * rows, (img + 1) * rows)
            query, key, value = joint_ref[span, at_q], joint_ref[span, at_k], joint_ref[span, at_v]
            p = half * share + q
            at = slice(p * LANES, (p + 1) * LANES)
            grad = stacked(gm_ref[span, at])
            dots = stacked(-(gm_ref[span, at].astype(f32) * mixed_ref[span, at].astype(f32)).astype(bf16))
            low = probs_ref[q, img]
            grad_scores = (low.astype(f32) * nt(beside(grad, dots), beside(value, ones))).astype(bf16)
            gj[span, at_q] = (unstacked(nn(grad_scores, key)) * 0.125).astype(bf16)
            gj[span, at_k] = (tn(grad_scores, stacked(query)) * 0.125).astype(bf16)
            gj[span, at_v] = tn(low, grad).astype(bf16)


def sums_lanes(width, part_rows):
    return slice(8, 8 + 3 * width // part_rows)


def small_lanes(width, part_rows):
    return -(-sums_lanes(width, part_rows).stop // LANES) * LANES


def half_loads(width, half, joint_in, joint_ref, probs_in, probs_ref, sems):
    part, share = width // 2, HEADS // 4
    loads = [
        pltpu.make_async_copy(
            joint_in.at[:, i * width + half * part : i * width + (half + 1) * part],
            joint_ref.at[:, i * part : (i + 1) * part],
            sems.at[i],
        )
        for i in range(3)
    ]
    loads.append(pltpu.make_async_copy(probs_in.at[half * share : (half + 1) * share], probs_ref, sems.at[3]))
    return loads


def second_norm_kernel(sizes):
    images, rows, width, *_ = sizes

    def body(meta, res_in, n2_in, xn_ref, dev_ref, n2_ref, res_ref, sems):
        loads = [pltpu.make_async_copy(res_in, res_ref, sems.at[0]), pltpu.make_async_copy(n2_in, n2_ref, sems.at[1])]
        for load in loads:
            load.start()
        loads[0].wait()

        @pl.loop(0, images * rows // CHUNK, unroll=UNROLL)
        def _(i):
            at = rows_at(i, CHUNK)
            x = res_ref[at]
            x = x - jnp.mean(x, axis=-1, keepdims=True)
            rstd = lax.rsqrt(jnp.mean(x * x, axis=-1, keepdims=True) + EPSILON)
            xn_ref[at] = x * rstd
            dev_ref[at] = jnp.broadcast_to(rstd, (CHUNK, LANES))

        loads[1].wait()

    return body


def slots_pull_kernel(sizes):
    images, rows, width, experts, chips, part_rows, shares = sizes
    pieces = len(shares)
    total = images * rows
    share = HEADS // 4

    def body(meta, cot_ref, par_ref, log_ref, sum_ref, r1_ref, r2_ref, r3_ref, xn_ref, dev_ref, n2_ref, w_in, xh_in,
             joint_in, probs_in, mixed_in, res_in, block_ref, xgrad_ref, gm, gj, grads, sums_ref, xh_ref,
             mixed_ref, joint_late, probs_late, *refs):
        outs, (gn, gb, tile, small, w_ref, joint_ref, probs_ref, res_ref, sems) = refs[:-9], refs[-9:]
        early = [pltpu.make_async_copy(res_in, res_ref, sems.at[0])]
        late = [
            pltpu.make_async_copy(mixed_in, mixed_ref, sems.at[1]),
            pltpu.make_async_copy(w_in.at[:, 3 * width : 4 * width], w_ref, sems.at[2]),
        ]
        loads = half_loads(width, 0, joint_in, joint_ref, probs_in, probs_ref, sems.at[3:7])
        last = [pltpu.make_async_copy(xh_in, xh_ref, sems.at[7])]
        ahead = half_loads(width, 1, joint_in, joint_late, probs_in, probs_late, sems.at[8:12])
        for load in early + late + loads + last + ahead:
            load.start()

        def put(first, count):
            if pieces:
                cut(meta, images, chips, part_rows, tile, count, *outs, first)
            else:
                outs[0][:, first : first + count] = tile[:, :count]

        sums = sum_ref[0].astype(f32) + r1_ref[0].astype(f32) + r2_ref[0].astype(f32) + r3_ref[0].astype(f32)
        small[...] = sums.astype(bf16).astype(f32)
        slot_w = par_ref[4 : 4 + experts]
        column = lax.broadcasted_iota(jnp.int32, (1, rows), 1)
        slot_grad = jnp.zeros((experts, width), f32)
        for img in range(images):
            span = slice(img * rows, (img + 1) * rows)
            live = column < meta[img]
            dispatch, combine = routing(log_ref[img], live)
            out32 = small[img * experts : (img + 1) * experts]
            grad32 = small[(images + img) * experts : (images + img + 1) * experts]
            slot_out = out32.astype(bf16)
            grad_comb = jnp.where(live, nt(slot_out, cot_ref[span]), 0.0)
            grad_disp = nt(grad32.astype(bf16), n2_ref[span])
            grad_log = combine * (grad_comb - jnp.sum(combine * grad_comb, axis=0, keepdims=True))
            grad_log = grad_log + dispatch * (
                grad_disp - jnp.sum(dispatch * grad_disp, axis=1, keepdims=True)
            )
            slot_grad = slot_grad + nn(grad_log.astype(bf16), n2_ref[span])
            left = jnp.concatenate([dispatch, grad_log], axis=0).astype(bf16)
            right = jnp.concatenate([grad32, slot_w], axis=0).astype(bf16)
            gn[span] = tn(left, right)
            live_row = lax.broadcasted_iota(jnp.int32, (rows, 1), 0) < meta[img]
            expert_sum = tn(combine.astype(bf16), slot_out)
            for load in early if img == 0 else []:
                load.wait()
            block_ref[span] = jnp.where(live_row, res_ref[span] + expert_sum, 0.0).astype(bf16)
        grads[0:2] = jnp.zeros((2, width), f32)
        grads[4 : 4 + experts] = slot_grad

        gain_m = par_ref[2:3]
        zero = jnp.zeros((8, width), f32)
        for img in range(images):

            def step(i, carry):
                at = pl.ds(pl.multiple_of(img * rows + i * CHUNK, CHUNK), CHUNK)
                grad = gn[at]
                x = xn_ref[at]
                pulled = norm_pull(x, dev_ref[at, 0:1], gain_m, grad)
                row = i * CHUNK + lax.broadcasted_iota(jnp.int32, (CHUNK, 1), 0)
                pulled = pulled + jnp.where(row < meta[img], cot_ref[at].astype(f32), 0.0)
                xgrad_ref[at] = pulled
                gb[at] = pulled.astype(bf16)
                return carry[0] + fold_rows(grad * x), carry[1] + fold_rows(grad)

            sums = lax.fori_loop(0, rows // CHUNK, step, (zero, zero) if img == 0 else sums, unroll=UNROLL)
        grads[2:3] = jnp.sum(sums[0], axis=0, keepdims=True)
        grads[3:4] = jnp.sum(sums[1], axis=0, keepdims=True)

        for load in late:
            load.wait()
        tile[:, :width] = tn(mixed_ref[...], gb[...])
        put(0, width)
        gm[...] = nt(gb[...], w_ref[...]).astype(bf16)
        for load in loads:
            load.wait()
        attend_pull(meta, sizes, 0, joint_ref, probs_ref, mixed_ref, gm, gj)
        for load in last:
            load.wait()
        tile[...] = tn(xh_ref[...], gj[...])
        sums_ref[0:1] = column_sums(gj)
        put(width, 3 * width // 2)
        for load in ahead:
            load.wait()

    return body


def heads_pull_kernel(sizes):
    width = sizes[2]

    def body(meta, gm_ref, joint_ref, probs_ref, mixed_ref, gj):
        attend_pull(meta, sizes, 1, joint_ref, probs_ref, mixed_ref, gm_ref, gj)

    return body


def heads_grad_kernel(sizes):
    images, rows, width, experts, chips, part_rows, shares = sizes
    half = 3 * width // 2

    def body(meta, gj, grads, sums_ref, xh_ref, w_in, w_ref, *refs):
        outs, (tile, small, sems) = refs[:-3], refs[-3:]
        loads = weight_loads(width, w_in, w_ref, sems)
        for load in loads:
            load.start()
        sums = [sums_ref[0:1], column_sums(gj)]
        wide = sums_lanes(width, part_rows)
        small[:, :LANES] = jnp.concatenate([grads[...], jnp.zeros((LANES - 8, width), f32)], axis=0).T
        each = 3 * width // part_rows
        for r in range(part_rows):
            row = [s[:, c0 - i * half : c1 - i * half] for i, s in enumerate(sums)
                   for c0, c1 in [(max(r * each, i * half), min((r + 1) * each, (i + 1) * half))] if c0 < c1]
            small[r : r + 1, wide] = jnp.concatenate(row, axis=1)
        for t in range(1, width // part_rows):
            small[t * part_rows : (t + 1) * part_rows, wide] = small[:part_rows, wide]
        tile[...] = tn(xh_ref[...], gj[...])

        def put(ref, count, first):
            if shares:
                cut(meta, images, chips, part_rows, ref, count, *outs, first)
            else:
                outs[0][:, first : first + count] = ref[:, :count]

        put(tile, half, 0)
        put(small, small.shape[1], half)
        for load in loads:
            load.wait()

    return body


def inputs_pull_kernel(sizes):
    images, rows, width, experts, chips, part_rows, shares = sizes
    total = images * rows
    half = 3 * width // 2

    def body(meta, x_ref, par_ref, gj0_ref, gj1_ref, w_ref, part_ref, xgrad_ref, gn):
        gn[...] = nt(gj0_ref[...], w_ref[:, :half]) + nt(gj1_ref[...], w_ref[:, half:])
        gain_a = par_ref[0:1]

        @pl.loop(0, total // CHUNK, unroll=UNROLL)
        def _(i):
            at = rows_at(i, CHUNK)
            x = x_ref[at].astype(f32)
            x = x - jnp.mean(x, axis=-1, keepdims=True)
            rstd = lax.rsqrt(jnp.mean(x * x, axis=-1, keepdims=True) + EPSILON)
            xgrad_ref[at] = part_ref[at] + norm_pull(x * rstd, rstd, gain_a, gn[at])

    return body


def split_sum(parts, first_type=f32):
    def run(*args):
        count, rest = args[0].shape[0], args[0].shape[1:]
        share = count // parts

        def body(*refs):
            ins, outs = refs[: len(args)], refs[len(args) :]
            for part in range(parts):

                @pl.loop(0, share)
                def _(i):
                    total = ins[0][part * share + i].astype(f32)
                    for ref in ins[1:]:
                        total = total + ref[part * share + i].astype(f32)
                    outs[part][i] = total.astype(outs[part].dtype)

        types = [first_type] + [bf16] * (parts - 1)
        return pl.pallas_call(
            body,
            out_shape=[jax.ShapeDtypeStruct((share,) + rest, t) for t in types],
            in_specs=[vmem()] * len(args),
            out_specs=[vmem()] * parts,
            compiler_params=pltpu.CompilerParams(vmem_limit_bytes=32 * MIB),
        )(*args)

    return run


def add_kernel(groups, types, share=2):
    def run(*args):
        rest = args[0].shape[1:]
        sizes = [share * len(g) for g in groups]

        def body(*refs):
            ins, outs = refs[: len(args)], refs[len(args) :]
            for out, group in zip(outs, groups):
                for j, terms in enumerate(group):
                    for i in range(share):
                        total = ins[terms[0][0]][terms[0][1] + i].astype(f32)
                        for a, first in terms[1:]:
                            total = total + ins[a][first + i].astype(f32)
                        out[j * share + i] = total.astype(out.dtype)

        return pl.pallas_call(
            body,
            out_shape=[jax.ShapeDtypeStruct((c,) + rest, t) for c, t in zip(sizes, types)],
            in_specs=[vmem()] * len(args),
            out_specs=[vmem()] * len(groups),
            compiler_params=pltpu.CompilerParams(vmem_limit_bytes=16 * MIB),
        )(*args)

    return run


def finish_kernel(width, experts, part_rows):
    half = width // 2
    wide = sums_lanes(width, part_rows)

    def body(a0, a1, b0, b1, w_ref, gain_ref, shift_ref, out_ref, in_ref, ns_ref, nb_ref, ms_ref, mb_ref, slot_ref,
             square, sums):
        first = a0[0] + a1[0].astype(f32)
        second = b0[0] + b1[0].astype(f32)
        out_ref[...] = first[:, :width]
        small = second[:, 3 * half :]
        each = 3 * width // part_rows
        for r in range(part_rows):
            sums[0:1, r * each : (r + 1) * each] = small[r : r + 1, wide]
        square[...] = jnp.zeros_like(square)
        square[0:1, :part_rows] = gain_ref[...].astype(f32)
        square[1:2, :part_rows] = shift_ref[...].astype(f32)
        turned = square[...].T
        gain, shift = turned[:part_rows, 0:1], turned[:part_rows, 1:2]
        by_gain = jnp.zeros((part_rows, half), f32)
        by_shift = jnp.zeros((part_rows, half), f32)
        for i in range(3):
            for j, value in enumerate((first[:, width + i * half : width + (i + 1) * half], second[:, i * half : (i + 1) * half])):
                at = slice(i * width + j * half, i * width + (j + 1) * half)
                total = sums[0:1, (j * 3 + i) * half : (j * 3 + i + 1) * half]
                weight = w_ref[:, at].astype(f32)
                in_ref[:, at] = value * gain + shift * total
                by_gain = by_gain + value * weight
                by_shift = by_shift + total * weight
        lane = lax.broadcasted_iota(jnp.int32, (1, LANES), 1)
        small = jnp.where(lane == 0, jnp.sum(by_gain, axis=1, keepdims=True), small[:, :LANES])
        small = jnp.where(lane == 1, jnp.sum(by_shift, axis=1, keepdims=True), small)
        square[:part_rows] = small
        turned = square[...].T
        for i, ref in enumerate((ns_ref, nb_ref, ms_ref, mb_ref)):
            ref[...] = turned[i : i + 1, :part_rows]
        slot_ref[...] = turned[4 : 4 + experts, :part_rows]

    return body


def stages_of(devices):
    chips = devices // 2
    groups, bit = [], 1
    while bit < chips:
        count = min(4, chips // bit)
        groups.append([bit * i for i in range(count)])
        bit *= count
    return groups


def swap(value, devices, chip_offset, core_offset):
    mask = 2 * chip_offset + core_offset
    return lax.ppermute(value, "fsdp", [(i, i ^ mask) for i in range(devices)])


def gather_slots(block, devices):
    *lower, last = stages_of(devices)[::-1]
    for group in lower:
        parts = [block] + [swap(block, devices, o, 0) for o in group[1:]]
        block = jnp.concatenate(parts, axis=0)
    own = [block] + [swap(block, devices, o, 0) for o in last[1:]]
    return own, [swap(part, devices, 0, 1) for part in own]


def scatter_chips(mine, other, devices):
    terms = [mine, swap(other, devices, 0, 1)]
    for group in stages_of(devices):
        parts = split_sum(len(group))(*terms)
        terms = [parts[0]] + [swap(p, devices, o, 0) for p, o in zip(parts[1:], group[1:])]
    return terms


SHARES = (2,) * 8


def gather_pieces(block, devices):
    block = block[None]
    far = swap(block, devices, 8, 0)
    z0 = jnp.concatenate([block, swap(block, devices, 4, 0)], axis=0)
    x0, y0 = swap(z0, devices, 1, 0), swap(z0, devices, 2, 0)
    z1 = jnp.concatenate([far, swap(far, devices, 4, 0)], axis=0)
    x1, y1 = swap(z1, devices, 1, 0), swap(z1, devices, 2, 0)
    d0, d1 = swap(y0, devices, 1, 0), swap(x1, devices, 2, 0)
    own = [z0, z1, x0, x1, y0, y1, d0, d1]
    return own + [swap(piece, devices, 0, 1) for piece in own]


def after(values, events):
    return lax.optimization_barrier((*values, *events))[: len(values)]


def scatter_begin(mine, other, devices, events=()):
    got = swap(other, devices, 0, 1)
    if events:
        (got,) = after([got], events)
    z0, z1, x0, x1, y0, y1, d0, d1 = [[(0, i), (1, i)] for i in range(0, 16, 2)]
    return add_kernel(
        [[z0], [z1], [d0, x0], [d1, y1], [x1], [y0]], [f32, f32, bf16, bf16, bf16, bf16]
    )(mine, got)


def scatter_middle(parts, devices, events=()):
    z0, z1, to_x, to_y, x1, y0 = parts
    from_x, from_y = swap(to_x, devices, 1, 0), swap(to_y, devices, 2, 0)
    if events:
        x1, y0 = after([x1, y0], events)
    x1, y0 = add_kernel([[[(0, 0), (2, 0)]], [[(1, 0), (3, 0)]]], [bf16, bf16])(x1, y0, from_y, from_x)
    return z0, z1, x1, y0, from_x, from_y


def scatter_near(parts, devices):
    z0, z1, x1, y0, from_x, from_y = parts
    from_x1, from_y0 = swap(x1, devices, 1, 0), swap(y0, devices, 2, 0)
    (z1,) = add_kernel([[[(0, 0), (1, 0), (2, 2)]]], [bf16])(z1, from_x1, from_y)
    return z0, from_x, from_y0, swap(z1, devices, 4, 0), z1


def scatter_end(parts, devices):
    z0, from_x, from_y0, from_z1, _ = parts
    keep, send = add_kernel(
        [[[(0, i), (1, 2 + i), (2, i), (3, i)]] for i in range(2)], [f32, bf16], 1
    )(z0, from_x, from_y0, from_z1)
    return keep, swap(send, devices, 8, 0)


def build(devices):
    def shards(images, lengths, norm_scale, norm_shift, attend_in, attend_out, mixer_scale, mixer_shift,
               slot_params, expert_in, expert_out, cotangent):
        count, rows, width = images.shape
        experts, _, hidden = expert_in.shape
        part_rows = attend_in.shape[0]
        chips = devices // 2
        total = count * rows
        pairs = HEADS // 2
        half = width // 2
        wide = 4 * width + LANES
        shares = SHARES if part_rows % 8 == 0 and chips == 16 else ()
        sizes = (count, rows, width, experts, chips, part_rows, shares)
        meta = lengths
        x = images.reshape(total, width)
        cot = cotangent.reshape(total, width)
        vectors = [v.reshape(1, part_rows) for v in (norm_scale, norm_shift, mixer_scale, mixer_shift)]
        given = [attend_in, attend_out, *vectors, slot_params.T]
        pack = pl.pallas_call(
            pack_kernel(width, experts),
            out_shape=jax.ShapeDtypeStruct((part_rows, wide), bf16),
            in_specs=[hbm()] * 7,
            out_specs=vmem(),
            scratch_shapes=[pltpu.VMEM((LANES, LANES), f32)]
            + [pltpu.VMEM(a.shape, bf16) for a in given]
            + [pltpu.SemaphoreType.DMA((7,))],
            compiler_params=pltpu.CompilerParams(vmem_limit_bytes=8 * MIB),
        )(*[pltpu.with_memory_space_constraint(a, pltpu.HBM) for a in given])
        if shares:
            weights = gather_pieces(pack, devices)
        else:
            weights = [lax.all_gather(pack, "fsdp", axis=0, tiled=True)]
        kept = [
            ((total, width), bf16),
            ((total, width), bf16),
            ((total, 3 * width), bf16),
            ((pairs, count, 2 * rows, rows), bf16),
            ((total, width), f32),
            ((total, width), bf16),
        ]
        outs = [
            ((8, width), f32),
            ((count, experts, rows), f32),
            ((2 * count * experts, width), bf16),
        ] + kept
        scratch = kept + [((2 * count * experts, width), f32)] + [((total, width), bf16)] * 3
        if shares:
            outs.append(((width, wide), bf16))
            scratch += [outs[-1]] + [((chips, part_rows, wide), bf16)] * 2
        par, logs, slots, xh, mixed, joint, probs, res, n2, *more = call(
            forward_kernel(sizes),
            outs,
            scratch,
            40,
            far_in=range(2),
            any_in=range(2, 2 + 2 * len(shares)),
            far_out=range(3, len(outs)),
            sems=10 + pairs + 2 * len(shares),
        )(meta, x, cot, *weights)
        w = more[0] if shares else weights[0]

        own, oth = gather_slots(slots[None], devices)
        lanes = -(-hidden // LANES) * LANES
        held = devices * count * experts
        most = max(width, experts * lanes)
        mine, other, s_all, g_all, act, gpre = call(
            expert_kernel(count, experts, width, hidden, chips, len(own)),
            [
                ((chips, 2 * count * experts, width), bf16),
                ((chips, 2 * count * experts, width), bf16),
                ((held, width), bf16),
                ((held, width), bf16),
                ((held, experts * lanes), bf16),
                ((held, experts * lanes), bf16),
            ],
            [
                ((experts * lanes, width), bf16),
                ((experts * lanes, width), bf16),
                ((held, most), f32),
                ((held, most), f32),
            ],
            24 if held <= 256 else 56,
        )(meta, *own, *oth, jnp.swapaxes(expert_in, 1, 2), expert_out)
        expin_grad, expout_grad = call(
            expert_grad_kernel(experts, hidden),
            [((experts, hidden, width), f32), ((experts, hidden, width), f32)],
            [],
            24 if held <= 256 else 56,
            flops=2 * 10**9,
        )(meta, s_all, g_all, act, gpre)
        terms = scatter_chips(mine, other, devices)
        if len(terms) < 4:
            terms = terms + [jnp.zeros_like(terms[-1])] * (4 - len(terms))
        terms[0], expin_grad, expout_grad = lax.optimization_barrier((terms[0], expin_grad, expout_grad))

        def blocks(columns):
            if shares:
                return [((chips, part_rows, columns), bf16)] * 2
            return [((width, columns), f32)]

        halves = [((total, 3 * half), bf16), ((pairs // 2, count, 2 * rows, rows), bf16)]
        xn, dev, n2 = call(
            second_norm_kernel(sizes),
            [((total, width), f32), ((total, LANES), f32), ((total, width), bf16)],
            [((total, width), f32)],
            16,
            flops=10**9,
            far_in=range(2),
            sems=2,
        )(meta, res, n2)
        block, part, gm, gj, early, sums, xh, mixed, joint1, probs1, *first = call(
            slots_pull_kernel(sizes),
            [
                ((total, width), bf16),
                ((total, width), f32),
                ((total, width), bf16),
                ((total, 3 * half), bf16),
                ((8, width), f32),
                ((8, 3 * half), f32),
                ((total, width), bf16),
                ((total, width), bf16),
            ]
            + halves
            + blocks(width + 3 * half),
            [
                ((total, width), f32),
                ((total, width), bf16),
                ((width, 3 * half), f32),
                ((2 * count * experts, width), f32),
                ((width, width), bf16),
            ]
            + halves
            + [((total, width), f32)],
            VMEM_MIB,
            far_in=range(10, 16),
            sems=12,
        )(meta, cot, par, logs, *terms, xn, dev, n2, w, xh, joint, probs, mixed, res)
        gj1 = call(
            heads_pull_kernel(sizes), [((total, 3 * half), bf16)], [], VMEM_MIB, flops=3 * 10**9
        )(meta, gm, joint1, probs1, mixed)[0]
        gj_late = gj1
        if shares:
            first = scatter_begin(*first, devices)
            gj_late = after([gj1], first)[0]
        tiny = small_lanes(width, part_rows)
        w_all, *second = call(
            heads_grad_kernel(sizes),
            [((width, 3 * width), bf16)] + blocks(3 * half + tiny),
            [((width, 3 * half), f32), ((width, tiny), f32)],
            VMEM_MIB,
            flops=4 * 10**9,
            far_in=range(4, 5),
            sems=6,
        )(meta, gj_late, early, sums, xh, w)
        if shares:
            second = scatter_begin(*second, devices)
            part = after([part], second)[0]
        xgrad = call(
            inputs_pull_kernel(sizes),
            [((total, width), f32)],
            [((total, width), f32)],
            VMEM_MIB,
            flops=5 * 10**9,
        )(meta, x, par, gj, gj1, w_all, part)[0]
        if shares:
            first = scatter_middle(first, devices, [xgrad])
            second = scatter_middle(second, devices, first[2:4])
            first, second = scatter_near(first, devices), scatter_near(second, devices)
            ends = [*scatter_end(first, devices), *scatter_end(second, devices)]
        else:
            ends = []
            for full in (first[0], second[0]):
                full = lax.psum_scatter(full, "fsdp", scatter_dimension=0, tiled=True)[None]
                ends += [full, jnp.zeros_like(full)]
        out_grad, in_grad, ns, nb, ms, mb, slot_grad = pl.pallas_call(
            finish_kernel(width, experts, part_rows),
            out_shape=[jax.ShapeDtypeStruct((part_rows, c), f32) for c in (width, 3 * width)]
            + [jax.ShapeDtypeStruct((1, part_rows), f32)] * 4
            + [jax.ShapeDtypeStruct((experts, part_rows), f32)],
            in_specs=[vmem()] * 7,
            out_specs=[vmem()] * 7,
            scratch_shapes=[pltpu.VMEM((LANES, LANES), f32), pltpu.VMEM((8, 3 * width), f32)],
            compiler_params=pltpu.CompilerParams(vmem_limit_bytes=8 * MIB),
        )(*ends, attend_in, *vectors[:2])
        return (
            block.reshape(images.shape),
            xgrad.reshape(images.shape),
            ns.reshape(part_rows),
            nb.reshape(part_rows),
            in_grad,
            out_grad,
            ms.reshape(part_rows),
            mb.reshape(part_rows),
            slot_grad.T,
            jnp.swapaxes(expin_grad, 1, 2),
            expout_grad,
        )

    return shards


def solution(mesh):
    rows = P("fsdp", None, None)
    cols = P(None, None, "fsdp")
    mids = P(None, "fsdp", None)
    flat = P("fsdp", None)
    vec = P("fsdp")
    return jax.shard_map(
        build(mesh.shape["fsdp"]),
        mesh=mesh,
        in_specs=(rows, vec, vec, vec, flat, flat, vec, vec, flat, cols, mids, rows),
        out_specs=(rows, rows, vec, vec, flat, flat, vec, vec, flat, cols, mids),
        check_vma=False,
    )
```

```python
import jax
import jax.numpy as jnp
from jax import lax
from jax.experimental import pallas as pl
from jax.experimental.pallas import tpu as pltpu
from jax.sharding import PartitionSpec as P

HEADS = 12
NEGATIVE = -1e30
EPSILON = 1e-06
GELU_C = 0.7978845608
GELU_A = 0.044715
LANES = 128
CHUNK = 16
UNROLL = 13
VMEM_MIB = 28
MIB = 1 << 20

bf16 = jnp.bfloat16
f32 = jnp.float32


def dot(a, b, ca, cb):
    return lax.dot_general(a, b, (((ca,), (cb,)), ((), ())), preferred_element_type=f32)


def nn(a, b):
    return dot(a, b, 1, 0)


def nt(a, b):
    return dot(a, b, 1, 1)


def tn(a, b):
    return dot(a, b, 0, 0)


def vmem():
    return pl.BlockSpec(memory_space=pltpu.VMEM)


def anywhere():
    return pl.BlockSpec(memory_space=pl.ANY)


def hbm():
    return pl.BlockSpec(memory_space=pltpu.HBM)


def smem():
    return pl.BlockSpec(memory_space=pltpu.SMEM)


def call(body, outs, scratch, limit_mib, flops=0, far_in=(), any_in=(), far_out=(), sems=0):
    def run(scalars, *args):
        return pl.pallas_call(
            body,
            out_shape=[
                pltpu.HBM(s, d) if i in far_out else jax.ShapeDtypeStruct(s, d)
                for i, (s, d) in enumerate(outs)
            ],
            in_specs=[smem()]
            + [hbm() if i in far_in else anywhere() if i in any_in else vmem() for i in range(len(args))],
            out_specs=[hbm() if i in far_out else vmem() for i in range(len(outs))],
            scratch_shapes=[pltpu.VMEM(s, d) for s, d in scratch]
            + ([pltpu.SemaphoreType.DMA((sems,))] if sems else []),
            compiler_params=pltpu.CompilerParams(vmem_limit_bytes=limit_mib * MIB),
            cost_estimate=pl.CostEstimate(flops=flops, bytes_accessed=0, transcendentals=0),
        )(
            scalars,
            *[pltpu.with_memory_space_constraint(a, pltpu.HBM) if i in far_in else a for i, a in enumerate(args)],
        )

    return run


def rows_at(step, count):
    return pl.ds(pl.multiple_of(step * count, count), count)


def fold_rows(value):
    return value[:8] + value[8:]


def head_masks():
    lane = lax.broadcasted_iota(jnp.int32, (1, LANES), 1)
    return lane < LANES // 2


def stacked(pair):
    first = head_masks()
    zero = jnp.zeros_like(pair)
    return jnp.concatenate([jnp.where(first, pair, zero), jnp.where(first, zero, pair)], axis=0)


def beside(left, right):
    return jnp.concatenate([left, right], axis=1)


def unstacked(both):
    rows = both.shape[0] // 2
    return jnp.where(head_masks(), both[:rows], both[rows:])


def routing(logits, live):
    masked = jnp.where(live, logits, NEGATIVE)
    weight = jnp.exp(masked - jnp.max(masked, axis=1, keepdims=True))
    dispatch = weight / jnp.sum(weight, axis=1, keepdims=True)
    share = jnp.exp(logits - jnp.max(logits, axis=0, keepdims=True))
    combine = share / jnp.sum(share, axis=0, keepdims=True)
    return dispatch, combine


def pack_kernel(width, experts):
    def body(*refs):
        given, pack_ref, square, here, sems = refs[:7], refs[7], refs[8], refs[9:16], refs[16]
        loads = [pltpu.make_async_copy(a, b, sems.at[i]) for i, (a, b) in enumerate(zip(given, here))]
        for load in loads:
            load.start()
        for load in loads:
            load.wait()
        in_ref, out_ref, ns_ref, nb_ref, ms_ref, mb_ref, slot_ref = here
        pack_ref[:, : 3 * width] = in_ref[...]
        pack_ref[:, 3 * width : 4 * width] = out_ref[...]
        rows = in_ref.shape[0]
        square[...] = jnp.zeros_like(square)
        for i, ref in enumerate((ns_ref, nb_ref, ms_ref, mb_ref)):
            square[i : i + 1, :rows] = ref[...].astype(f32)
        square[4 : 4 + experts, :rows] = slot_ref[...].astype(f32)
        pack_ref[:, 4 * width :] = square[...].T[:rows].astype(bf16)

    return body


def gathered_chip(f, chips):
    return (lax.axis_index("fsdp") // 2) ^ (f // 4 + (f % 4) * (chips // 4))


def scattered_chip(f, chips):
    k = f % 4
    return (lax.axis_index("fsdp") // 2) ^ (f // 4 + (k % 2) * (chips // 2) + (k // 2) * (chips // 4))


def assemble(first, share, chips, part_rows, own_ref, oth_ref, w_ref):
    columns = w_ref.shape[1]
    for own_first in (True, False):

        @pl.when(lax.axis_index("fsdp") % 2 == (0 if own_first else 1))
        def _():
            low_ref, high_ref = (own_ref, oth_ref) if own_first else (oth_ref, own_ref)
            for f in range(first, first + share):
                at = rows_at(gathered_chip(f, chips), 2 * part_rows)
                for c0 in range(0, columns, 640):
                    c1 = min(columns, c0 + 640)
                    both = [low_ref[f, :, c0:c1].astype(f32), high_ref[f, :, c0:c1].astype(f32)]
                    w_ref[at, c0:c1] = jnp.concatenate(both, axis=0).astype(bf16)


def cut(meta, images, chips, part_rows, tile, count, mine_ref, other_ref, first):
    for own_first in (True, False):

        @pl.when(lax.axis_index("fsdp") % 2 == (0 if own_first else 1))
        def _():
            @pl.loop(0, chips, unroll=4)
            def _(f):
                at = rows_at(scattered_chip(f, chips), 2 * part_rows)
                for c0 in range(0, count, 384):
                    c1 = min(count, c0 + 384)
                    both = tile[at, c0:c1]
                    low, high = both[:part_rows].astype(bf16), both[part_rows:].astype(bf16)
                    mine_ref[f, :, first + c0 : first + c1] = low if own_first else high
                    other_ref[f, :, first + c0 : first + c1] = high if own_first else low


def column_sums(ref):
    total = jnp.zeros((CHUNK, ref.shape[1]), f32)
    for i in range(ref.shape[0] // CHUNK):
        total = total + ref[i * CHUNK : (i + 1) * CHUNK].astype(f32)
    return jnp.sum(total, axis=0, keepdims=True)


def weight_loads(width, w_in, w_ref, sems):
    part = width // 2
    loads = []
    for i in range(6):
        first = (i % 3) * width + (i // 3) * part
        loads.append(
            pltpu.make_async_copy(
                w_in.at[:, first : first + part], w_ref.at[:, i * part : (i + 1) * part], sems.at[i]
            )
        )
    return loads


def forward_kernel(sizes):
    images, rows, width, experts, chips, part_rows, shares = sizes
    total = images * rows
    pairs = HEADS // 2
    pieces = len(shares)

    def body(meta, x_in, cot_in, *refs):
        ins, refs = refs[: 2 * pieces or 1], refs[2 * pieces or 1 :]
        par_ref, log_ref, slots_ref, xh_out, mixed_out, joint_out, probs_out, res_out, n2_out, *refs = refs
        if pieces:
            w_out, *refs = refs
        xh_ref, mixed_ref, joint_ref, probs_ref, res_ref, n2_ref, small, x_ref, cot_ref, n1_ref, *refs = refs
        given = [
            pltpu.make_async_copy(x_in, x_ref, refs[-1].at[8 + pairs + 2 * pieces]),
            pltpu.make_async_copy(cot_in, cot_ref, refs[-1].at[9 + pairs + 2 * pieces]),
        ]
        for load in given:
            load.start()
        if pieces:
            w_ref, own_ref, oth_ref, sems = refs
            loads, first = [], 0
            for i, share in enumerate(shares):
                loads.append(
                    [
                        pltpu.make_async_copy(
                            ins[side * pieces + i],
                            stage.at[first : first + share],
                            sems.at[8 + pairs + side * pieces + i],
                        )
                        for side, stage in enumerate((own_ref, oth_ref))
                    ]
                )
                first += share
            for load in sum(loads, []):
                load.start()
            first = 0
            for pair, share in zip(loads, shares):
                for load in pair:
                    load.wait()
                assemble(first, share, chips, part_rows, own_ref, oth_ref, w_ref)
                first += share
        else:
            (sems,) = refs
            w_ref = ins[0]
        stores = []

        def store(ref, out):
            stores.append(pltpu.make_async_copy(ref, out, sems.at[len(stores)]))
            stores[-1].start()

        if pieces:
            store(w_ref, w_out)
        par_ref[...] = w_ref[:, 4 * width : 4 * width + LANES].astype(f32).T[:8]
        gain_a, shift_a = par_ref[0:1], par_ref[1:2]
        gain_m, shift_m = par_ref[2:3], par_ref[3:4]
        for load in given:
            load.wait()

        @pl.loop(0, total // CHUNK, unroll=UNROLL)
        def _(i):
            at = rows_at(i, CHUNK)
            x = x_ref[at].astype(f32)
            x = x - jnp.mean(x, axis=-1, keepdims=True)
            rstd = lax.rsqrt(jnp.mean(x * x, axis=-1, keepdims=True) + EPSILON)
            x = x * rstd
            xh_ref[at] = x.astype(bf16)
            n1_ref[at] = (x * gain_a + shift_a).astype(bf16)

        store(xh_ref, xh_out)

        @pl.loop(0, 3)
        def _(i):
            at = rows_at(i, width)
            joint_ref[:, at] = nn(n1_ref[...], w_ref[:, at]).astype(bf16)

        store(joint_ref, joint_out)
        column = lax.broadcasted_iota(jnp.int32, (1, rows), 1)
        ones = jnp.ones((rows, LANES), bf16)
        lane = lax.broadcasted_iota(jnp.int32, (2 * rows, LANES), 1)
        first_lane = jnp.where(lane == 0, 1.0, 0.0).astype(bf16)
        row = lax.broadcasted_iota(jnp.int32, (rows, LANES), 0)
        bias = [jnp.where((row >= meta[i]) & (lane[:rows] == 0), NEGATIVE, 0.0).astype(bf16) for i in range(images)]
        for p in range(pairs):
            at_q, at_k, at_v = [slice(i * width + p * LANES, i * width + (p + 1) * LANES) for i in range(3)]
            for img in range(images):
                span = slice(img * rows, (img + 1) * rows)
                query, key, value = joint_ref[span, at_q], joint_ref[span, at_k], joint_ref[span, at_v]
                scores = nt(beside(stacked(query * 0.125), first_lane), beside(key, bias[img]))
                weight = jnp.exp(scores - jnp.max(scores, axis=-1, keepdims=True))
                sums = nn(weight.astype(bf16), beside(value, ones))
                share = 1.0 / sums[:, LANES:]
                probs_ref[p, img] = (weight * jnp.concatenate([share, share[:, : rows - LANES]], axis=1)).astype(bf16)
                mixed_ref[span, at_q] = unstacked(sums[:, :LANES] * share).astype(bf16)
            store(probs_ref.at[p], probs_out.at[p])
        store(mixed_ref, mixed_out)

        res_ref[...] = x_ref[...].astype(f32) + nn(mixed_ref[...], w_ref[:, 3 * width : 4 * width])
        store(res_ref, res_out)

        @pl.loop(0, total // CHUNK, unroll=UNROLL)
        def _(i):
            at = rows_at(i, CHUNK)
            x = res_ref[at]
            x = x - jnp.mean(x, axis=-1, keepdims=True)
            rstd = lax.rsqrt(jnp.mean(x * x, axis=-1, keepdims=True) + EPSILON)
            n2_ref[at] = (x * rstd * gain_m + shift_m).astype(bf16)

        store(n2_ref, n2_out)
        slot_w = par_ref[4 : 4 + experts].astype(bf16)
        for img in range(images):
            span = slice(img * rows, (img + 1) * rows)
            logits = nt(slot_w, n2_ref[span])
            log_ref[img] = logits
            live = column < meta[img]
            dispatch, combine = routing(logits, live)
            small[img * experts : (img + 1) * experts] = nn(dispatch.astype(bf16), n2_ref[span])
            combine = jnp.where(live, combine, 0.0).astype(bf16)
            small[(images + img) * experts : (images + img + 1) * experts] = nn(combine, cot_ref[span])
        slots_ref[...] = small[...].astype(bf16)
        for copy in stores:
            copy.wait()

    return body


def expert_kernel(images, experts, width, hidden, chips, pieces):
    lanes = -(-hidden // LANES) * LANES
    per = images * experts
    half = chips * per

    def body(_, *refs):
        own_refs, oth_refs, refs = refs[:pieces], refs[pieces : 2 * pieces], refs[2 * pieces :]
        in_ref, out_ref, mine_ref, other_ref, s_ref, g_ref, act_ref, gpre_ref, win, wout, so, gs = refs
        win[...] = jnp.zeros(win.shape, bf16)
        wout[...] = jnp.zeros(wout.shape, bf16)
        for e in range(experts):
            win[e * lanes : e * lanes + hidden, :] = in_ref[e]
            wout[e * lanes : e * lanes + hidden, :] = out_ref[e]

        for side, group in enumerate((own_refs, oth_refs)):
            for j, ref in enumerate(group):
                share = ref.shape[0] // 2

                @pl.loop(0, share)
                def _(i):
                    first, second = ref[2 * i].astype(f32), ref[2 * i + 1].astype(f32)
                    at = pl.ds(pl.multiple_of(side * half + (j * share + i) * 2 * per, 2 * per), 2 * per)
                    s_ref[at] = jnp.concatenate([first[:per], second[:per]], axis=0).astype(bf16)
                    g_ref[at] = jnp.concatenate([first[per:], second[per:]], axis=0).astype(bf16)

        block = 2 * half if 2 * half <= 256 else 256

        @pl.loop(0, 2 * half // block)
        def _(i):
            at = rows_at(i, block)
            so[at, : experts * lanes] = nt(s_ref[at], win[...])
            gs[at, : experts * lanes] = nt(g_ref[at], wout[...])

        @pl.loop(0, 2 * half // CHUNK, unroll=4)
        def _(i):
            at = rows_at(i, CHUNK)
            shape = (CHUNK, experts * lanes)
            keep = (lax.broadcasted_iota(jnp.int32, shape, 0) % experts) == (
                lax.broadcasted_iota(jnp.int32, shape, 1) // lanes
            )
            v = so[at, : experts * lanes]
            grad = gs[at, : experts * lanes]
            tanh = jnp.tanh(GELU_C * (v + GELU_A * v * v * v))
            act = 0.5 * v * (1.0 + tanh)
            slope = 0.5 * (1.0 + tanh) + 0.5 * v * (1.0 - tanh * tanh) * (
                GELU_C * (1.0 + 3.0 * GELU_A * v * v)
            )
            act_ref[at] = jnp.where(keep, act, 0.0).astype(bf16)
            gpre_ref[at] = jnp.where(keep, slope * grad, 0.0).astype(bf16)

        @pl.loop(0, 2 * half // block)
        def _(i):
            at = rows_at(i, block)
            so[at, :width] = nn(act_ref[at], wout[...])
            gs[at, :width] = nn(gpre_ref[at], win[...])

        for side, ref in enumerate((mine_ref, other_ref)):

            @pl.loop(0, chips)
            def _(f):
                at = pl.ds(pl.multiple_of(side * half + f * per, per), per)
                ref[f] = jnp.concatenate([so[at, :width], gs[at, :width]], axis=0).astype(bf16)

    return body


def expert_grad_kernel(experts, hidden):
    lanes = -(-hidden // LANES) * LANES

    def body(_, s_ref, g_ref, act_ref, gpre_ref, in_ref, out_ref):
        for e in range(experts):
            at = slice(e * lanes, (e + 1) * lanes)
            in_ref[e] = tn(gpre_ref[:, at], s_ref[...])[:hidden]
            out_ref[e] = tn(act_ref[:, at], g_ref[...])[:hidden]

    return body


def norm_pull(x, rstd, gain, grad):
    scaled = grad * gain
    first = jnp.mean(scaled, axis=-1, keepdims=True)
    second = jnp.mean(scaled * x, axis=-1, keepdims=True)
    return rstd * (scaled - first - x * second)


def attend_pull(meta, sizes, half, joint_ref, probs_ref, mixed_ref, gm_ref, gj):
    images, rows, width, *_ = sizes
    share = HEADS // 4
    ones = jnp.ones((rows, LANES), bf16)
    for q in range(share):
        at_q, at_k, at_v = [slice(i * width // 2 + q * LANES, i * width // 2 + (q + 1) * LANES) for i in range(3)]
        for img in range(images):
            span = slice(img * rows, (img + 1) * rows)
            query, key, value = joint_ref[span, at_q], joint_ref[span, at_k], joint_ref[span, at_v]
            p = half * share + q
            at = slice(p * LANES, (p + 1) * LANES)
            grad = stacked(gm_ref[span, at])
            dots = stacked(-(gm_ref[span, at].astype(f32) * mixed_ref[span, at].astype(f32)).astype(bf16))
            low = probs_ref[q, img]
            grad_scores = (low.astype(f32) * nt(beside(grad, dots), beside(value, ones))).astype(bf16)
            gj[span, at_q] = (unstacked(nn(grad_scores, key)) * 0.125).astype(bf16)
            gj[span, at_k] = (tn(grad_scores, stacked(query)) * 0.125).astype(bf16)
            gj[span, at_v] = tn(low, grad).astype(bf16)


def sums_lanes(width, part_rows):
    return slice(8, 8 + 3 * width // part_rows)


def small_lanes(width, part_rows):
    return -(-sums_lanes(width, part_rows).stop // LANES) * LANES


def half_loads(width, half, joint_in, joint_ref, probs_in, probs_ref, sems):
    part, share = width // 2, HEADS // 4
    loads = [
        pltpu.make_async_copy(
            joint_in.at[:, i * width + half * part : i * width + (half + 1) * part],
            joint_ref.at[:, i * part : (i + 1) * part],
            sems.at[i],
        )
        for i in range(3)
    ]
    loads.append(pltpu.make_async_copy(probs_in.at[half * share : (half + 1) * share], probs_ref, sems.at[3]))
    return loads


def second_norm_kernel(sizes):
    images, rows, width, *_ = sizes

    def body(meta, res_in, n2_in, xn_ref, dev_ref, n2_ref, res_ref, sems):
        loads = [pltpu.make_async_copy(res_in, res_ref, sems.at[0]), pltpu.make_async_copy(n2_in, n2_ref, sems.at[1])]
        for load in loads:
            load.start()
        loads[0].wait()

        @pl.loop(0, images * rows // CHUNK, unroll=UNROLL)
        def _(i):
            at = rows_at(i, CHUNK)
            x = res_ref[at]
            x = x - jnp.mean(x, axis=-1, keepdims=True)
            rstd = lax.rsqrt(jnp.mean(x * x, axis=-1, keepdims=True) + EPSILON)
            xn_ref[at] = x * rstd
            dev_ref[at] = jnp.broadcast_to(rstd, (CHUNK, LANES))

        loads[1].wait()

    return body


def slots_pull_kernel(sizes):
    images, rows, width, experts, chips, part_rows, shares = sizes
    pieces = len(shares)
    total = images * rows
    share = HEADS // 4

    def body(meta, cot_ref, par_ref, log_ref, sum_ref, r1_ref, r2_ref, r3_ref, xn_ref, dev_ref, n2_ref, w_in, xh_in,
             joint_in, probs_in, mixed_in, small, grad_logs, xgrad_ref, gm, gj, grads, sums_ref, xh_ref,
             mixed_ref, joint_late, probs_late, w_late, *refs):
        outs, (gn, gb, tile, w_ref, joint_ref, probs_ref, sems) = refs[:-7], refs[-7:]
        late = [
            pltpu.make_async_copy(mixed_in, mixed_ref, sems.at[1]),
            pltpu.make_async_copy(w_in.at[:, 3 * width : 4 * width], w_ref, sems.at[2]),
        ]
        loads = half_loads(width, 0, joint_in, joint_ref, probs_in, probs_ref, sems.at[3:7])
        last = [pltpu.make_async_copy(xh_in, xh_ref, sems.at[7])]
        ahead = half_loads(width, 1, joint_in, joint_late, probs_in, probs_late, sems.at[8:12])
        ahead += weight_loads(width, w_in, w_late, sems.at[12:18])
        for load in late + loads + last + ahead:
            load.start()

        def put(first, count):
            if pieces:
                cut(meta, images, chips, part_rows, tile, count, *outs, first)
            else:
                outs[0][:, first : first + count] = tile[:, :count]

        sums = sum_ref[0].astype(f32) + r1_ref[0].astype(f32) + r2_ref[0].astype(f32) + r3_ref[0].astype(f32)
        small[...] = sums.astype(bf16).astype(f32)
        slot_w = par_ref[4 : 4 + experts]
        column = lax.broadcasted_iota(jnp.int32, (1, rows), 1)
        for img in range(images):
            span = slice(img * rows, (img + 1) * rows)
            live = column < meta[img]
            dispatch, combine = routing(log_ref[img], live)
            out32 = small[img * experts : (img + 1) * experts]
            grad32 = small[(images + img) * experts : (images + img + 1) * experts]
            slot_out = out32.astype(bf16)
            grad_comb = jnp.where(live, nt(slot_out, cot_ref[span]), 0.0)
            grad_disp = nt(grad32.astype(bf16), n2_ref[span])
            grad_log = combine * (grad_comb - jnp.sum(combine * grad_comb, axis=0, keepdims=True))
            grad_log = grad_log + dispatch * (
                grad_disp - jnp.sum(dispatch * grad_disp, axis=1, keepdims=True)
            )
            grad_logs[img] = grad_log
            left = jnp.concatenate([dispatch, grad_log], axis=0).astype(bf16)
            right = jnp.concatenate([grad32, slot_w], axis=0).astype(bf16)
            gn[span] = tn(left, right)
        grads[...] = jnp.zeros(grads.shape, f32)

        gain_m = par_ref[2:3]
        zero = jnp.zeros((8, width), f32)
        for img in range(images):

            def step(i, carry):
                at = pl.ds(pl.multiple_of(img * rows + i * CHUNK, CHUNK), CHUNK)
                grad = gn[at]
                x = xn_ref[at]
                pulled = norm_pull(x, dev_ref[at, 0:1], gain_m, grad)
                row = i * CHUNK + lax.broadcasted_iota(jnp.int32, (CHUNK, 1), 0)
                pulled = pulled + jnp.where(row < meta[img], cot_ref[at].astype(f32), 0.0)
                xgrad_ref[at] = pulled
                gb[at] = pulled.astype(bf16)
                return carry[0] + fold_rows(grad * x), carry[1] + fold_rows(grad)

            sums = lax.fori_loop(0, rows // CHUNK, step, (zero, zero) if img == 0 else sums, unroll=UNROLL)
        grads[2:3] = jnp.sum(sums[0], axis=0, keepdims=True)
        grads[3:4] = jnp.sum(sums[1], axis=0, keepdims=True)

        for load in late:
            load.wait()
        tile[:, :width] = tn(mixed_ref[...], gb[...])
        put(0, width)
        gm[...] = nt(gb[...], w_ref[...]).astype(bf16)
        for load in loads:
            load.wait()
        attend_pull(meta, sizes, 0, joint_ref, probs_ref, mixed_ref, gm, gj)
        for load in last:
            load.wait()
        tile[...] = tn(xh_ref[...], gj[...])
        sums_ref[0:1] = column_sums(gj)
        put(width, 3 * width // 2)
        for load in ahead:
            load.wait()

    return body


def heads_pull_kernel(sizes):
    images, rows, width, experts, *_ = sizes

    def body(meta, gm_ref, joint_ref, probs_ref, mixed_ref, grad_logs, n2_ref, gj, slot_ref):
        total = jnp.zeros((experts, width), f32)
        for img in range(images):
            total = total + nn(grad_logs[img].astype(bf16), n2_ref[img * rows : (img + 1) * rows])
        slot_ref[...] = jnp.zeros(slot_ref.shape, f32)
        slot_ref[4 : 4 + experts] = total
        attend_pull(meta, sizes, 1, joint_ref, probs_ref, mixed_ref, gm_ref, gj)

    return body


def heads_grad_kernel(sizes):
    images, rows, width, experts, chips, part_rows, shares = sizes
    half = 3 * width // 2

    def body(meta, gj, grads, slot_ref, sums_ref, xh_ref, *refs):
        outs, (tile, small) = refs[:-2], refs[-2:]
        sums = [sums_ref[0:1], column_sums(gj)]
        wide = sums_lanes(width, part_rows)
        small[:, :LANES] = jnp.concatenate([grads[...] + slot_ref[...], jnp.zeros((LANES - 8, width), f32)], axis=0).T
        each = 3 * width // part_rows
        for r in range(part_rows):
            row = [s[:, c0 - i * half : c1 - i * half] for i, s in enumerate(sums)
                   for c0, c1 in [(max(r * each, i * half), min((r + 1) * each, (i + 1) * half))] if c0 < c1]
            small[r : r + 1, wide] = jnp.concatenate(row, axis=1)
        for t in range(1, width // part_rows):
            small[t * part_rows : (t + 1) * part_rows, wide] = small[:part_rows, wide]
        tile[...] = tn(xh_ref[...], gj[...])

        def put(ref, count, first):
            if shares:
                cut(meta, images, chips, part_rows, ref, count, *outs, first)
            else:
                outs[0][:, first : first + count] = ref[:, :count]

        put(tile, half, 0)
        put(small, small.shape[1], half)

    return body


def inputs_pull_kernel(sizes):
    images, rows, width, experts, chips, part_rows, shares = sizes
    total = images * rows
    half = 3 * width // 2

    def body(meta, x_ref, par_ref, gj0_ref, gj1_ref, w_ref, part_ref, log_ref, small, res_in, xgrad_ref, block_ref,
             gn, res_ref, sems):
        load = pltpu.make_async_copy(res_in, res_ref, sems.at[0])
        load.start()
        gn[...] = nt(gj0_ref[...], w_ref[:, :half]) + nt(gj1_ref[...], w_ref[:, half:])
        column = lax.broadcasted_iota(jnp.int32, (1, rows), 1)
        load.wait()
        for img in range(images):
            span = slice(img * rows, (img + 1) * rows)
            _, combine = routing(log_ref[img], column < meta[img])
            live_row = lax.broadcasted_iota(jnp.int32, (rows, 1), 0) < meta[img]
            expert_sum = tn(combine.astype(bf16), small[img * experts : (img + 1) * experts].astype(bf16))
            block_ref[span] = jnp.where(live_row, res_ref[span] + expert_sum, 0.0).astype(bf16)
        gain_a = par_ref[0:1]

        @pl.loop(0, total // CHUNK, unroll=UNROLL)
        def _(i):
            at = rows_at(i, CHUNK)
            x = x_ref[at].astype(f32)
            x = x - jnp.mean(x, axis=-1, keepdims=True)
            rstd = lax.rsqrt(jnp.mean(x * x, axis=-1, keepdims=True) + EPSILON)
            xgrad_ref[at] = part_ref[at] + norm_pull(x * rstd, rstd, gain_a, gn[at])

    return body


def split_sum(parts, first_type=f32):
    def run(*args):
        count, rest = args[0].shape[0], args[0].shape[1:]
        share = count // parts

        def body(*refs):
            ins, outs = refs[: len(args)], refs[len(args) :]
            for part in range(parts):

                @pl.loop(0, share)
                def _(i):
                    total = ins[0][part * share + i].astype(f32)
                    for ref in ins[1:]:
                        total = total + ref[part * share + i].astype(f32)
                    outs[part][i] = total.astype(outs[part].dtype)

        types = [first_type] + [bf16] * (parts - 1)
        return pl.pallas_call(
            body,
            out_shape=[jax.ShapeDtypeStruct((share,) + rest, t) for t in types],
            in_specs=[vmem()] * len(args),
            out_specs=[vmem()] * parts,
            compiler_params=pltpu.CompilerParams(vmem_limit_bytes=32 * MIB),
        )(*args)

    return run


def add_kernel(groups, types, share=2):
    def run(*args):
        rest = args[0].shape[1:]
        sizes = [share * len(g) for g in groups]

        def body(*refs):
            ins, outs = refs[: len(args)], refs[len(args) :]
            for out, group in zip(outs, groups):
                for j, terms in enumerate(group):
                    for i in range(share):
                        total = ins[terms[0][0]][terms[0][1] + i].astype(f32)
                        for a, first in terms[1:]:
                            total = total + ins[a][first + i].astype(f32)
                        out[j * share + i] = total.astype(out.dtype)

        return pl.pallas_call(
            body,
            out_shape=[jax.ShapeDtypeStruct((c,) + rest, t) for c, t in zip(sizes, types)],
            in_specs=[vmem()] * len(args),
            out_specs=[vmem()] * len(groups),
            compiler_params=pltpu.CompilerParams(vmem_limit_bytes=16 * MIB),
        )(*args)

    return run


def finish_kernel(width, experts, part_rows):
    half = width // 2
    wide = sums_lanes(width, part_rows)

    def body(a0, a1, b0, b1, w_ref, gain_ref, shift_ref, out_ref, in_ref, ns_ref, nb_ref, ms_ref, mb_ref, slot_ref,
             square, sums):
        first = a0[0] + a1[0].astype(f32)
        second = b0[0] + b1[0].astype(f32)
        out_ref[...] = first[:, :width]
        small = second[:, 3 * half :]
        each = 3 * width // part_rows
        for r in range(part_rows):
            sums[0:1, r * each : (r + 1) * each] = small[r : r + 1, wide]
        square[...] = jnp.zeros_like(square)
        square[0:1, :part_rows] = gain_ref[...].astype(f32)
        square[1:2, :part_rows] = shift_ref[...].astype(f32)
        turned = square[...].T
        gain, shift = turned[:part_rows, 0:1], turned[:part_rows, 1:2]
        by_gain = jnp.zeros((part_rows, half), f32)
        by_shift = jnp.zeros((part_rows, half), f32)
        for i in range(3):
            for j, value in enumerate((first[:, width + i * half : width + (i + 1) * half], second[:, i * half : (i + 1) * half])):
                at = slice(i * width + j * half, i * width + (j + 1) * half)
                total = sums[0:1, (j * 3 + i) * half : (j * 3 + i + 1) * half]
                weight = w_ref[:, at].astype(f32)
                in_ref[:, at] = value * gain + shift * total
                by_gain = by_gain + value * weight
                by_shift = by_shift + total * weight
        lane = lax.broadcasted_iota(jnp.int32, (1, LANES), 1)
        small = jnp.where(lane == 0, jnp.sum(by_gain, axis=1, keepdims=True), small[:, :LANES])
        small = jnp.where(lane == 1, jnp.sum(by_shift, axis=1, keepdims=True), small)
        square[:part_rows] = small
        turned = square[...].T
        for i, ref in enumerate((ns_ref, nb_ref, ms_ref, mb_ref)):
            ref[...] = turned[i : i + 1, :part_rows]
        slot_ref[...] = turned[4 : 4 + experts, :part_rows]

    return body


def stages_of(devices):
    chips = devices // 2
    groups, bit = [], 1
    while bit < chips:
        count = min(4, chips // bit)
        groups.append([bit * i for i in range(count)])
        bit *= count
    return groups


def swap(value, devices, chip_offset, core_offset):
    mask = 2 * chip_offset + core_offset
    return lax.ppermute(value, "fsdp", [(i, i ^ mask) for i in range(devices)])


def gather_slots(block, devices):
    *lower, last = stages_of(devices)[::-1]
    for group in lower:
        parts = [block] + [swap(block, devices, o, 0) for o in group[1:]]
        block = jnp.concatenate(parts, axis=0)
    own = [block] + [swap(block, devices, o, 0) for o in last[1:]]
    return own, [swap(part, devices, 0, 1) for part in own]


def scatter_chips(mine, other, devices):
    terms = [mine, swap(other, devices, 0, 1)]
    for group in stages_of(devices):
        parts = split_sum(len(group))(*terms)
        terms = [parts[0]] + [swap(p, devices, o, 0) for p, o in zip(parts[1:], group[1:])]
    return terms


SHARES = (2,) * 8


def gather_pieces(block, devices):
    block = block[None]
    far = swap(block, devices, 8, 0)
    z0 = jnp.concatenate([block, swap(block, devices, 4, 0)], axis=0)
    x0, y0 = swap(z0, devices, 1, 0), swap(z0, devices, 2, 0)
    z1 = jnp.concatenate([far, swap(far, devices, 4, 0)], axis=0)
    x1, y1 = swap(z1, devices, 1, 0), swap(z1, devices, 2, 0)
    d0, d1 = swap(y0, devices, 1, 0), swap(x1, devices, 2, 0)
    own = [z0, z1, x0, x1, y0, y1, d0, d1]
    return own + [swap(piece, devices, 0, 1) for piece in own]


def after(values, events):
    return lax.optimization_barrier((*values, *events))[: len(values)]


def scatter_begin(mine, other, devices, events=()):
    got = swap(other, devices, 0, 1)
    if events:
        (got,) = after([got], events)
    z0, z1, x0, x1, y0, y1, d0, d1 = [[(0, i), (1, i)] for i in range(0, 16, 2)]
    return add_kernel(
        [[z0], [z1], [d0, x0], [d1, y1], [x1], [y0]], [f32, f32, bf16, bf16, bf16, bf16]
    )(mine, got)


def scatter_middle(parts, devices, events=()):
    z0, z1, to_x, to_y, x1, y0 = parts
    from_x, from_y = swap(to_x, devices, 1, 0), swap(to_y, devices, 2, 0)
    if events:
        x1, y0 = after([x1, y0], events)
    x1, y0 = add_kernel([[[(0, 0), (2, 0)]], [[(1, 0), (3, 0)]]], [bf16, bf16])(x1, y0, from_y, from_x)
    return z0, z1, x1, y0, from_x, from_y


def scatter_near(parts, devices):
    z0, z1, x1, y0, from_x, from_y = parts
    from_x1, from_y0 = swap(x1, devices, 1, 0), swap(y0, devices, 2, 0)
    (z1,) = add_kernel([[[(0, 0), (1, 0), (2, 2)]]], [bf16])(z1, from_x1, from_y)
    return z0, from_x, from_y0, swap(z1, devices, 4, 0), z1


def scatter_end(parts, devices):
    z0, from_x, from_y0, from_z1, _ = parts
    keep, send = add_kernel(
        [[[(0, i), (1, 2 + i), (2, i), (3, i)]] for i in range(2)], [f32, bf16], 1
    )(z0, from_x, from_y0, from_z1)
    return keep, swap(send, devices, 8, 0)


def build(devices):
    def shards(images, lengths, norm_scale, norm_shift, attend_in, attend_out, mixer_scale, mixer_shift,
               slot_params, expert_in, expert_out, cotangent):
        count, rows, width = images.shape
        experts, _, hidden = expert_in.shape
        part_rows = attend_in.shape[0]
        chips = devices // 2
        total = count * rows
        pairs = HEADS // 2
        half = width // 2
        wide = 4 * width + LANES
        shares = SHARES if part_rows % 8 == 0 and chips == 16 else ()
        sizes = (count, rows, width, experts, chips, part_rows, shares)
        meta = lengths
        x = images.reshape(total, width)
        cot = cotangent.reshape(total, width)
        vectors = [v.reshape(1, part_rows) for v in (norm_scale, norm_shift, mixer_scale, mixer_shift)]
        given = [attend_in, attend_out, *vectors, slot_params.T]
        pack = pl.pallas_call(
            pack_kernel(width, experts),
            out_shape=jax.ShapeDtypeStruct((part_rows, wide), bf16),
            in_specs=[hbm()] * 7,
            out_specs=vmem(),
            scratch_shapes=[pltpu.VMEM((LANES, LANES), f32)]
            + [pltpu.VMEM(a.shape, bf16) for a in given]
            + [pltpu.SemaphoreType.DMA((7,))],
            compiler_params=pltpu.CompilerParams(vmem_limit_bytes=8 * MIB),
        )(*[pltpu.with_memory_space_constraint(a, pltpu.HBM) for a in given])
        if shares:
            weights = gather_pieces(pack, devices)
        else:
            weights = [lax.all_gather(pack, "fsdp", axis=0, tiled=True)]
        kept = [
            ((total, width), bf16),
            ((total, width), bf16),
            ((total, 3 * width), bf16),
            ((pairs, count, 2 * rows, rows), bf16),
            ((total, width), f32),
            ((total, width), bf16),
        ]
        outs = [
            ((8, width), f32),
            ((count, experts, rows), f32),
            ((2 * count * experts, width), bf16),
        ] + kept
        scratch = kept + [((2 * count * experts, width), f32)] + [((total, width), bf16)] * 3
        if shares:
            outs.append(((width, wide), bf16))
            scratch += [outs[-1]] + [((chips, part_rows, wide), bf16)] * 2
        par, logs, slots, xh, mixed, joint, probs, res, n2, *more = call(
            forward_kernel(sizes),
            outs,
            scratch,
            40,
            far_in=range(2),
            any_in=range(2, 2 + 2 * len(shares)),
            far_out=range(3, len(outs)),
            sems=10 + pairs + 2 * len(shares),
        )(meta, x, cot, *weights)
        w = more[0] if shares else weights[0]

        own, oth = gather_slots(slots[None], devices)
        lanes = -(-hidden // LANES) * LANES
        held = devices * count * experts
        most = max(width, experts * lanes)
        mine, other, s_all, g_all, act, gpre = call(
            expert_kernel(count, experts, width, hidden, chips, len(own)),
            [
                ((chips, 2 * count * experts, width), bf16),
                ((chips, 2 * count * experts, width), bf16),
                ((held, width), bf16),
                ((held, width), bf16),
                ((held, experts * lanes), bf16),
                ((held, experts * lanes), bf16),
            ],
            [
                ((experts * lanes, width), bf16),
                ((experts * lanes, width), bf16),
                ((held, most), f32),
                ((held, most), f32),
            ],
            24 if held <= 256 else 56,
        )(meta, *own, *oth, jnp.swapaxes(expert_in, 1, 2), expert_out)
        expin_grad, expout_grad = call(
            expert_grad_kernel(experts, hidden),
            [((experts, hidden, width), f32), ((experts, hidden, width), f32)],
            [],
            24 if held <= 256 else 56,
            flops=2 * 10**9,
        )(meta, s_all, g_all, act, gpre)
        terms = scatter_chips(mine, other, devices)
        if len(terms) < 4:
            terms = terms + [jnp.zeros_like(terms[-1])] * (4 - len(terms))
        terms[0], expin_grad, expout_grad = lax.optimization_barrier((terms[0], expin_grad, expout_grad))

        def blocks(columns):
            if shares:
                return [((chips, part_rows, columns), bf16)] * 2
            return [((width, columns), f32)]

        halves = [((total, 3 * half), bf16), ((pairs // 2, count, 2 * rows, rows), bf16)]
        xn, dev, n2 = call(
            second_norm_kernel(sizes),
            [((total, width), f32), ((total, LANES), f32), ((total, width), bf16)],
            [((total, width), f32)],
            16,
            flops=10**9,
            far_in=range(2),
            sems=2,
        )(meta, res, n2)
        slot_sums, grad_logs, part, gm, gj, early, sums, xh, mixed, joint1, probs1, w_all, *first = call(
            slots_pull_kernel(sizes),
            [
                ((2 * count * experts, width), f32),
                ((count, experts, rows), f32),
                ((total, width), f32),
                ((total, width), bf16),
                ((total, 3 * half), bf16),
                ((8, width), f32),
                ((8, 3 * half), f32),
                ((total, width), bf16),
                ((total, width), bf16),
            ]
            + halves
            + [((width, 3 * width), bf16)]
            + blocks(width + 3 * half),
            [
                ((total, width), f32),
                ((total, width), bf16),
                ((width, 3 * half), f32),
                ((width, width), bf16),
            ]
            + halves,
            VMEM_MIB,
            far_in=range(10, 15),
            sems=18,
        )(meta, cot, par, logs, *terms, xn, dev, n2, w, xh, joint, probs, mixed)
        gj1, slot_grads = call(
            heads_pull_kernel(sizes), [((total, 3 * half), bf16), ((8, width), f32)], [], VMEM_MIB, flops=3 * 10**9
        )(meta, gm, joint1, probs1, mixed, grad_logs, n2)
        gj_late = gj1
        if shares:
            first = scatter_begin(*first, devices)
            gj_late = after([gj1], first)[0]
        tiny = small_lanes(width, part_rows)
        second = call(
            heads_grad_kernel(sizes),
            blocks(3 * half + tiny),
            [((width, 3 * half), f32), ((width, tiny), f32)],
            VMEM_MIB,
            flops=4 * 10**9,
        )(meta, gj_late, early, slot_grads, sums, xh)
        if shares:
            second = scatter_begin(*second, devices)
            part = after([part], second)[0]
        xgrad, block = call(
            inputs_pull_kernel(sizes),
            [((total, width), f32), ((total, width), bf16)],
            [((total, width), f32)] * 2,
            VMEM_MIB,
            flops=5 * 10**9,
            far_in=(8,),
            sems=1,
        )(meta, x, par, gj, gj1, w_all, part, logs, slot_sums, res)
        if shares:
            first = scatter_middle(first, devices, [xgrad])
            second = scatter_middle(second, devices, first[2:4])
            first, second = scatter_near(first, devices), scatter_near(second, devices)
            ends = [*scatter_end(first, devices), *scatter_end(second, devices)]
        else:
            ends = []
            for full in (first[0], second[0]):
                full = lax.psum_scatter(full, "fsdp", scatter_dimension=0, tiled=True)[None]
                ends += [full, jnp.zeros_like(full)]
        out_grad, in_grad, ns, nb, ms, mb, slot_grad = pl.pallas_call(
            finish_kernel(width, experts, part_rows),
            out_shape=[jax.ShapeDtypeStruct((part_rows, c), f32) for c in (width, 3 * width)]
            + [jax.ShapeDtypeStruct((1, part_rows), f32)] * 4
            + [jax.ShapeDtypeStruct((experts, part_rows), f32)],
            in_specs=[vmem()] * 7,
            out_specs=[vmem()] * 7,
            scratch_shapes=[pltpu.VMEM((LANES, LANES), f32), pltpu.VMEM((8, 3 * width), f32)],
            compiler_params=pltpu.CompilerParams(vmem_limit_bytes=8 * MIB),
        )(*ends, attend_in, *vectors[:2])
        return (
            block.reshape(images.shape),
            xgrad.reshape(images.shape),
            ns.reshape(part_rows),
            nb.reshape(part_rows),
            in_grad,
            out_grad,
            ms.reshape(part_rows),
            mb.reshape(part_rows),
            slot_grad.T,
            jnp.swapaxes(expin_grad, 1, 2),
            expout_grad,
        )

    return shards


def solution(mesh):
    rows = P("fsdp", None, None)
    cols = P(None, None, "fsdp")
    mids = P(None, "fsdp", None)
    flat = P("fsdp", None)
    vec = P("fsdp")
    return jax.shard_map(
        build(mesh.shape["fsdp"]),
        mesh=mesh,
        in_specs=(rows, vec, vec, vec, flat, flat, vec, vec, flat, cols, mids, rows),
        out_specs=(rows, rows, vec, vec, flat, flat, vec, vec, flat, cols, mids),
        check_vma=False,
    )
```

```python
import jax
import jax.numpy as jnp
from jax import lax
from jax.experimental import pallas as pl
from jax.experimental.pallas import tpu as pltpu
from jax.sharding import PartitionSpec as P

HEADS = 12
NEGATIVE = -1e30
EPSILON = 1e-06
GELU_C = 0.7978845608
GELU_A = 0.044715
LANES = 128
CHUNK = 16
UNROLL = 13
VMEM_MIB = 28
MIB = 1 << 20

bf16 = jnp.bfloat16
f32 = jnp.float32


def dot(a, b, ca, cb):
    return lax.dot_general(a, b, (((ca,), (cb,)), ((), ())), preferred_element_type=f32)


def nn(a, b):
    return dot(a, b, 1, 0)


def nt(a, b):
    return dot(a, b, 1, 1)


def tn(a, b):
    return dot(a, b, 0, 0)


def vmem():
    return pl.BlockSpec(memory_space=pltpu.VMEM)


def anywhere():
    return pl.BlockSpec(memory_space=pl.ANY)


def hbm():
    return pl.BlockSpec(memory_space=pltpu.HBM)


def smem():
    return pl.BlockSpec(memory_space=pltpu.SMEM)


def call(body, outs, scratch, limit_mib, flops=0, far_in=(), any_in=(), far_out=(), sems=0):
    def run(scalars, *args):
        return pl.pallas_call(
            body,
            out_shape=[
                pltpu.HBM(s, d) if i in far_out else jax.ShapeDtypeStruct(s, d)
                for i, (s, d) in enumerate(outs)
            ],
            in_specs=[smem()]
            + [hbm() if i in far_in else anywhere() if i in any_in else vmem() for i in range(len(args))],
            out_specs=[hbm() if i in far_out else vmem() for i in range(len(outs))],
            scratch_shapes=[pltpu.VMEM(s, d) for s, d in scratch]
            + ([pltpu.SemaphoreType.DMA((sems,))] if sems else []),
            compiler_params=pltpu.CompilerParams(vmem_limit_bytes=limit_mib * MIB),
            cost_estimate=pl.CostEstimate(flops=flops, bytes_accessed=0, transcendentals=0),
        )(
            scalars,
            *[pltpu.with_memory_space_constraint(a, pltpu.HBM) if i in far_in else a for i, a in enumerate(args)],
        )

    return run


def rows_at(step, count):
    return pl.ds(pl.multiple_of(step * count, count), count)


def fold_rows(value):
    return value[:8] + value[8:]


def head_masks():
    lane = lax.broadcasted_iota(jnp.int32, (1, LANES), 1)
    return lane < LANES // 2


def stacked(pair):
    first = head_masks()
    zero = jnp.zeros_like(pair)
    return jnp.concatenate([jnp.where(first, pair, zero), jnp.where(first, zero, pair)], axis=0)


def beside(left, right):
    return jnp.concatenate([left, right], axis=1)


def unstacked(both):
    rows = both.shape[0] // 2
    return jnp.where(head_masks(), both[:rows], both[rows:])


def routing(logits, live):
    masked = jnp.where(live, logits, NEGATIVE)
    weight = jnp.exp(masked - jnp.max(masked, axis=1, keepdims=True))
    dispatch = weight / jnp.sum(weight, axis=1, keepdims=True)
    share = jnp.exp(logits - jnp.max(logits, axis=0, keepdims=True))
    combine = share / jnp.sum(share, axis=0, keepdims=True)
    return dispatch, combine


def pack_kernel(width, experts):
    def body(*refs):
        given, pack_ref, square, here, sems = refs[:7], refs[7], refs[8], refs[9:16], refs[16]
        loads = [pltpu.make_async_copy(a, b, sems.at[i]) for i, (a, b) in enumerate(zip(given, here))]
        for load in loads:
            load.start()
        for load in loads:
            load.wait()
        in_ref, out_ref, ns_ref, nb_ref, ms_ref, mb_ref, slot_ref = here
        pack_ref[:, : 3 * width] = in_ref[...]
        pack_ref[:, 3 * width : 4 * width] = out_ref[...]
        rows = in_ref.shape[0]
        square[...] = jnp.zeros_like(square)
        for i, ref in enumerate((ns_ref, nb_ref, ms_ref, mb_ref)):
            square[i : i + 1, :rows] = ref[...].astype(f32)
        square[4 : 4 + experts, :rows] = slot_ref[...].astype(f32)
        pack_ref[:, 4 * width :] = square[...].T[:rows].astype(bf16)

    return body


def gathered_chip(f, chips):
    return (lax.axis_index("fsdp") // 2) ^ (f // 4 + (f % 4) * (chips // 4))


def scattered_chip(f, chips):
    k = f % 4
    return (lax.axis_index("fsdp") // 2) ^ (f // 4 + (k % 2) * (chips // 2) + (k // 2) * (chips // 4))


def assemble(first, share, chips, part_rows, own_ref, oth_ref, w_ref):
    columns = w_ref.shape[1]
    for own_first in (True, False):

        @pl.when(lax.axis_index("fsdp") % 2 == (0 if own_first else 1))
        def _():
            low_ref, high_ref = (own_ref, oth_ref) if own_first else (oth_ref, own_ref)
            for f in range(first, first + share):
                at = rows_at(gathered_chip(f, chips), 2 * part_rows)
                for c0 in range(0, columns, 640):
                    c1 = min(columns, c0 + 640)
                    both = [low_ref[f, :, c0:c1].astype(f32), high_ref[f, :, c0:c1].astype(f32)]
                    w_ref[at, c0:c1] = jnp.concatenate(both, axis=0).astype(bf16)


def cut(meta, images, chips, part_rows, tile, count, mine_ref, other_ref, first):
    for own_first in (True, False):

        @pl.when(lax.axis_index("fsdp") % 2 == (0 if own_first else 1))
        def _():
            @pl.loop(0, chips, unroll=4)
            def _(f):
                at = rows_at(scattered_chip(f, chips), 2 * part_rows)
                for c0 in range(0, count, 384):
                    c1 = min(count, c0 + 384)
                    both = tile[at, c0:c1]
                    low, high = both[:part_rows].astype(bf16), both[part_rows:].astype(bf16)
                    mine_ref[f, :, first + c0 : first + c1] = low if own_first else high
                    other_ref[f, :, first + c0 : first + c1] = high if own_first else low


def column_sums(ref):
    total = jnp.zeros((CHUNK, ref.shape[1]), f32)
    for i in range(ref.shape[0] // CHUNK):
        total = total + ref[i * CHUNK : (i + 1) * CHUNK].astype(f32)
    return jnp.sum(total, axis=0, keepdims=True)


def weight_loads(width, w_in, w_ref, sems):
    part = width // 2
    loads = []
    for i in range(6):
        first = (i % 3) * width + (i // 3) * part
        loads.append(
            pltpu.make_async_copy(
                w_in.at[:, first : first + part], w_ref.at[:, i * part : (i + 1) * part], sems.at[i]
            )
        )
    return loads


def forward_kernel(sizes):
    images, rows, width, experts, chips, part_rows, shares = sizes
    total = images * rows
    pairs = HEADS // 2
    pieces = len(shares)

    def body(meta, x_in, cot_in, *refs):
        ins, refs = refs[: 2 * pieces or 1], refs[2 * pieces or 1 :]
        par_ref, log_ref, slots_ref, xh_out, mixed_out, joint_out, probs_out, res_out, n2_out, *refs = refs
        if pieces:
            w_out, *refs = refs
        xh_ref, mixed_ref, joint_ref, probs_ref, res_ref, n2_ref, small, x_ref, cot_ref, n1_ref, *refs = refs
        given = [
            pltpu.make_async_copy(x_in, x_ref, refs[-1].at[8 + pairs + 2 * pieces]),
            pltpu.make_async_copy(cot_in, cot_ref, refs[-1].at[9 + pairs + 2 * pieces]),
        ]
        for load in given:
            load.start()
        if pieces:
            w_ref, own_ref, oth_ref, sems = refs
            loads, first = [], 0
            for i, share in enumerate(shares):
                loads.append(
                    [
                        pltpu.make_async_copy(
                            ins[side * pieces + i],
                            stage.at[first : first + share],
                            sems.at[8 + pairs + side * pieces + i],
                        )
                        for side, stage in enumerate((own_ref, oth_ref))
                    ]
                )
                first += share
            for load in sum(loads, []):
                load.start()
            first = 0
            for pair, share in zip(loads, shares):
                for load in pair:
                    load.wait()
                assemble(first, share, chips, part_rows, own_ref, oth_ref, w_ref)
                first += share
        else:
            (sems,) = refs
            w_ref = ins[0]
        stores = []

        def store(ref, out):
            stores.append(pltpu.make_async_copy(ref, out, sems.at[len(stores)]))
            stores[-1].start()

        if pieces:
            store(w_ref, w_out)
        par_ref[...] = w_ref[:, 4 * width : 4 * width + LANES].astype(f32).T[:8]
        gain_a, shift_a = par_ref[0:1], par_ref[1:2]
        gain_m, shift_m = par_ref[2:3], par_ref[3:4]
        for load in given:
            load.wait()

        @pl.loop(0, total // CHUNK, unroll=2 * UNROLL)
        def _(i):
            at = rows_at(i, CHUNK)
            x = x_ref[at].astype(f32)
            x = x - jnp.mean(x, axis=-1, keepdims=True)
            rstd = lax.rsqrt(jnp.mean(x * x, axis=-1, keepdims=True) + EPSILON)
            x = x * rstd
            xh_ref[at] = x.astype(bf16)
            n1_ref[at] = (x * gain_a + shift_a).astype(bf16)

        store(xh_ref, xh_out)

        @pl.loop(0, 3)
        def _(i):
            at = rows_at(i, width)
            joint_ref[:, at] = nn(n1_ref[...], w_ref[:, at]).astype(bf16)

        store(joint_ref, joint_out)
        column = lax.broadcasted_iota(jnp.int32, (1, rows), 1)
        ones = jnp.ones((rows, LANES), bf16)
        lane = lax.broadcasted_iota(jnp.int32, (2 * rows, LANES), 1)
        first_lane = jnp.where(lane == 0, 1.0, 0.0).astype(bf16)
        row = lax.broadcasted_iota(jnp.int32, (rows, LANES), 0)
        bias = [jnp.where((row >= meta[i]) & (lane[:rows] == 0), NEGATIVE, 0.0).astype(bf16) for i in range(images)]
        for p in range(pairs):
            at_q, at_k, at_v = [slice(i * width + p * LANES, i * width + (p + 1) * LANES) for i in range(3)]
            for img in range(images):
                span = slice(img * rows, (img + 1) * rows)
                query, key, value = joint_ref[span, at_q], joint_ref[span, at_k], joint_ref[span, at_v]
                scores = nt(beside(stacked(query * 0.125), first_lane), beside(key, bias[img]))
                weight = jnp.exp(scores - jnp.max(scores, axis=-1, keepdims=True))
                sums = nn(weight.astype(bf16), beside(value, ones))
                share = 1.0 / sums[:, LANES:]
                probs_ref[p, img] = (weight * jnp.concatenate([share, share[:, : rows - LANES]], axis=1)).astype(bf16)
                mixed_ref[span, at_q] = unstacked(sums[:, :LANES] * share).astype(bf16)
            store(probs_ref.at[p], probs_out.at[p])
        store(mixed_ref, mixed_out)

        res_ref[...] = x_ref[...].astype(f32) + nn(mixed_ref[...], w_ref[:, 3 * width : 4 * width])
        store(res_ref, res_out)

        @pl.loop(0, total // CHUNK, unroll=2 * UNROLL)
        def _(i):
            at = rows_at(i, CHUNK)
            x = res_ref[at]
            x = x - jnp.mean(x, axis=-1, keepdims=True)
            rstd = lax.rsqrt(jnp.mean(x * x, axis=-1, keepdims=True) + EPSILON)
            n2_ref[at] = (x * rstd * gain_m + shift_m).astype(bf16)

        store(n2_ref, n2_out)
        slot_w = par_ref[4 : 4 + experts].astype(bf16)
        for img in range(images):
            span = slice(img * rows, (img + 1) * rows)
            logits = nt(slot_w, n2_ref[span])
            log_ref[img] = logits
            live = column < meta[img]
            dispatch, combine = routing(logits, live)
            small[img * experts : (img + 1) * experts] = nn(dispatch.astype(bf16), n2_ref[span])
            combine = jnp.where(live, combine, 0.0).astype(bf16)
            small[(images + img) * experts : (images + img + 1) * experts] = nn(combine, cot_ref[span])
        slots_ref[...] = small[...].astype(bf16)
        for copy in stores:
            copy.wait()

    return body


def expert_kernel(images, experts, width, hidden, chips, pieces):
    lanes = -(-hidden // LANES) * LANES
    per = images * experts
    half = chips * per

    def body(_, *refs):
        own_refs, oth_refs, refs = refs[:pieces], refs[pieces : 2 * pieces], refs[2 * pieces :]
        in_ref, out_ref, mine_ref, other_ref, s_ref, g_ref, act_ref, gpre_ref, win, wout, so, gs = refs
        win[...] = jnp.zeros(win.shape, bf16)
        wout[...] = jnp.zeros(wout.shape, bf16)
        for e in range(experts):
            win[e * lanes : e * lanes + hidden, :] = in_ref[e]
            wout[e * lanes : e * lanes + hidden, :] = out_ref[e]

        for side, group in enumerate((own_refs, oth_refs)):
            for j, ref in enumerate(group):
                share = ref.shape[0] // 2

                @pl.loop(0, share)
                def _(i):
                    first, second = ref[2 * i].astype(f32), ref[2 * i + 1].astype(f32)
                    at = pl.ds(pl.multiple_of(side * half + (j * share + i) * 2 * per, 2 * per), 2 * per)
                    s_ref[at] = jnp.concatenate([first[:per], second[:per]], axis=0).astype(bf16)
                    g_ref[at] = jnp.concatenate([first[per:], second[per:]], axis=0).astype(bf16)

        block = 2 * half if 2 * half <= 256 else 256

        @pl.loop(0, 2 * half // block)
        def _(i):
            at = rows_at(i, block)
            so[at, : experts * lanes] = nt(s_ref[at], win[...])
            gs[at, : experts * lanes] = nt(g_ref[at], wout[...])

        @pl.loop(0, 2 * half // CHUNK, unroll=4)
        def _(i):
            at = rows_at(i, CHUNK)
            shape = (CHUNK, experts * lanes)
            keep = (lax.broadcasted_iota(jnp.int32, shape, 0) % experts) == (
                lax.broadcasted_iota(jnp.int32, shape, 1) // lanes
            )
            v = so[at, : experts * lanes]
            grad = gs[at, : experts * lanes]
            tanh = jnp.tanh(GELU_C * (v + GELU_A * v * v * v))
            act = 0.5 * v * (1.0 + tanh)
            slope = 0.5 * (1.0 + tanh) + 0.5 * v * (1.0 - tanh * tanh) * (
                GELU_C * (1.0 + 3.0 * GELU_A * v * v)
            )
            act_ref[at] = jnp.where(keep, act, 0.0).astype(bf16)
            gpre_ref[at] = jnp.where(keep, slope * grad, 0.0).astype(bf16)

        @pl.loop(0, 2 * half // block)
        def _(i):
            at = rows_at(i, block)
            so[at, :width] = nn(act_ref[at], wout[...])
            gs[at, :width] = nn(gpre_ref[at], win[...])

        for side, ref in enumerate((mine_ref, other_ref)):

            @pl.loop(0, chips)
            def _(f):
                at = pl.ds(pl.multiple_of(side * half + f * per, per), per)
                ref[f] = jnp.concatenate([so[at, :width], gs[at, :width]], axis=0).astype(bf16)

    return body


def expert_grad_kernel(experts, hidden):
    lanes = -(-hidden // LANES) * LANES

    def body(_, s_ref, g_ref, act_ref, gpre_ref, in_ref, out_ref):
        for e in range(experts):
            at = slice(e * lanes, (e + 1) * lanes)
            in_ref[e] = tn(gpre_ref[:, at], s_ref[...])[:hidden]
            out_ref[e] = tn(act_ref[:, at], g_ref[...])[:hidden]

    return body


def norm_pull(x, rstd, gain, grad):
    scaled = grad * gain
    first = jnp.mean(scaled, axis=-1, keepdims=True)
    second = jnp.mean(scaled * x, axis=-1, keepdims=True)
    return rstd * (scaled - first - x * second)


def attend_pull(meta, sizes, half, joint_ref, probs_ref, mixed_ref, gm_ref, gj):
    images, rows, width, *_ = sizes
    share = HEADS // 4
    ones = jnp.ones((rows, LANES), bf16)
    for q in range(share):
        at_q, at_k, at_v = [slice(i * width // 2 + q * LANES, i * width // 2 + (q + 1) * LANES) for i in range(3)]
        for img in range(images):
            span = slice(img * rows, (img + 1) * rows)
            query, key, value = joint_ref[span, at_q], joint_ref[span, at_k], joint_ref[span, at_v]
            p = half * share + q
            at = slice(p * LANES, (p + 1) * LANES)
            grad = stacked(gm_ref[span, at])
            dots = stacked(-(gm_ref[span, at].astype(f32) * mixed_ref[span, at].astype(f32)).astype(bf16))
            low = probs_ref[q, img]
            grad_scores = (low.astype(f32) * nt(beside(grad, dots), beside(value, ones))).astype(bf16)
            gj[span, at_q] = (unstacked(nn(grad_scores, key)) * 0.125).astype(bf16)
            gj[span, at_k] = (tn(grad_scores, stacked(query)) * 0.125).astype(bf16)
            gj[span, at_v] = tn(low, grad).astype(bf16)


def sums_lanes(width, part_rows):
    return slice(8, 8 + 3 * width // part_rows)


def small_lanes(width, part_rows):
    return -(-sums_lanes(width, part_rows).stop // LANES) * LANES


def half_loads(width, half, joint_in, joint_ref, probs_in, probs_ref, sems):
    part, share = width // 2, HEADS // 4
    loads = [
        pltpu.make_async_copy(
            joint_in.at[:, i * width + half * part : i * width + (half + 1) * part],
            joint_ref.at[:, i * part : (i + 1) * part],
            sems.at[i],
        )
        for i in range(3)
    ]
    loads.append(pltpu.make_async_copy(probs_in.at[half * share : (half + 1) * share], probs_ref, sems.at[3]))
    return loads


def second_norm_kernel(sizes):
    images, rows, width, *_ = sizes

    def body(meta, res_in, n2_in, xn_ref, dev_ref, n2_ref, res_ref, sems):
        loads = [pltpu.make_async_copy(res_in, res_ref, sems.at[0]), pltpu.make_async_copy(n2_in, n2_ref, sems.at[1])]
        for load in loads:
            load.start()
        loads[0].wait()

        @pl.loop(0, images * rows // CHUNK, unroll=2 * UNROLL)
        def _(i):
            at = rows_at(i, CHUNK)
            x = res_ref[at]
            x = x - jnp.mean(x, axis=-1, keepdims=True)
            rstd = lax.rsqrt(jnp.mean(x * x, axis=-1, keepdims=True) + EPSILON)
            xn_ref[at] = x * rstd
            dev_ref[at] = jnp.broadcast_to(rstd, (CHUNK, LANES))

        loads[1].wait()

    return body


def slots_pull_kernel(sizes):
    images, rows, width, experts, chips, part_rows, shares = sizes
    pieces = len(shares)
    total = images * rows
    share = HEADS // 4

    def body(meta, cot_ref, par_ref, log_ref, sum_ref, r1_ref, r2_ref, r3_ref, xn_ref, dev_ref, n2_ref, w_in, xh_in,
             joint_in, probs_in, mixed_in, small, grad_logs, xgrad_ref, gm, gj, grads, sums_ref, xh_ref,
             mixed_ref, joint_late, probs_late, w_late, *refs):
        outs, (gn, gb, tile, w_ref, joint_ref, probs_ref, sems) = refs[:-7], refs[-7:]
        late = [
            pltpu.make_async_copy(mixed_in, mixed_ref, sems.at[1]),
            pltpu.make_async_copy(w_in.at[:, 3 * width : 4 * width], w_ref, sems.at[2]),
        ]
        loads = half_loads(width, 0, joint_in, joint_ref, probs_in, probs_ref, sems.at[3:7])
        last = [pltpu.make_async_copy(xh_in, xh_ref, sems.at[7])]
        ahead = half_loads(width, 1, joint_in, joint_late, probs_in, probs_late, sems.at[8:12])
        ahead += weight_loads(width, w_in, w_late, sems.at[12:18])
        for load in late + loads + last + ahead:
            load.start()

        def put(first, count):
            if pieces:
                cut(meta, images, chips, part_rows, tile, count, *outs, first)
            else:
                outs[0][:, first : first + count] = tile[:, :count]

        sums = sum_ref[0].astype(f32) + r1_ref[0].astype(f32) + r2_ref[0].astype(f32) + r3_ref[0].astype(f32)
        small[...] = sums.astype(bf16).astype(f32)
        slot_w = par_ref[4 : 4 + experts]
        column = lax.broadcasted_iota(jnp.int32, (1, rows), 1)
        for img in range(images):
            span = slice(img * rows, (img + 1) * rows)
            live = column < meta[img]
            dispatch, combine = routing(log_ref[img], live)
            out32 = small[img * experts : (img + 1) * experts]
            grad32 = small[(images + img) * experts : (images + img + 1) * experts]
            slot_out = out32.astype(bf16)
            grad_comb = jnp.where(live, nt(slot_out, cot_ref[span]), 0.0)
            grad_disp = nt(grad32.astype(bf16), n2_ref[span])
            grad_log = combine * (grad_comb - jnp.sum(combine * grad_comb, axis=0, keepdims=True))
            grad_log = grad_log + dispatch * (
                grad_disp - jnp.sum(dispatch * grad_disp, axis=1, keepdims=True)
            )
            grad_logs[img] = grad_log
            left = jnp.concatenate([dispatch, grad_log], axis=0).astype(bf16)
            right = jnp.concatenate([grad32, slot_w], axis=0).astype(bf16)
            gn[span] = tn(left, right)
        grads[...] = jnp.zeros(grads.shape, f32)

        gain_m = par_ref[2:3]
        zero = jnp.zeros((8, width), f32)
        for img in range(images):

            def step(i, carry):
                at = pl.ds(pl.multiple_of(img * rows + i * CHUNK, CHUNK), CHUNK)
                grad = gn[at]
                x = xn_ref[at]
                pulled = norm_pull(x, dev_ref[at, 0:1], gain_m, grad)
                row = i * CHUNK + lax.broadcasted_iota(jnp.int32, (CHUNK, 1), 0)
                pulled = pulled + jnp.where(row < meta[img], cot_ref[at].astype(f32), 0.0)
                xgrad_ref[at] = pulled
                gb[at] = pulled.astype(bf16)
                return carry[0] + fold_rows(grad * x), carry[1] + fold_rows(grad)

            sums = lax.fori_loop(0, rows // CHUNK, step, (zero, zero) if img == 0 else sums, unroll=UNROLL)
        grads[2:3] = jnp.sum(sums[0], axis=0, keepdims=True)
        grads[3:4] = jnp.sum(sums[1], axis=0, keepdims=True)

        for load in late:
            load.wait()
        tile[:, :width] = tn(mixed_ref[...], gb[...])
        put(0, width)
        gm[...] = nt(gb[...], w_ref[...]).astype(bf16)
        for load in loads:
            load.wait()
        attend_pull(meta, sizes, 0, joint_ref, probs_ref, mixed_ref, gm, gj)
        for load in last:
            load.wait()
        tile[...] = tn(xh_ref[...], gj[...])
        sums_ref[0:1] = column_sums(gj)
        put(width, 3 * width // 2)
        for load in ahead:
            load.wait()

    return body


def heads_pull_kernel(sizes):
    images, rows, width, experts, *_ = sizes

    def body(meta, gm_ref, joint_ref, probs_ref, mixed_ref, grad_logs, n2_ref, gj, slot_ref):
        total = jnp.zeros((experts, width), f32)
        for img in range(images):
            total = total + nn(grad_logs[img].astype(bf16), n2_ref[img * rows : (img + 1) * rows])
        slot_ref[...] = jnp.zeros(slot_ref.shape, f32)
        slot_ref[4 : 4 + experts] = total
        attend_pull(meta, sizes, 1, joint_ref, probs_ref, mixed_ref, gm_ref, gj)

    return body


def heads_grad_kernel(sizes):
    images, rows, width, experts, chips, part_rows, shares = sizes
    half = 3 * width // 2

    def body(meta, gj, grads, slot_ref, sums_ref, xh_ref, *refs):
        outs, (tile, small) = refs[:-2], refs[-2:]
        sums = [sums_ref[0:1], column_sums(gj)]
        wide = sums_lanes(width, part_rows)
        small[:, :LANES] = jnp.concatenate([grads[...] + slot_ref[...], jnp.zeros((LANES - 8, width), f32)], axis=0).T
        each = 3 * width // part_rows
        for r in range(part_rows):
            row = [s[:, c0 - i * half : c1 - i * half] for i, s in enumerate(sums)
                   for c0, c1 in [(max(r * each, i * half), min((r + 1) * each, (i + 1) * half))] if c0 < c1]
            small[r : r + 1, wide] = jnp.concatenate(row, axis=1)
        for t in range(1, width // part_rows):
            small[t * part_rows : (t + 1) * part_rows, wide] = small[:part_rows, wide]
        tile[...] = tn(xh_ref[...], gj[...])

        def put(ref, count, first):
            if shares:
                cut(meta, images, chips, part_rows, ref, count, *outs, first)
            else:
                outs[0][:, first : first + count] = ref[:, :count]

        put(tile, half, 0)
        put(small, small.shape[1], half)

    return body


def inputs_pull_kernel(sizes):
    images, rows, width, experts, chips, part_rows, shares = sizes
    total = images * rows
    half = 3 * width // 2

    def body(meta, x_ref, par_ref, gj0_ref, gj1_ref, w_ref, part_ref, log_ref, small, res_in, xgrad_ref, block_ref,
             gn, res_ref, sems):
        load = pltpu.make_async_copy(res_in, res_ref, sems.at[0])
        load.start()
        gn[...] = nt(gj0_ref[...], w_ref[:, :half]) + nt(gj1_ref[...], w_ref[:, half:])
        column = lax.broadcasted_iota(jnp.int32, (1, rows), 1)
        load.wait()
        for img in range(images):
            span = slice(img * rows, (img + 1) * rows)
            _, combine = routing(log_ref[img], column < meta[img])
            live_row = lax.broadcasted_iota(jnp.int32, (rows, 1), 0) < meta[img]
            expert_sum = tn(combine.astype(bf16), small[img * experts : (img + 1) * experts].astype(bf16))
            block_ref[span] = jnp.where(live_row, res_ref[span] + expert_sum, 0.0).astype(bf16)
        gain_a = par_ref[0:1]

        @pl.loop(0, total // CHUNK, unroll=2 * UNROLL)
        def _(i):
            at = rows_at(i, CHUNK)
            x = x_ref[at].astype(f32)
            x = x - jnp.mean(x, axis=-1, keepdims=True)
            rstd = lax.rsqrt(jnp.mean(x * x, axis=-1, keepdims=True) + EPSILON)
            xgrad_ref[at] = part_ref[at] + norm_pull(x * rstd, rstd, gain_a, gn[at])

    return body


def split_sum(parts, first_type=f32):
    def run(*args):
        count, rest = args[0].shape[0], args[0].shape[1:]
        share = count // parts

        def body(*refs):
            ins, outs = refs[: len(args)], refs[len(args) :]
            for part in range(parts):

                @pl.loop(0, share)
                def _(i):
                    total = ins[0][part * share + i].astype(f32)
                    for ref in ins[1:]:
                        total = total + ref[part * share + i].astype(f32)
                    outs[part][i] = total.astype(outs[part].dtype)

        types = [first_type] + [bf16] * (parts - 1)
        return pl.pallas_call(
            body,
            out_shape=[jax.ShapeDtypeStruct((share,) + rest, t) for t in types],
            in_specs=[vmem()] * len(args),
            out_specs=[vmem()] * parts,
            compiler_params=pltpu.CompilerParams(vmem_limit_bytes=32 * MIB),
        )(*args)

    return run


def add_kernel(groups, types, share=2):
    def run(*args):
        rest = args[0].shape[1:]
        sizes = [share * len(g) for g in groups]

        def body(*refs):
            ins, outs = refs[: len(args)], refs[len(args) :]
            for out, group in zip(outs, groups):
                for j, terms in enumerate(group):
                    for i in range(share):
                        total = ins[terms[0][0]][terms[0][1] + i].astype(f32)
                        for a, first in terms[1:]:
                            total = total + ins[a][first + i].astype(f32)
                        out[j * share + i] = total.astype(out.dtype)

        return pl.pallas_call(
            body,
            out_shape=[jax.ShapeDtypeStruct((c,) + rest, t) for c, t in zip(sizes, types)],
            in_specs=[vmem()] * len(args),
            out_specs=[vmem()] * len(groups),
            compiler_params=pltpu.CompilerParams(vmem_limit_bytes=16 * MIB),
        )(*args)

    return run


def finish_kernel(width, experts, part_rows):
    half = width // 2
    wide = sums_lanes(width, part_rows)

    def body(a0, a1, b0, b1, w_ref, gain_ref, shift_ref, out_ref, in_ref, ns_ref, nb_ref, ms_ref, mb_ref, slot_ref,
             square, sums):
        first = a0[0] + a1[0].astype(f32)
        second = b0[0] + b1[0].astype(f32)
        out_ref[...] = first[:, :width]
        small = second[:, 3 * half :]
        each = 3 * width // part_rows
        for r in range(part_rows):
            sums[0:1, r * each : (r + 1) * each] = small[r : r + 1, wide]
        square[...] = jnp.zeros_like(square)
        square[0:1, :part_rows] = gain_ref[...].astype(f32)
        square[1:2, :part_rows] = shift_ref[...].astype(f32)
        turned = square[...].T
        gain, shift = turned[:part_rows, 0:1], turned[:part_rows, 1:2]
        by_gain = jnp.zeros((part_rows, half), f32)
        by_shift = jnp.zeros((part_rows, half), f32)
        for i in range(3):
            for j, value in enumerate((first[:, width + i * half : width + (i + 1) * half], second[:, i * half : (i + 1) * half])):
                at = slice(i * width + j * half, i * width + (j + 1) * half)
                total = sums[0:1, (j * 3 + i) * half : (j * 3 + i + 1) * half]
                weight = w_ref[:, at].astype(f32)
                in_ref[:, at] = value * gain + shift * total
                by_gain = by_gain + value * weight
                by_shift = by_shift + total * weight
        lane = lax.broadcasted_iota(jnp.int32, (1, LANES), 1)
        small = jnp.where(lane == 0, jnp.sum(by_gain, axis=1, keepdims=True), small[:, :LANES])
        small = jnp.where(lane == 1, jnp.sum(by_shift, axis=1, keepdims=True), small)
        square[:part_rows] = small
        turned = square[...].T
        for i, ref in enumerate((ns_ref, nb_ref, ms_ref, mb_ref)):
            ref[...] = turned[i : i + 1, :part_rows]
        slot_ref[...] = turned[4 : 4 + experts, :part_rows]

    return body


def stages_of(devices):
    chips = devices // 2
    groups, bit = [], 1
    while bit < chips:
        count = min(4, chips // bit)
        groups.append([bit * i for i in range(count)])
        bit *= count
    return groups


def swap(value, devices, chip_offset, core_offset):
    mask = 2 * chip_offset + core_offset
    return lax.ppermute(value, "fsdp", [(i, i ^ mask) for i in range(devices)])


def gather_slots(block, devices):
    *lower, last = stages_of(devices)[::-1]
    for group in lower:
        parts = [block] + [swap(block, devices, o, 0) for o in group[1:]]
        block = jnp.concatenate(parts, axis=0)
    own = [block] + [swap(block, devices, o, 0) for o in last[1:]]
    return own, [swap(part, devices, 0, 1) for part in own]


def scatter_chips(mine, other, devices):
    terms = [mine, swap(other, devices, 0, 1)]
    for group in stages_of(devices):
        parts = split_sum(len(group))(*terms)
        terms = [parts[0]] + [swap(p, devices, o, 0) for p, o in zip(parts[1:], group[1:])]
    return terms


SHARES = (2,) * 8


def gather_pieces(block, devices):
    block = block[None]
    far = swap(block, devices, 8, 0)
    z0 = jnp.concatenate([block, swap(block, devices, 4, 0)], axis=0)
    x0, y0 = swap(z0, devices, 1, 0), swap(z0, devices, 2, 0)
    z1 = jnp.concatenate([far, swap(far, devices, 4, 0)], axis=0)
    x1, y1 = swap(z1, devices, 1, 0), swap(z1, devices, 2, 0)
    d0, d1 = swap(y0, devices, 1, 0), swap(x1, devices, 2, 0)
    own = [z0, z1, x0, x1, y0, y1, d0, d1]
    return own + [swap(piece, devices, 0, 1) for piece in own]


def after(values, events):
    return lax.optimization_barrier((*values, *events))[: len(values)]


def scatter_begin(mine, other, devices, events=()):
    got = swap(other, devices, 0, 1)
    if events:
        (got,) = after([got], events)
    z0, z1, x0, x1, y0, y1, d0, d1 = [[(0, i), (1, i)] for i in range(0, 16, 2)]
    return add_kernel(
        [[z0], [z1], [d0, x0], [d1, y1], [x1], [y0]], [f32, f32, bf16, bf16, bf16, bf16]
    )(mine, got)


def scatter_middle(parts, devices, events=()):
    z0, z1, to_x, to_y, x1, y0 = parts
    from_x, from_y = swap(to_x, devices, 1, 0), swap(to_y, devices, 2, 0)
    if events:
        x1, y0 = after([x1, y0], events)
    x1, y0 = add_kernel([[[(0, 0), (2, 0)]], [[(1, 0), (3, 0)]]], [bf16, bf16])(x1, y0, from_y, from_x)
    return z0, z1, x1, y0, from_x, from_y


def scatter_near(parts, devices):
    z0, z1, x1, y0, from_x, from_y = parts
    from_x1, from_y0 = swap(x1, devices, 1, 0), swap(y0, devices, 2, 0)
    (z1,) = add_kernel([[[(0, 0), (1, 0), (2, 2)]]], [bf16])(z1, from_x1, from_y)
    return z0, from_x, from_y0, swap(z1, devices, 4, 0), z1


def scatter_end(parts, devices):
    z0, from_x, from_y0, from_z1, _ = parts
    keep, send = add_kernel(
        [[[(0, i), (1, 2 + i), (2, i), (3, i)]] for i in range(2)], [f32, bf16], 1
    )(z0, from_x, from_y0, from_z1)
    return keep, swap(send, devices, 8, 0)


def build(devices):
    def shards(images, lengths, norm_scale, norm_shift, attend_in, attend_out, mixer_scale, mixer_shift,
               slot_params, expert_in, expert_out, cotangent):
        count, rows, width = images.shape
        experts, _, hidden = expert_in.shape
        part_rows = attend_in.shape[0]
        chips = devices // 2
        total = count * rows
        pairs = HEADS // 2
        half = width // 2
        wide = 4 * width + LANES
        shares = SHARES if part_rows % 8 == 0 and chips == 16 else ()
        sizes = (count, rows, width, experts, chips, part_rows, shares)
        meta = lengths
        x = images.reshape(total, width)
        cot = cotangent.reshape(total, width)
        vectors = [v.reshape(1, part_rows) for v in (norm_scale, norm_shift, mixer_scale, mixer_shift)]
        given = [attend_in, attend_out, *vectors, slot_params.T]
        pack = pl.pallas_call(
            pack_kernel(width, experts),
            out_shape=jax.ShapeDtypeStruct((part_rows, wide), bf16),
            in_specs=[hbm()] * 7,
            out_specs=vmem(),
            scratch_shapes=[pltpu.VMEM((LANES, LANES), f32)]
            + [pltpu.VMEM(a.shape, bf16) for a in given]
            + [pltpu.SemaphoreType.DMA((7,))],
            compiler_params=pltpu.CompilerParams(vmem_limit_bytes=8 * MIB),
        )(*[pltpu.with_memory_space_constraint(a, pltpu.HBM) for a in given])
        if shares:
            weights = gather_pieces(pack, devices)
        else:
            weights = [lax.all_gather(pack, "fsdp", axis=0, tiled=True)]
        kept = [
            ((total, width), bf16),
            ((total, width), bf16),
            ((total, 3 * width), bf16),
            ((pairs, count, 2 * rows, rows), bf16),
            ((total, width), f32),
            ((total, width), bf16),
        ]
        outs = [
            ((8, width), f32),
            ((count, experts, rows), f32),
            ((2 * count * experts, width), bf16),
        ] + kept
        scratch = kept + [((2 * count * experts, width), f32)] + [((total, width), bf16)] * 3
        if shares:
            outs.append(((width, wide), bf16))
            scratch += [outs[-1]] + [((chips, part_rows, wide), bf16)] * 2
        par, logs, slots, xh, mixed, joint, probs, res, n2, *more = call(
            forward_kernel(sizes),
            outs,
            scratch,
            40,
            far_in=range(2),
            any_in=range(2, 2 + 2 * len(shares)),
            far_out=range(3, len(outs)),
            sems=10 + pairs + 2 * len(shares),
        )(meta, x, cot, *weights)
        w = more[0] if shares else weights[0]

        own, oth = gather_slots(slots[None], devices)
        lanes = -(-hidden // LANES) * LANES
        held = devices * count * experts
        most = max(width, experts * lanes)
        mine, other, s_all, g_all, act, gpre = call(
            expert_kernel(count, experts, width, hidden, chips, len(own)),
            [
                ((chips, 2 * count * experts, width), bf16),
                ((chips, 2 * count * experts, width), bf16),
                ((held, width), bf16),
                ((held, width), bf16),
                ((held, experts * lanes), bf16),
                ((held, experts * lanes), bf16),
            ],
            [
                ((experts * lanes, width), bf16),
                ((experts * lanes, width), bf16),
                ((held, most), f32),
                ((held, most), f32),
            ],
            24 if held <= 256 else 56,
        )(meta, *own, *oth, jnp.swapaxes(expert_in, 1, 2), expert_out)
        expin_grad, expout_grad = call(
            expert_grad_kernel(experts, hidden),
            [((experts, hidden, width), f32), ((experts, hidden, width), f32)],
            [],
            24 if held <= 256 else 56,
            flops=2 * 10**9,
        )(meta, s_all, g_all, act, gpre)
        terms = scatter_chips(mine, other, devices)
        if len(terms) < 4:
            terms = terms + [jnp.zeros_like(terms[-1])] * (4 - len(terms))
        terms[0], expin_grad, expout_grad = lax.optimization_barrier((terms[0], expin_grad, expout_grad))

        def blocks(columns):
            if shares:
                return [((chips, part_rows, columns), bf16)] * 2
            return [((width, columns), f32)]

        halves = [((total, 3 * half), bf16), ((pairs // 2, count, 2 * rows, rows), bf16)]
        xn, dev, n2 = call(
            second_norm_kernel(sizes),
            [((total, width), f32), ((total, LANES), f32), ((total, width), bf16)],
            [((total, width), f32)],
            16,
            flops=10**9,
            far_in=range(2),
            sems=2,
        )(meta, res, n2)
        slot_sums, grad_logs, part, gm, gj, early, sums, xh, mixed, joint1, probs1, w_all, *first = call(
            slots_pull_kernel(sizes),
            [
                ((2 * count * experts, width), f32),
                ((count, experts, rows), f32),
                ((total, width), f32),
                ((total, width), bf16),
                ((total, 3 * half), bf16),
                ((8, width), f32),
                ((8, 3 * half), f32),
                ((total, width), bf16),
                ((total, width), bf16),
            ]
            + halves
            + [((width, 3 * width), bf16)]
            + blocks(width + 3 * half),
            [
                ((total, width), f32),
                ((total, width), bf16),
                ((width, 3 * half), f32),
                ((width, width), bf16),
            ]
            + halves,
            VMEM_MIB,
            far_in=range(10, 15),
            sems=18,
        )(meta, cot, par, logs, *terms, xn, dev, n2, w, xh, joint, probs, mixed)
        gj1, slot_grads = call(
            heads_pull_kernel(sizes), [((total, 3 * half), bf16), ((8, width), f32)], [], VMEM_MIB, flops=3 * 10**9
        )(meta, gm, joint1, probs1, mixed, grad_logs, n2)
        gj_late = gj1
        if shares:
            first = scatter_begin(*first, devices)
            gj_late = after([gj1], first)[0]
        tiny = small_lanes(width, part_rows)
        second = call(
            heads_grad_kernel(sizes),
            blocks(3 * half + tiny),
            [((width, 3 * half), f32), ((width, tiny), f32)],
            VMEM_MIB,
            flops=4 * 10**9,
        )(meta, gj_late, early, slot_grads, sums, xh)
        if shares:
            second = scatter_begin(*second, devices)
            part = after([part], second)[0]
        xgrad, block = call(
            inputs_pull_kernel(sizes),
            [((total, width), f32), ((total, width), bf16)],
            [((total, width), f32)] * 2,
            VMEM_MIB,
            flops=5 * 10**9,
            far_in=(8,),
            sems=1,
        )(meta, x, par, gj, gj1, w_all, part, logs, slot_sums, res)
        if shares:
            first = scatter_middle(first, devices, [xgrad])
            second = scatter_middle(second, devices, first[2:4])
            first, second = scatter_near(first, devices), scatter_near(second, devices)
            ends = [*scatter_end(first, devices), *scatter_end(second, devices)]
        else:
            ends = []
            for full in (first[0], second[0]):
                full = lax.psum_scatter(full, "fsdp", scatter_dimension=0, tiled=True)[None]
                ends += [full, jnp.zeros_like(full)]
        out_grad, in_grad, ns, nb, ms, mb, slot_grad = pl.pallas_call(
            finish_kernel(width, experts, part_rows),
            out_shape=[jax.ShapeDtypeStruct((part_rows, c), f32) for c in (width, 3 * width)]
            + [jax.ShapeDtypeStruct((1, part_rows), f32)] * 4
            + [jax.ShapeDtypeStruct((experts, part_rows), f32)],
            in_specs=[vmem()] * 7,
            out_specs=[vmem()] * 7,
            scratch_shapes=[pltpu.VMEM((LANES, LANES), f32), pltpu.VMEM((8, 3 * width), f32)],
            compiler_params=pltpu.CompilerParams(vmem_limit_bytes=8 * MIB),
        )(*ends, attend_in, *vectors[:2])
        return (
            block.reshape(images.shape),
            xgrad.reshape(images.shape),
            ns.reshape(part_rows),
            nb.reshape(part_rows),
            in_grad,
            out_grad,
            ms.reshape(part_rows),
            mb.reshape(part_rows),
            slot_grad.T,
            jnp.swapaxes(expin_grad, 1, 2),
            expout_grad,
        )

    return shards


def solution(mesh):
    rows = P("fsdp", None, None)
    cols = P(None, None, "fsdp")
    mids = P(None, "fsdp", None)
    flat = P("fsdp", None)
    vec = P("fsdp")
    return jax.shard_map(
        build(mesh.shape["fsdp"]),
        mesh=mesh,
        in_specs=(rows, vec, vec, vec, flat, flat, vec, vec, flat, cols, mids, rows),
        out_specs=(rows, rows, vec, vec, flat, flat, vec, vec, flat, cols, mids),
        check_vma=False,
    )
```
